32 devices in a mesh: groups: 2 (over y), ctx: 8 (over z, x), tp: 2 (over core).
Axes of the slice: x: 2, y: 2, z: 4, core: 2. Of those that a mesh axis runs over, the one named last changes fastest.
Arguments:
- queries: bfloat16 [2048, 4096], P(('groups', 'ctx'), 'tp'), parts along dimension 0, may hold values from -10 to 10
- win_keys: bfloat16 [2048, 512], P(('groups', 'ctx'), 'tp'), parts along dimension 0, may hold values from -6 to 6
- win_values: bfloat16 [2048, 512], P(('groups', 'ctx'), 'tp'), parts along dimension 0, may hold values from -6 to 6
- cache_keys: bfloat16 [1024, 512], P(('groups', 'ctx'), 'tp'), parts along dimension 0, may hold values from -6 to 6
- cache_values: bfloat16 [1024, 512], P(('groups', 'ctx'), 'tp'), parts along dimension 0, may hold values from -6 to 6
- valid_counts: int32 [16], P('groups'), parts along dimension 0, may hold values from 1 to 128
- first_block: int32 [16], P('groups'), parts along dimension 0, may hold values from 0 to 3, as said below
Outputs:
- attended: bfloat16 [2048, 4096], P(('groups', 'ctx'), 'tp'), parts along dimension 0
The draws below stay inside these ranges and needn't reach their ends.
There are 2 independent parts, one for each index of `groups`. The reference program is written for one: setup_inputs(seed, part) draws one part's arguments, and reference() takes and returns one part's arrays. A program takes and returns all parts, laid end to end along the dimension named above; each array names one. Nothing has to cross between parts.
Inputs may be any that keep to these rules, and one draw needn't show every extreme that they name: first_block[b] is at most b // 2.
All inputs are finite; a program needn't handle non-finite values.
Results may differ from the reference program's by a relative error of at most 0.005.
Values may be sent and summed in bfloat16 or wider, within the bound.
No kernel may reach another device: no remote copies, remote signals or barrier semaphores. Data moves between devices by JAX's collectives and lax.ppermute only.
A program may use at most 64 MiB of HBM per device.

```python
import math
import jax
import jax.numpy as jnp
from jax import lax

HD = 128
HEADS = 32
KV_HEADS = 4
TOK_DEV = 128
NBLOCKS = 8
TOKENS = 1024
CACHE = 512


def draw_queries(key, part):
    key = jax.random.fold_in(key, 11)
    return jnp.clip(2.5 * jax.random.normal(key, (TOKENS, HEADS * HD), jnp.float32), -10.0, 10.0).astype(jnp.bfloat16)


def draw_win_keys(key, part):
    key = jax.random.fold_in(key, 13)
    return jnp.clip(jax.random.normal(key, (TOKENS, KV_HEADS * HD), jnp.float32), -6.0, 6.0).astype(jnp.bfloat16)


def draw_cache_keys(key, part):
    key = jax.random.fold_in(key, 17)
    return jnp.clip(jax.random.normal(key, (CACHE, KV_HEADS * HD), jnp.float32), -6.0, 6.0).astype(jnp.bfloat16)


def draw_valid_counts(key, part):
    key = jax.random.fold_in(key, 23)
    first_key, second_key, third_key = jax.random.split(key, 3)
    counts = jax.random.randint(first_key, (NBLOCKS,), TOK_DEV // 2, TOK_DEV + 1)
    full_at = jax.random.randint(second_key, (), 0, NBLOCKS)
    short_at = (full_at + jax.random.randint(third_key, (), 1, NBLOCKS)) % NBLOCKS
    counts = counts.at[full_at].set(TOK_DEV).at[short_at].set(1)
    return counts.astype(jnp.int32)


def draw_first_block(key, part):
    key = jax.random.fold_in(key, 37)
    blocks = jnp.arange(NBLOCKS, dtype=jnp.int32)
    starts = jax.random.randint(key, (NBLOCKS,), 0, blocks // 2 + 1)
    return starts.at[NBLOCKS - 1].set((NBLOCKS - 1) // 2).astype(jnp.int32)


def block_scale(key, shape, pieces, low, largest):
    def one(position, shards_of):
        steps = jax.random.uniform(jax.random.fold_in(jax.random.fold_in(key, 6), position), (shards_of,), jnp.float32, low / len(pieces), largest / len(pieces))
        return jnp.repeat(jnp.exp(steps), shape[position] // shards_of).reshape((-1,) + (1,) * (len(shape) - position - 1))

    level = one(*pieces[0])
    for cut in pieces[1:]:
        level = level * one(*cut)
    return level


def normal_values(key, shape, scale, bound, shards=(), kind=jnp.bfloat16):
    result = scale * jax.random.normal(key, shape, jnp.float32)
    if shards:
        result = result * block_scale(key, shape, shards, -0.22, 0.18)
    return jnp.clip(result, -bound, bound).astype(kind)


def setup_inputs(seed: int = 0, part: int = 0) -> dict:
    keys = jax.random.split(jax.random.key(seed), 8)
    part_splits = jax.random.split(jax.random.fold_in(keys[7], part), 8)
    return {
        "queries": draw_queries(jax.random.fold_in(jax.random.fold_in(keys[7], part), 71), part),
        "win_keys": draw_win_keys(jax.random.fold_in(jax.random.fold_in(keys[7], part), 71), part),
        "win_values": normal_values(part_splits[2], (TOKENS, KV_HEADS * HD), 1.0, 6.0, ((0, 8), (1, 2))),
        "cache_keys": draw_cache_keys(jax.random.fold_in(jax.random.fold_in(keys[7], part), 71), part),
        "cache_values": normal_values(part_splits[4], (CACHE, KV_HEADS * HD), 1.0, 6.0, ((0, 8), (1, 2))),
        "valid_counts": draw_valid_counts(jax.random.fold_in(jax.random.fold_in(keys[7], part), 71), part),
        "first_block": draw_first_block(jax.random.fold_in(jax.random.fold_in(keys[7], part), 71), part),
    }


masked_score = -1.0e30


def reference(queries, win_keys, win_values, cache_keys, cache_values, valid_counts, first_block):
    score_scale = HD ** -0.5
    group_size = HEADS // KV_HEADS
    all_keys = jnp.concatenate([cache_keys, win_keys], axis=0).reshape(CACHE + TOKENS, KV_HEADS, HD)
    all_values = jnp.concatenate([cache_values, win_values], axis=0).reshape(CACHE + TOKENS, KV_HEADS, HD)
    key_pos = jnp.arange(TOKENS, dtype=jnp.int32)
    key_block = key_pos // TOK_DEV
    key_valid = (key_pos % TOK_DEV) < jnp.take(valid_counts, key_block)
    grouped = queries.reshape(TOKENS, HEADS, HD)
    block_rows = math.gcd(512, TOKENS)
    block_total = TOKENS // block_rows

    def one_head(head_idx):
        kv_idx = head_idx // group_size
        head_keys = lax.dynamic_index_in_dim(all_keys, kv_idx, 1, keepdims=False)
        head_values = lax.dynamic_index_in_dim(all_values, kv_idx, 1, keepdims=False)
        head_queries = lax.dynamic_index_in_dim(grouped, head_idx, 1, keepdims=False)

        def one_block(block_idx):
            row_start = (block_idx * block_rows).astype(jnp.int32)
            rows_q = lax.dynamic_slice_in_dim(head_queries, row_start, block_rows, 0)
            query_pos = row_start + jnp.arange(block_rows, dtype=jnp.int32)
            starts = jnp.take(first_block, query_pos // TOK_DEV)
            window_mask = (key_pos[None, :] <= query_pos[:, None]) & (key_block[None, :] >= starts[:, None]) & key_valid[None, :]
            full_mask = jnp.concatenate([jnp.ones((block_rows, CACHE), dtype=bool), window_mask], axis=1)
            score_tile = jnp.dot(rows_q, head_keys.T, preferred_element_type=jnp.float32) * score_scale
            score_tile = jnp.where(full_mask, score_tile, masked_score)
            top = jnp.max(score_tile, axis=1, keepdims=True)
            exp_tile = jnp.where(full_mask, jnp.exp(score_tile - top), 0.0)
            total = jnp.sum(exp_tile, axis=1, keepdims=True)
            summed = jnp.dot(exp_tile.astype(jnp.bfloat16), head_values, preferred_element_type=jnp.float32)
            return (summed / total).astype(jnp.bfloat16)

        return lax.map(one_block, jnp.arange(block_total, dtype=jnp.int32)).reshape(TOKENS, HD)

    outputs = lax.map(one_head, jnp.arange(HEADS, dtype=jnp.int32))
    return jnp.transpose(outputs, (1, 0, 2)).reshape(TOKENS, HEADS * HD)
```

```python
import functools
import math

import jax
import jax.numpy as jnp
from jax import lax
from jax.experimental import pallas as pl
from jax.experimental.pallas import tpu as pltpu
from jax.sharding import PartitionSpec as P

HD = 128
EXP_SCALE = HD**-0.5 * math.log2(math.e)
HIDDEN = -1.0e30
CHUNK_HEADS = 4


def ring_width(count):
    width = round(count ** (1 / 3))
    if width > 1 and count % width == 0 and (count // width) % 2 == 0:
        return width
    return 1


def place_at(position, count):
    width = ring_width(count)
    if width == 1:
        return position
    rows = count // width
    row, step = position // (width - 1), position % (width - 1)
    forth = row * width + 1 + step
    back = row * width + width - 1 - step
    home = (rows - 1 - (position - rows * (width - 1))) * width
    if isinstance(position, int):
        return home if position >= rows * (width - 1) else (back if row % 2 else forth)
    return jnp.where(position >= rows * (width - 1), home, jnp.where(row % 2 == 1, back, forth))


def position_of(place, count):
    width = ring_width(count)
    if width == 1:
        return place
    rows = count // width
    row, column = place // width, place % width
    snake = row * (width - 1) + jnp.where(row % 2 == 1, width - 1 - column, column - 1)
    return jnp.where(column == 0, rows * (width - 1) + rows - 1 - row, snake)


def attend_kernel(offsets, own, last, count, window_rows, *refs):
    valid_ref, first_ref, q_ref = refs[:3]
    refs = refs[3:]
    key_refs, value_refs = refs[: len(offsets)], refs[len(offsets) : 2 * len(offsets)]
    refs = refs[2 * len(offsets) :]
    if not own:
        acc_in, top_in = refs[:2]
        refs = refs[2:]
    if last:
        (out_ref, keys, values) = refs
    else:
        (acc_out, top_out, keys, values) = refs

    me = lax.axis_index("ctx")
    position = position_of(me, count)
    first = first_ref[me]
    rows = q_ref.shape[0]
    kv_heads = key_refs[0].shape[1] // HD
    group = q_ref.shape[1] // HD // kv_heads
    cache_rows = key_refs[0].shape[0] - window_rows
    total_keys = keys.shape[1]
    cache_at = len(offsets) * window_rows
    row_iota = lax.broadcasted_iota(jnp.int32, (window_rows, HD), 0)

    for index, offset in enumerate(offsets):
        place = place_at(lax.rem(position + offset + 2 * count, count), count)
        if own:
            limit = window_rows
        else:
            limit = jnp.where((place >= first) & (place <= me), valid_ref[place], 0)
        shown = row_iota < limit
        for head in range(kv_heads):
            lanes = slice(head * HD, (head + 1) * HD)
            key, value = key_refs[index], value_refs[index]
            fill = key[window_rows : window_rows + 1, lanes].astype(jnp.float32)
            at = slice(index * window_rows, (index + 1) * window_rows)
            win_key = key[:window_rows, lanes]
            win_value = value[:window_rows, lanes]
            if own:
                keys[head, at, :] = win_key
                values[head, at, :HD] = win_value
                values[head, at, HD:] = jnp.ones((window_rows, HD), jnp.bfloat16)
            else:
                keys[head, at, :] = jnp.where(shown, win_key.astype(jnp.float32), fill).astype(jnp.bfloat16)
                values[head, at, :HD] = jnp.where(shown, win_value.astype(jnp.float32), 0.0).astype(jnp.bfloat16)
                values[head, at, HD:] = jnp.where(shown, 1.0, 0.0).astype(jnp.bfloat16)
            at = slice(cache_at + index * cache_rows, cache_at + (index + 1) * cache_rows)
            keys[head, at, :] = key[window_rows:, lanes]
            values[head, at, :HD] = value[window_rows:, lanes]
            values[head, at, HD:] = jnp.ones((cache_rows, HD), jnp.bfloat16)
    filled = cache_at + len(offsets) * cache_rows
    if filled < total_keys:
        spare = total_keys - filled
        for head in range(kv_heads):
            row = key_refs[0][window_rows : window_rows + 1, head * HD : (head + 1) * HD].astype(jnp.float32)
            keys[head, filled:, :] = jnp.broadcast_to(row, (spare, HD)).astype(jnp.bfloat16)
            values[head, filled:, :] = jnp.zeros((spare, 2 * HD), jnp.bfloat16)

    if own:
        key_iota = lax.broadcasted_iota(jnp.int32, (rows, window_rows), 1)
        query_iota = lax.broadcasted_iota(jnp.int32, (rows, window_rows), 0)
        seen = (key_iota <= query_iota) & (key_iota < valid_ref[me])
        bias = jnp.concatenate([jnp.where(seen, 0.0, HIDDEN)] * CHUNK_HEADS, axis=0)

    for head in range(kv_heads):
        for start in range(0, group, CHUNK_HEADS):
            base = head * group + start
            at = slice(base * rows, (base + CHUNK_HEADS) * rows)
            query = jnp.concatenate(
                [q_ref[:, (base + i) * HD : (base + i + 1) * HD] for i in range(CHUNK_HEADS)], axis=0
            )
            score = lax.dot_general(
                query, keys[head], (((1,), (1,)), ((), ())), preferred_element_type=jnp.float32
            )
            if own:
                score = jnp.concatenate([score[:, :window_rows] + bias, score[:, window_rows:]], axis=1)
            top = jnp.max(score, axis=1, keepdims=True)
            if not own:
                before = top_in[at, :]
                top = jnp.maximum(before[:, :1], top)
            weight = jnp.exp2((score - top) * EXP_SCALE).astype(jnp.bfloat16)
            acc = jnp.dot(weight, values[head], preferred_element_type=jnp.float32)
            if not own:
                fade = jnp.exp2((before - top) * EXP_SCALE)
                acc = acc + acc_in[at, :] * jnp.concatenate([fade, fade], axis=1)
            if last:
                result = (acc[:, :HD] / acc[:, HD:]).astype(jnp.bfloat16)
                for i in range(CHUNK_HEADS):
                    out_ref[:, (base + i) * HD : (base + i + 1) * HD] = result[i * rows : (i + 1) * rows]
            else:
                acc_out[at, :] = acc
                top_out[at, :] = jnp.broadcast_to(top, (top.shape[0], HD))


def attend(offsets, keys, values, state, last, queries, valid_counts, first_block, count, window_rows):
    own = state is None
    rows, width = queries.shape
    heads = width // HD
    kv_heads = keys[0].shape[1] // HD
    total_keys = -(-sum(k.shape[0] for k in keys) // HD) * HD
    vmem = pl.BlockSpec(memory_space=pltpu.VMEM)
    smem = pl.BlockSpec(memory_space=pltpu.SMEM)
    if last:
        out_shape = jax.ShapeDtypeStruct(queries.shape, jnp.bfloat16)
        out_specs = vmem
    else:
        out_shape = (
            jax.ShapeDtypeStruct((heads * rows, 2 * HD), jnp.float32),
            jax.ShapeDtypeStruct((heads * rows, HD), jnp.float32),
        )
        out_specs = (vmem, vmem)
    operands = [valid_counts, first_block, queries, *keys, *values, *(() if own else state)]
    return pl.pallas_call(
        functools.partial(attend_kernel, offsets, own, last, count, window_rows),
        out_shape=out_shape,
        in_specs=[smem, smem] + [vmem] * (len(operands) - 2),
        out_specs=out_specs,
        scratch_shapes=[
            pltpu.VMEM((kv_heads, total_keys, HD), jnp.bfloat16),
            pltpu.VMEM((kv_heads, total_keys, 2 * HD), jnp.bfloat16),
        ],
        compiler_params=pltpu.CompilerParams(vmem_limit_bytes=40 * 1024 * 1024),
        cost_estimate=pl.CostEstimate(
            flops=4 * heads * rows * total_keys * HD,
            bytes_accessed=2 * rows * width,
            transcendentals=heads * rows * total_keys,
        ),
        name="attend_%s" % ("first" if own else "last" if last else "next"),
    )(*operands)


def shards(count, queries, win_keys, win_values, cache_keys, cache_values, valid_counts, first_block):
    window_rows = win_keys.shape[0]
    ring = [place_at(p, count) for p in range(count)]
    onward = [(ring[p], ring[(p + 1) % count]) for p in range(count)]
    backward = [(b, a) for a, b in onward]
    keys = jnp.concatenate([win_keys, cache_keys], axis=0)
    values = jnp.concatenate([win_values, cache_values], axis=0)
    common = (queries, valid_counts, first_block, count, window_rows)

    arrived = []
    key_on = key_back = keys
    value_on = value_back = values
    half = count // 2
    for step in range(1, half + 1):
        key_on = lax.ppermute(key_on, "ctx", onward)
        value_back = lax.ppermute(value_back, "ctx", backward)
        if step < half:
            value_on = lax.ppermute(value_on, "ctx", onward)
            key_back = lax.ppermute(key_back, "ctx", backward)
            arrived.append([(-step, key_on, value_on), (step, key_back, value_back)])
        else:
            arrived.append([(step, key_on, value_back)])

    state = attend((0,), [keys], [values], None, False, *common)
    for begin in range(0, half, 2):
        pieces = [piece for step in arrived[begin : begin + 2] for piece in step]
        state = attend(
            tuple(p[0] for p in pieces),
            [p[1] for p in pieces],
            [p[2] for p in pieces],
            state,
            begin + 2 >= half,
            *common,
        )
    return state


def solution(mesh):
    in_specs = (
        P(("groups", "ctx"), "tp"),
        P(("groups", "ctx"), "tp"),
        P(("groups", "ctx"), "tp"),
        P(("groups", "ctx"), "tp"),
        P(("groups", "ctx"), "tp"),
        P("groups"),
        P("groups"),
    )
    out_specs = P(("groups", "ctx"), "tp")
    return jax.shard_map(
        functools.partial(shards, mesh.shape["ctx"]),
        mesh=mesh,
        in_specs=in_specs,
        out_specs=out_specs,
        check_vma=False,
    )
```

```python
import functools
import math

import jax
import jax.numpy as jnp
from jax import lax
from jax.experimental import pallas as pl
from jax.experimental.pallas import tpu as pltpu
from jax.sharding import PartitionSpec as P

HD = 128
EXP_SCALE = HD**-0.5 * math.log2(math.e)
HIDDEN = -1.0e30
CHUNK_HEADS = 4


def ring_width(count):
    width = round(count ** (1 / 3))
    if width > 1 and count % width == 0 and (count // width) % 2 == 0:
        return width
    return 1


def place_at(position, count):
    width = ring_width(count)
    if width == 1:
        return position
    rows = count // width
    row, step = position // (width - 1), position % (width - 1)
    forth = row * width + 1 + step
    back = row * width + width - 1 - step
    home = (rows - 1 - (position - rows * (width - 1))) * width
    if isinstance(position, int):
        return home if position >= rows * (width - 1) else (back if row % 2 else forth)
    return jnp.where(position >= rows * (width - 1), home, jnp.where(row % 2 == 1, back, forth))


def position_of(place, count):
    width = ring_width(count)
    if width == 1:
        return place
    rows = count // width
    row, column = place // width, place % width
    snake = row * (width - 1) + jnp.where(row % 2 == 1, width - 1 - column, column - 1)
    return jnp.where(column == 0, rows * (width - 1) + rows - 1 - row, snake)


def pack_kernel(win_keys, win_values, cache_keys, cache_values, packed, sems):
    start = 0
    copies = []
    for index, piece in enumerate((win_keys, cache_keys, win_values, cache_values)):
        rows = piece.shape[0]
        copies.append(pltpu.make_async_copy(piece, packed.at[start : start + rows], sems.at[index]))
        start += rows
    for copy in copies:
        copy.start()
    for copy in copies:
        copy.wait()


def pack(win_keys, win_values, cache_keys, cache_values):
    rows = 2 * (win_keys.shape[0] + cache_keys.shape[0])
    return pl.pallas_call(
        pack_kernel,
        out_shape=jax.ShapeDtypeStruct((rows, win_keys.shape[1]), win_keys.dtype),
        in_specs=[pl.BlockSpec(memory_space=pltpu.HBM)] * 4,
        out_specs=pl.BlockSpec(memory_space=pltpu.VMEM),
        scratch_shapes=[pltpu.SemaphoreType.DMA((4,))],
        cost_estimate=pl.CostEstimate(flops=0, bytes_accessed=4 * rows * win_keys.shape[1], transcendentals=0),
        name="pack",
    )(win_keys, win_values, cache_keys, cache_values)


def ring_offsets(count):
    half = count // 2
    return [sign * step for step in range(1, half) for sign in (-1, 1)] + [half]


def place_pieces(pieces, own, window_rows, cache_rows, limits, key_refs, value_refs, keys, values):
    stride = window_rows + cache_rows
    kv_heads, total_keys = keys.shape[:2]
    cache_at = len(pieces) * window_rows
    row_iota = lax.broadcasted_iota(jnp.int32, (window_rows, HD), 0)
    for index, (limit_row, key_base, value_base) in enumerate(pieces):
        key, value = key_refs[index], value_refs[index]
        if not own:
            shown = row_iota < limits[limit_row : limit_row + 1, :]
        for head in range(kv_heads):
            lanes = slice(head * HD, (head + 1) * HD)
            at = slice(index * window_rows, (index + 1) * window_rows)
            win_key = key[key_base : key_base + window_rows, lanes]
            win_value = value[value_base : value_base + window_rows, lanes]
            if own:
                keys[head, at, :] = win_key
                values[head, at, :HD] = win_value
                values[head, at, HD:] = jnp.ones((window_rows, HD), jnp.bfloat16)
            else:
                fill = key[key_base + window_rows : key_base + window_rows + 1, lanes].astype(jnp.float32)
                keys[head, at, :] = jnp.where(shown, win_key.astype(jnp.float32), fill).astype(jnp.bfloat16)
                values[head, at, :HD] = jnp.where(shown, win_value.astype(jnp.float32), 0.0).astype(jnp.bfloat16)
                values[head, at, HD:] = jnp.where(shown, 1.0, 0.0).astype(jnp.bfloat16)
            at = slice(cache_at + index * cache_rows, cache_at + (index + 1) * cache_rows)
            keys[head, at, :] = key[key_base + window_rows : key_base + stride, lanes]
            values[head, at, :HD] = value[value_base + window_rows : value_base + stride, lanes]
            values[head, at, HD:] = jnp.ones((cache_rows, HD), jnp.bfloat16)
    filled = len(pieces) * stride
    if filled < total_keys:
        key_base = pieces[0][1] + window_rows
        for head in range(kv_heads):
            row = key_refs[0][key_base : key_base + 1, head * HD : (head + 1) * HD].astype(jnp.float32)
            keys[head, filled:, :] = jnp.broadcast_to(row, (total_keys - filled, HD)).astype(jnp.bfloat16)
            values[head, filled:, :] = jnp.zeros((total_keys - filled, 2 * HD), jnp.bfloat16)


def absorb(query, keys, values, bias, before, acc_before):
    score = lax.dot_general(query, keys, (((1,), (1,)), ((), ())), preferred_element_type=jnp.float32)
    if bias is not None:
        width = bias.shape[1]
        score = jnp.concatenate([score[:, :width] + bias, score[:, width:]], axis=1)
    top = jnp.max(score, axis=1, keepdims=True)
    if before is not None:
        top = jnp.maximum(before[:, :1], top)
    weight = jnp.exp2((score - top) * EXP_SCALE).astype(jnp.bfloat16)
    acc = jnp.dot(weight, values, preferred_element_type=jnp.float32)
    if before is not None:
        fade = jnp.exp2((before - top) * EXP_SCALE)
        acc = acc + acc_before * jnp.concatenate([fade, fade], axis=1)
    return top, acc


def chunks(q_ref, kv_heads):
    rows = q_ref.shape[0]
    group = q_ref.shape[1] // HD // kv_heads
    for head in range(kv_heads):
        for start in range(0, group, CHUNK_HEADS):
            base = head * group + start
            query = jnp.concatenate(
                [q_ref[:, (base + i) * HD : (base + i + 1) * HD] for i in range(CHUNK_HEADS)], axis=0
            )
            yield head, slice(base * rows, (base + CHUNK_HEADS) * rows), query, base


def first_kernel(
    count, window_rows, cache_rows, valid_hbm, first_hbm, q_hbm, packed, acc_out, top_out, q_ref, limits,
    keys, values, valid_ref, first_ref, sems,
):
    copies = [
        pltpu.make_async_copy(valid_hbm, valid_ref, sems.at[0]),
        pltpu.make_async_copy(first_hbm, first_ref, sems.at[1]),
        pltpu.make_async_copy(q_hbm, q_ref, sems.at[2]),
    ]
    for copy in copies:
        copy.start()
    stride = window_rows + cache_rows
    place_pieces(((0, 0, stride),), True, window_rows, cache_rows, None, (packed,), (packed,), keys, values)
    for copy in copies:
        copy.wait()

    me = lax.axis_index("ctx")
    position = position_of(me, count)
    first = first_ref[me]
    for row, offset in enumerate(ring_offsets(count)):
        place = place_at(lax.rem(position + offset + count, count), count)
        limit = jnp.where((place >= first) & (place <= me), valid_ref[place], 0)
        limits[row : row + 1, :] = jnp.full((1, HD), limit, jnp.int32)

    rows = q_ref.shape[0]
    key_iota = lax.broadcasted_iota(jnp.int32, (rows, window_rows), 1)
    query_iota = lax.broadcasted_iota(jnp.int32, (rows, window_rows), 0)
    seen = (key_iota <= query_iota) & (key_iota < valid_ref[me])
    bias = jnp.concatenate([jnp.where(seen, 0.0, HIDDEN)] * CHUNK_HEADS, axis=0)
    for head, at, query, _ in chunks(q_ref, keys.shape[0]):
        top, acc = absorb(query, keys[head], values[head], bias, None, None)
        acc_out[at, :] = acc
        top_out[at, :] = jnp.broadcast_to(top, (top.shape[0], HD))


def next_kernel(pieces, last, window_rows, cache_rows, q_ref, limits, *refs):
    number = len(pieces)
    key_refs, value_refs = refs[:number], refs[number : 2 * number]
    acc_in, top_in, *outs, keys, values = refs[2 * number :]
    place_pieces(pieces, False, window_rows, cache_rows, limits, key_refs, value_refs, keys, values)
    rows = q_ref.shape[0]
    for head, at, query, base in chunks(q_ref, keys.shape[0]):
        top, acc = absorb(query, keys[head], values[head], None, top_in[at, :], acc_in[at, :])
        if last:
            result = (acc[:, :HD] / acc[:, HD:]).astype(jnp.bfloat16)
            for i in range(CHUNK_HEADS):
                outs[0][:, (base + i) * HD : (base + i + 1) * HD] = result[i * rows : (i + 1) * rows]
        else:
            outs[0][at, :] = acc
            outs[1][at, :] = jnp.broadcast_to(top, (top.shape[0], HD))


def kernel_options(queries, total_keys, kv_heads):
    rows, width = queries.shape
    return {
        "compiler_params": pltpu.CompilerParams(vmem_limit_bytes=40 * 1024 * 1024),
        "cost_estimate": pl.CostEstimate(
            flops=6 * rows * width * total_keys,
            bytes_accessed=2 * rows * width,
            transcendentals=rows * (width // HD) * total_keys,
        ),
    }


def room(kv_heads, total_keys):
    return [
        pltpu.VMEM((kv_heads, total_keys, HD), jnp.bfloat16),
        pltpu.VMEM((kv_heads, total_keys, 2 * HD), jnp.bfloat16),
    ]


def state_shapes(queries):
    rows = queries.shape[0] * queries.shape[1] // HD
    return [jax.ShapeDtypeStruct((rows, 2 * HD), jnp.float32), jax.ShapeDtypeStruct((rows, HD), jnp.float32)]


def attend_first(count, window_rows, cache_rows, valid_counts, first_block, queries, packed):
    kv_heads = packed.shape[1] // HD
    total_keys = -(-(window_rows + cache_rows) // HD) * HD
    vmem, anywhere = pl.BlockSpec(memory_space=pltpu.VMEM), pl.BlockSpec(memory_space=pltpu.HBM)
    acc, top, q_near, limits = pl.pallas_call(
        functools.partial(first_kernel, count, window_rows, cache_rows),
        out_shape=[
            *state_shapes(queries),
            jax.ShapeDtypeStruct(queries.shape, queries.dtype),
            jax.ShapeDtypeStruct((-(-count // 8) * 8, HD), jnp.int32),
        ],
        in_specs=[anywhere, anywhere, anywhere, vmem],
        out_specs=[vmem] * 4,
        scratch_shapes=[
            *room(kv_heads, total_keys),
            pltpu.SMEM(valid_counts.shape, jnp.int32),
            pltpu.SMEM(first_block.shape, jnp.int32),
            pltpu.SemaphoreType.DMA((3,)),
        ],
        name="attend_first",
        **kernel_options(queries, total_keys, kv_heads),
    )(valid_counts, first_block, queries, packed)
    return (acc, top), q_near, limits


def attend_next(pieces, keys, values, state, last, window_rows, cache_rows, queries, limits):
    kv_heads = keys[0].shape[1] // HD
    total_keys = -(-len(pieces) * (window_rows + cache_rows) // HD) * HD
    vmem = pl.BlockSpec(memory_space=pltpu.VMEM)
    operands = [queries, limits, *keys, *values, *state]
    shapes = [jax.ShapeDtypeStruct(queries.shape, queries.dtype)] if last else state_shapes(queries)
    outs = pl.pallas_call(
        functools.partial(next_kernel, tuple(pieces), last, window_rows, cache_rows),
        out_shape=shapes,
        in_specs=[vmem] * len(operands),
        out_specs=[vmem] * len(shapes),
        scratch_shapes=room(kv_heads, total_keys),
        name="attend_last" if last else "attend_next",
        **kernel_options(queries, total_keys, kv_heads),
    )(*operands)
    return outs[0] if last else tuple(outs)


def shards(count, queries, win_keys, win_values, cache_keys, cache_values, valid_counts, first_block):
    window_rows, cache_rows = win_keys.shape[0], cache_keys.shape[0]
    stride = window_rows + cache_rows
    half = count // 2
    ring = [place_at(p, count) for p in range(count)]
    onward = [(ring[p], ring[(p + 1) % count]) for p in range(count)]
    backward = [(b, a) for a, b in onward]

    win_keys, win_values, cache_keys, cache_values, valid_counts, first_block, queries = [
        pltpu.with_memory_space_constraint(x, pltpu.HBM)
        for x in (win_keys, win_values, cache_keys, cache_values, valid_counts, first_block, queries)
    ]
    on = back = pack(win_keys, win_values, cache_keys, cache_values)
    state = near = limits = None
    for step in range(1, half + 1):
        if step < half:
            next_on = lax.ppermute(on, "ctx", onward)
            next_back = lax.ppermute(back, "ctx", backward)
        else:
            next_on = lax.ppermute(on[:stride], "ctx", onward)
            next_back = lax.ppermute(back[stride:], "ctx", backward)
        if step == 1:
            state, near, limits = attend_first(
                count, window_rows, cache_rows, valid_counts, first_block, queries, on
            )
        else:
            row = 2 * (step - 2)
            pieces = [(row, 0, stride), (row + 1, 0, stride)]
            state = attend_next(
                pieces, [on, back], [on, back], state, False, window_rows, cache_rows, near, limits
            )
        on, top = lax.optimization_barrier((next_on, state[1]))
        back, top = lax.optimization_barrier((next_back, top))
        state = (state[0], top)
    pieces = [(2 * (half - 1), 0, 0)]
    return attend_next(pieces, [on], [back], state, True, window_rows, cache_rows, near, limits)


def solution(mesh):
    in_specs = (
        P(("groups", "ctx"), "tp"),
        P(("groups", "ctx"), "tp"),
        P(("groups", "ctx"), "tp"),
        P(("groups", "ctx"), "tp"),
        P(("groups", "ctx"), "tp"),
        P("groups"),
        P("groups"),
    )
    out_specs = P(("groups", "ctx"), "tp")
    return jax.shard_map(
        functools.partial(shards, mesh.shape["ctx"]),
        mesh=mesh,
        in_specs=in_specs,
        out_specs=out_specs,
        check_vma=False,
    )
```

```python
import functools
import math

import jax
import jax.numpy as jnp
from jax import lax
from jax.experimental import pallas as pl
from jax.experimental.pallas import tpu as pltpu
from jax.sharding import PartitionSpec as P

HD = 128
EXP_SCALE = HD**-0.5 * math.log2(math.e)
HIDDEN = -1.0e30
CHUNK_HEADS = 4
LARGEST_TOTAL = 2.0**100


def ring_width(count):
    width = round(count ** (1 / 3))
    if width > 1 and count % width == 0 and (count // width) % 2 == 0:
        return width
    return 1


def place_at(position, count):
    width = ring_width(count)
    if width == 1:
        return position
    rows = count // width
    row, step = position // (width - 1), position % (width - 1)
    forth = row * width + 1 + step
    back = row * width + width - 1 - step
    home = (rows - 1 - (position - rows * (width - 1))) * width
    if isinstance(position, int):
        return home if position >= rows * (width - 1) else (back if row % 2 else forth)
    return jnp.where(position >= rows * (width - 1), home, jnp.where(row % 2 == 1, back, forth))


def position_of(place, count):
    width = ring_width(count)
    if width == 1:
        return place
    rows = count // width
    row, column = place // width, place % width
    snake = row * (width - 1) + jnp.where(row % 2 == 1, width - 1 - column, column - 1)
    return jnp.where(column == 0, rows * (width - 1) + rows - 1 - row, snake)


def pack_kernel(win_keys, win_values, cache_keys, cache_values, packed, sems):
    start = 0
    copies = []
    for index, piece in enumerate((win_keys, cache_keys, win_values, cache_values)):
        rows = piece.shape[0]
        copies.append(pltpu.make_async_copy(piece, packed.at[start : start + rows], sems.at[index]))
        start += rows
    for copy in copies:
        copy.start()
    for copy in copies:
        copy.wait()


def pack(win_keys, win_values, cache_keys, cache_values):
    rows = 2 * (win_keys.shape[0] + cache_keys.shape[0])
    return pl.pallas_call(
        pack_kernel,
        out_shape=jax.ShapeDtypeStruct((rows, win_keys.shape[1]), win_keys.dtype),
        in_specs=[pl.BlockSpec(memory_space=pltpu.HBM)] * 4,
        out_specs=pl.BlockSpec(memory_space=pltpu.VMEM),
        scratch_shapes=[pltpu.SemaphoreType.DMA((4,))],
        compiler_params=pltpu.CompilerParams(vmem_limit_bytes=4 * 1024 * 1024),
        cost_estimate=pl.CostEstimate(flops=0, bytes_accessed=4 * rows * win_keys.shape[1], transcendentals=0),
        name="pack",
    )(win_keys, win_values, cache_keys, cache_values)


def ring_offsets(count):
    half = count // 2
    return [sign * step for step in range(1, half) for sign in (-1, 1)] + [half]


def place_pieces(pieces, own, window_rows, cache_rows, limits, key_refs, value_refs, keys, values):
    stride = window_rows + cache_rows
    kv_heads, total_keys = keys.shape[:2]
    cache_at = len(pieces) * window_rows
    row_iota = lax.broadcasted_iota(jnp.int32, (window_rows, HD), 0)
    for index, (limit_row, key_base, value_base) in enumerate(pieces):
        key, value = key_refs[index], value_refs[index]
        if not own:
            shown = row_iota < limits[limit_row : limit_row + 1, :]
        for head in range(kv_heads):
            lanes = slice(head * HD, (head + 1) * HD)
            at = slice(index * window_rows, (index + 1) * window_rows)
            win_key = key[key_base : key_base + window_rows, lanes]
            win_value = value[value_base : value_base + window_rows, lanes]
            if own:
                keys[head, at, :] = win_key
                values[head, at, :HD] = win_value
                values[head, at, HD:] = jnp.ones((window_rows, HD), jnp.bfloat16)
            else:
                fill = key[key_base + window_rows : key_base + window_rows + 1, lanes].astype(jnp.float32)
                keys[head, at, :] = jnp.where(shown, win_key.astype(jnp.float32), fill).astype(jnp.bfloat16)
                values[head, at, :HD] = jnp.where(shown, win_value.astype(jnp.float32), 0.0).astype(jnp.bfloat16)
                values[head, at, HD:] = jnp.where(shown, 1.0, 0.0).astype(jnp.bfloat16)
            at = slice(cache_at + index * cache_rows, cache_at + (index + 1) * cache_rows)
            keys[head, at, :] = key[key_base + window_rows : key_base + stride, lanes]
            values[head, at, :HD] = value[value_base + window_rows : value_base + stride, lanes]
            values[head, at, HD:] = jnp.ones((cache_rows, HD), jnp.bfloat16)
    filled = len(pieces) * stride
    if filled < total_keys:
        key_base = pieces[0][1] + window_rows
        for head in range(kv_heads):
            row = key_refs[0][key_base : key_base + 1, head * HD : (head + 1) * HD].astype(jnp.float32)
            keys[head, filled:, :] = jnp.broadcast_to(row, (total_keys - filled, HD)).astype(jnp.bfloat16)
            values[head, filled:, :] = jnp.zeros((total_keys - filled, 2 * HD), jnp.bfloat16)


def scores(query, keys):
    return lax.dot_general(query, keys, (((1,), (1,)), ((), ())), preferred_element_type=jnp.float32)


def weigh(score, top, values):
    lanes = score.shape[1] // HD
    weight = jnp.exp2(score * EXP_SCALE - jnp.concatenate([top] * lanes, axis=1)).astype(jnp.bfloat16)
    return jnp.dot(weight, values, preferred_element_type=jnp.float32)


def wide_top(score):
    return jnp.broadcast_to(jnp.max(score, axis=1, keepdims=True) * EXP_SCALE, (score.shape[0], HD))


def normalised(acc):
    total = acc[:, HD:]
    inverse = pl.reciprocal(total, approx=True)
    return (acc[:, :HD] * (inverse * (2.0 - total * inverse))).astype(jnp.bfloat16)


def chunks(q_ref, kv_heads):
    rows = q_ref.shape[0]
    group = q_ref.shape[1] // HD // kv_heads
    for head in range(kv_heads):
        for start in range(0, group, CHUNK_HEADS):
            base = head * group + start
            query = jnp.concatenate(
                [q_ref[:, (base + i) * HD : (base + i + 1) * HD] for i in range(CHUNK_HEADS)], axis=0
            )
            yield head, slice(base * rows, (base + CHUNK_HEADS) * rows), query, base


def first_kernel(
    count, window_rows, cache_rows, valid_hbm, first_hbm, q_hbm, packed, acc_out, top_out, q_ref, limits,
    keys, values, valid_ref, first_ref, sems,
):
    copies = [
        pltpu.make_async_copy(valid_hbm, valid_ref, sems.at[0]),
        pltpu.make_async_copy(first_hbm, first_ref, sems.at[1]),
        pltpu.make_async_copy(q_hbm, q_ref, sems.at[2]),
    ]
    for copy in copies:
        copy.start()
    stride = window_rows + cache_rows
    place_pieces(((0, 0, stride),), True, window_rows, cache_rows, None, (packed,), (packed,), keys, values)
    for copy in copies:
        copy.wait()

    me = lax.axis_index("ctx")
    position = position_of(me, count)
    first = first_ref[me]
    for row, offset in enumerate(ring_offsets(count)):
        place = place_at(lax.rem(position + offset + count, count), count)
        limit = jnp.where((place >= first) & (place <= me), valid_ref[place], 0)
        limits[row : row + 1, :] = jnp.full((1, HD), limit, jnp.int32)

    rows = q_ref.shape[0]
    key_iota = lax.broadcasted_iota(jnp.int32, (rows, window_rows), 1)
    query_iota = lax.broadcasted_iota(jnp.int32, (rows, window_rows), 0)
    seen = (key_iota <= query_iota) & (key_iota < valid_ref[me])
    bias = jnp.concatenate([jnp.where(seen, 0.0, HIDDEN)] * CHUNK_HEADS, axis=0)
    for head, at, query, _ in chunks(q_ref, keys.shape[0]):
        score = scores(query, keys[head])
        score = jnp.concatenate([score[:, :window_rows] + bias, score[:, window_rows:]], axis=1)
        top = wide_top(score)
        acc_out[at, :] = weigh(score, top, values[head])
        top_out[at, :] = top


def next_kernel(pieces, last, window_rows, cache_rows, q_ref, limits, *refs):
    number = len(pieces)
    key_refs, value_refs = refs[:number], refs[number : 2 * number]
    if last:
        acc_in, top_in, out, keys, values, result, sems = refs[2 * number :]
    else:
        acc_in, top_in, acc_out, top_out, keys, values = refs[2 * number :]
    place_pieces(pieces, False, window_rows, cache_rows, limits, key_refs, value_refs, keys, values)
    rows = q_ref.shape[0]
    kv_heads = keys.shape[0]

    def sent(base):
        lanes = slice(base * HD, (base + CHUNK_HEADS) * HD)
        return pltpu.make_async_copy(result.at[:, lanes], out.at[:, lanes], sems.at[base // CHUNK_HEADS])

    def settle(base, acc):
        done = normalised(acc)
        for i in range(CHUNK_HEADS):
            result[:, (base + i) * HD : (base + i + 1) * HD] = done[i * rows : (i + 1) * rows]
        sent(base).start()

    fine = jnp.ones((8, HD), jnp.float32)
    for head, at, query, base in chunks(q_ref, kv_heads):
        top = top_in[at, :]
        acc = acc_in[at, :] + weigh(scores(query, keys[head]), top, values[head])
        safe = jnp.where(acc[:, HD:] < LARGEST_TOTAL, 1.0, 0.0).reshape(-1, 8, HD)
        fine = jnp.minimum(fine, jnp.min(safe, axis=0))
        if last:
            settle(base, acc)
        else:
            acc_out[at, :] = acc
            top_out[at, :] = top
    if last:
        for base in range(0, kv_heads * (q_ref.shape[1] // HD // kv_heads), CHUNK_HEADS):
            sent(base).wait()

    @pl.when(jnp.min(fine) < 0.5)
    def _():
        for head, at, query, base in chunks(q_ref, kv_heads):
            score = scores(query, keys[head])
            before = top_in[at, :]
            top = jnp.maximum(before, wide_top(score))
            fade = jnp.exp2(before - top)
            acc = acc_in[at, :] * jnp.concatenate([fade, fade], axis=1) + weigh(score, top, values[head])
            if last:
                settle(base, acc)
                sent(base).wait()
            else:
                acc_out[at, :] = acc
                top_out[at, :] = top


def kernel_options(queries, total_keys, kv_heads):
    rows, width = queries.shape
    return {
        "compiler_params": pltpu.CompilerParams(vmem_limit_bytes=40 * 1024 * 1024),
        "cost_estimate": pl.CostEstimate(
            flops=6 * rows * width * total_keys,
            bytes_accessed=2 * rows * width,
            transcendentals=rows * (width // HD) * total_keys,
        ),
    }


def room(kv_heads, total_keys):
    return [
        pltpu.VMEM((kv_heads, total_keys, HD), jnp.bfloat16),
        pltpu.VMEM((kv_heads, total_keys, 2 * HD), jnp.bfloat16),
    ]


def state_shapes(queries):
    rows = queries.shape[0] * queries.shape[1] // HD
    return [jax.ShapeDtypeStruct((rows, 2 * HD), jnp.float32), jax.ShapeDtypeStruct((rows, HD), jnp.float32)]


def attend_first(count, window_rows, cache_rows, valid_counts, first_block, queries, packed):
    kv_heads = packed.shape[1] // HD
    total_keys = -(-(window_rows + cache_rows) // HD) * HD
    vmem, anywhere = pl.BlockSpec(memory_space=pltpu.VMEM), pl.BlockSpec(memory_space=pltpu.HBM)
    acc, top, q_near, limits = pl.pallas_call(
        functools.partial(first_kernel, count, window_rows, cache_rows),
        out_shape=[
            *state_shapes(queries),
            jax.ShapeDtypeStruct(queries.shape, queries.dtype),
            jax.ShapeDtypeStruct((-(-count // 8) * 8, HD), jnp.int32),
        ],
        in_specs=[anywhere, anywhere, anywhere, vmem],
        out_specs=[vmem] * 4,
        scratch_shapes=[
            *room(kv_heads, total_keys),
            pltpu.SMEM(valid_counts.shape, jnp.int32),
            pltpu.SMEM(first_block.shape, jnp.int32),
            pltpu.SemaphoreType.DMA((3,)),
        ],
        name="attend_first",
        **kernel_options(queries, total_keys, kv_heads),
    )(valid_counts, first_block, queries, packed)
    return (acc, top), q_near, limits


def attend_next(pieces, keys, values, state, last, window_rows, cache_rows, queries, limits):
    kv_heads = keys[0].shape[1] // HD
    total_keys = -(-len(pieces) * (window_rows + cache_rows) // HD) * HD
    vmem = pl.BlockSpec(memory_space=pltpu.VMEM)
    operands = [queries, limits, *keys, *values, *state]
    shapes = [jax.ShapeDtypeStruct(queries.shape, queries.dtype)] if last else state_shapes(queries)
    scratch = room(kv_heads, total_keys)
    if last:
        chunk_count = queries.shape[1] // HD // CHUNK_HEADS
        scratch += [pltpu.VMEM(queries.shape, queries.dtype), pltpu.SemaphoreType.DMA((chunk_count,))]
    outs = pl.pallas_call(
        functools.partial(next_kernel, tuple(pieces), last, window_rows, cache_rows),
        out_shape=shapes,
        in_specs=[vmem] * len(operands),
        out_specs=[pl.BlockSpec(memory_space=pltpu.HBM)] if last else [vmem] * len(shapes),
        scratch_shapes=scratch,
        name="attend_last" if last else "attend_next",
        **kernel_options(queries, total_keys, kv_heads),
    )(*operands)
    return outs[0] if last else tuple(outs)


def shards(count, queries, win_keys, win_values, cache_keys, cache_values, valid_counts, first_block):
    window_rows, cache_rows = win_keys.shape[0], cache_keys.shape[0]
    stride = window_rows + cache_rows
    half = count // 2
    ring = [place_at(p, count) for p in range(count)]
    onward = [(ring[p], ring[(p + 1) % count]) for p in range(count)]
    backward = [(b, a) for a, b in onward]

    win_keys, win_values, cache_keys, cache_values, valid_counts, first_block, queries = [
        pltpu.with_memory_space_constraint(x, pltpu.HBM)
        for x in (win_keys, win_values, cache_keys, cache_values, valid_counts, first_block, queries)
    ]
    on = back = pack(win_keys, win_values, cache_keys, cache_values)
    state = near = limits = None
    for step in range(1, half + 1):
        if step < half:
            next_on = lax.ppermute(on, "ctx", onward)
            next_back = lax.ppermute(back, "ctx", backward)
        else:
            next_on = lax.ppermute(on[:stride], "ctx", onward)
            next_back = lax.ppermute(back[stride:], "ctx", backward)
        if step == 1:
            state, near, limits = attend_first(
                count, window_rows, cache_rows, valid_counts, first_block, queries, on
            )
        else:
            row = 2 * (step - 2)
            pieces = [(row, 0, stride), (row + 1, 0, stride)]
            state = attend_next(
                pieces, [on, back], [on, back], state, False, window_rows, cache_rows, near, limits
            )
        on, top = lax.optimization_barrier((next_on, state[1]))
        back, top = lax.optimization_barrier((next_back, top))
        state = (state[0], top)
    pieces = [(2 * (half - 1), 0, 0)]
    return attend_next(pieces, [on], [back], state, True, window_rows, cache_rows, near, limits)


def solution(mesh):
    in_specs = (
        P(("groups", "ctx"), "tp"),
        P(("groups", "ctx"), "tp"),
        P(("groups", "ctx"), "tp"),
        P(("groups", "ctx"), "tp"),
        P(("groups", "ctx"), "tp"),
        P("groups"),
        P("groups"),
    )
    out_specs = P(("groups", "ctx"), "tp")
    return jax.shard_map(
        functools.partial(shards, mesh.shape["ctx"]),
        mesh=mesh,
        in_specs=in_specs,
        out_specs=out_specs,
        check_vma=False,
    )
```

```python
import functools
import math

import jax
import jax.numpy as jnp
from jax import lax
from jax.experimental import pallas as pl
from jax.experimental.pallas import tpu as pltpu
from jax.sharding import PartitionSpec as P

HD = 128
EXP_SCALE = HD**-0.5 * math.log2(math.e)
HIDDEN = -1.0e30
CHUNK_HEADS = 4
LARGEST_TOTAL = 2.0**100


def ring_width(count):
    width = round(count ** (1 / 3))
    if width > 1 and count % width == 0 and (count // width) % 2 == 0:
        return width
    return 1


def place_at(position, count):
    width = ring_width(count)
    if width == 1:
        return position
    rows = count // width
    row, step = position // (width - 1), position % (width - 1)
    forth = row * width + 1 + step
    back = row * width + width - 1 - step
    home = (rows - 1 - (position - rows * (width - 1))) * width
    if isinstance(position, int):
        return home if position >= rows * (width - 1) else (back if row % 2 else forth)
    return jnp.where(position >= rows * (width - 1), home, jnp.where(row % 2 == 1, back, forth))


def position_of(place, count):
    width = ring_width(count)
    if width == 1:
        return place
    rows = count // width
    row, column = place // width, place % width
    snake = row * (width - 1) + jnp.where(row % 2 == 1, width - 1 - column, column - 1)
    return jnp.where(column == 0, rows * (width - 1) + rows - 1 - row, snake)


def pack_kernel(win_keys, win_values, cache_keys, cache_values, packed, sems):
    start = 0
    copies = []
    for index, piece in enumerate((win_keys, cache_keys, win_values, cache_values)):
        rows = piece.shape[0]
        copies.append(pltpu.make_async_copy(piece, packed.at[start : start + rows], sems.at[index]))
        start += rows
    for copy in copies:
        copy.start()
    for copy in copies:
        copy.wait()


def pack(win_keys, win_values, cache_keys, cache_values):
    rows = 2 * (win_keys.shape[0] + cache_keys.shape[0])
    return pl.pallas_call(
        pack_kernel,
        out_shape=jax.ShapeDtypeStruct((rows, win_keys.shape[1]), win_keys.dtype),
        in_specs=[pl.BlockSpec(memory_space=pltpu.HBM)] * 4,
        out_specs=pl.BlockSpec(memory_space=pltpu.VMEM),
        scratch_shapes=[pltpu.SemaphoreType.DMA((4,))],
        compiler_params=pltpu.CompilerParams(vmem_limit_bytes=4 * 1024 * 1024),
        cost_estimate=pl.CostEstimate(flops=0, bytes_accessed=4 * rows * win_keys.shape[1], transcendentals=0),
        name="pack",
    )(win_keys, win_values, cache_keys, cache_values)


def ring_offsets(count):
    half = count // 2
    return [sign * step for step in range(1, half) for sign in (-1, 1)] + [half]


def place_pieces(pieces, own, window_rows, cache_rows, limits, key_refs, value_refs, keys, values):
    stride = window_rows + cache_rows
    kv_heads, total_keys = keys.shape[:2]
    cache_at = len(pieces) * window_rows
    row_iota = lax.broadcasted_iota(jnp.int32, (window_rows, HD), 0)
    for index, (limit_row, key_base, value_base) in enumerate(pieces):
        key, value = key_refs[index], value_refs[index]
        if not own:
            shown = row_iota < limits[limit_row : limit_row + 1, :]
        for head in range(kv_heads):
            lanes = slice(head * HD, (head + 1) * HD)
            at = slice(index * window_rows, (index + 1) * window_rows)
            win_key = key[key_base : key_base + window_rows, lanes]
            win_value = value[value_base : value_base + window_rows, lanes]
            if own:
                keys[head, at, :] = win_key
                values[head, at, :HD] = win_value
                values[head, at, HD:] = jnp.ones((window_rows, HD), jnp.bfloat16)
            else:
                fill = key[key_base + window_rows : key_base + window_rows + 1, lanes].astype(jnp.float32)
                keys[head, at, :] = jnp.where(shown, win_key.astype(jnp.float32), fill).astype(jnp.bfloat16)
                values[head, at, :HD] = jnp.where(shown, win_value.astype(jnp.float32), 0.0).astype(jnp.bfloat16)
                values[head, at, HD:] = jnp.where(shown, 1.0, 0.0).astype(jnp.bfloat16)
            at = slice(cache_at + index * cache_rows, cache_at + (index + 1) * cache_rows)
            keys[head, at, :] = key[key_base + window_rows : key_base + stride, lanes]
            values[head, at, :HD] = value[value_base + window_rows : value_base + stride, lanes]
            values[head, at, HD:] = jnp.ones((cache_rows, HD), jnp.bfloat16)
    filled = len(pieces) * stride
    if filled < total_keys:
        key_base = pieces[0][1] + window_rows
        for head in range(kv_heads):
            row = key_refs[0][key_base : key_base + 1, head * HD : (head + 1) * HD].astype(jnp.float32)
            keys[head, filled:, :] = jnp.broadcast_to(row, (total_keys - filled, HD)).astype(jnp.bfloat16)
            values[head, filled:, :] = jnp.zeros((total_keys - filled, 2 * HD), jnp.bfloat16)


def scores(query, keys):
    return lax.dot_general(query, keys, (((1,), (1,)), ((), ())), preferred_element_type=jnp.float32)


def weigh(score, top, values):
    lanes = score.shape[1] // HD
    weight = jnp.exp2(score * EXP_SCALE - jnp.concatenate([top] * lanes, axis=1)).astype(jnp.bfloat16)
    return jnp.dot(weight, values, preferred_element_type=jnp.float32)


def wide_top(score):
    return jnp.broadcast_to(jnp.max(score, axis=1, keepdims=True) * EXP_SCALE, (score.shape[0], HD))


def normalised(acc):
    total = acc[:, HD:]
    inverse = pl.reciprocal(total, approx=True)
    return (acc[:, :HD] * (inverse * (2.0 - total * inverse))).astype(jnp.bfloat16)


def chunks(q_ref, kv_heads):
    rows = q_ref.shape[0]
    group = q_ref.shape[1] // HD // kv_heads
    for head in range(kv_heads):
        for start in range(0, group, CHUNK_HEADS):
            base = head * group + start
            query = jnp.concatenate(
                [q_ref[:, (base + i) * HD : (base + i + 1) * HD] for i in range(CHUNK_HEADS)], axis=0
            )
            yield head, slice(base * rows, (base + CHUNK_HEADS) * rows), query, base


def first_kernel(
    count, window_rows, cache_rows, valid_hbm, first_hbm, q_hbm, packed, acc_out, top_out, q_ref, limits,
    keys, values, valid_ref, first_ref, sems,
):
    copies = [
        pltpu.make_async_copy(valid_hbm, valid_ref, sems.at[0]),
        pltpu.make_async_copy(first_hbm, first_ref, sems.at[1]),
        pltpu.make_async_copy(q_hbm, q_ref, sems.at[2]),
    ]
    for copy in copies:
        copy.start()
    stride = window_rows + cache_rows
    place_pieces(((0, 0, stride),), True, window_rows, cache_rows, None, (packed,), (packed,), keys, values)
    for copy in copies:
        copy.wait()

    me = lax.axis_index("ctx")
    position = position_of(me, count)
    first = first_ref[me]
    sign = 1 - 2 * lax.rem(lax.axis_index("tp"), 2)
    for row, offset in enumerate(ring_offsets(count)):
        place = place_at(lax.rem(position + sign * offset + count, count), count)
        limit = jnp.where((place >= first) & (place <= me), valid_ref[place], 0)
        limits[row : row + 1, :] = jnp.full((1, HD), limit, jnp.int32)

    rows = q_ref.shape[0]
    key_iota = lax.broadcasted_iota(jnp.int32, (rows, window_rows), 1)
    query_iota = lax.broadcasted_iota(jnp.int32, (rows, window_rows), 0)
    seen = (key_iota <= query_iota) & (key_iota < valid_ref[me])
    bias = jnp.concatenate([jnp.where(seen, 0.0, HIDDEN)] * CHUNK_HEADS, axis=0)
    for head, at, query, _ in chunks(q_ref, keys.shape[0]):
        score = scores(query, keys[head])
        score = jnp.concatenate([score[:, :window_rows] + bias, score[:, window_rows:]], axis=1)
        top = wide_top(score)
        acc_out[at, :] = weigh(score, top, values[head])
        top_out[at, :] = top


def next_kernel(pieces, last, window_rows, cache_rows, q_ref, limits, *refs):
    number = len(pieces)
    key_refs, value_refs = refs[:number], refs[number : 2 * number]
    if last:
        acc_in, top_in, out, keys, values, result, sems = refs[2 * number :]
    else:
        acc_in, top_in, acc_out, top_out, keys, values = refs[2 * number :]
    place_pieces(pieces, False, window_rows, cache_rows, limits, key_refs, value_refs, keys, values)
    rows = q_ref.shape[0]
    kv_heads = keys.shape[0]

    def sent(base):
        lanes = slice(base * HD, (base + CHUNK_HEADS) * HD)
        return pltpu.make_async_copy(result.at[:, lanes], out.at[:, lanes], sems.at[base // CHUNK_HEADS])

    def settle(base, acc):
        done = normalised(acc)
        for i in range(CHUNK_HEADS):
            result[:, (base + i) * HD : (base + i + 1) * HD] = done[i * rows : (i + 1) * rows]
        sent(base).start()

    fine = jnp.ones((8, HD), jnp.float32)
    for head, at, query, base in chunks(q_ref, kv_heads):
        top = top_in[at, :]
        acc = acc_in[at, :] + weigh(scores(query, keys[head]), top, values[head])
        safe = jnp.where(acc[:, HD:] < LARGEST_TOTAL, 1.0, 0.0).reshape(-1, 8, HD)
        fine = jnp.minimum(fine, jnp.min(safe, axis=0))
        if last:
            settle(base, acc)
        else:
            acc_out[at, :] = acc
            top_out[at, :] = top
    if last:
        for base in range(0, kv_heads * (q_ref.shape[1] // HD // kv_heads), CHUNK_HEADS):
            sent(base).wait()

    @pl.when(jnp.min(fine) < 0.5)
    def _():
        for head, at, query, base in chunks(q_ref, kv_heads):
            score = scores(query, keys[head])
            before = top_in[at, :]
            top = jnp.maximum(before, wide_top(score))
            fade = jnp.exp2(before - top)
            acc = acc_in[at, :] * jnp.concatenate([fade, fade], axis=1) + weigh(score, top, values[head])
            if last:
                settle(base, acc)
                sent(base).wait()
            else:
                acc_out[at, :] = acc
                top_out[at, :] = top


def kernel_options(queries, total_keys, kv_heads):
    rows, width = queries.shape
    return {
        "compiler_params": pltpu.CompilerParams(vmem_limit_bytes=40 * 1024 * 1024),
        "cost_estimate": pl.CostEstimate(
            flops=6 * rows * width * total_keys,
            bytes_accessed=2 * rows * width,
            transcendentals=rows * (width // HD) * total_keys,
        ),
    }


def room(kv_heads, total_keys):
    return [
        pltpu.VMEM((kv_heads, total_keys, HD), jnp.bfloat16),
        pltpu.VMEM((kv_heads, total_keys, 2 * HD), jnp.bfloat16),
    ]


def state_shapes(queries):
    rows = queries.shape[0] * queries.shape[1] // HD
    return [jax.ShapeDtypeStruct((rows, 2 * HD), jnp.float32), jax.ShapeDtypeStruct((rows, HD), jnp.float32)]


def attend_first(count, window_rows, cache_rows, valid_counts, first_block, queries, packed):
    kv_heads = packed.shape[1] // HD
    total_keys = -(-(window_rows + cache_rows) // HD) * HD
    vmem, anywhere = pl.BlockSpec(memory_space=pltpu.VMEM), pl.BlockSpec(memory_space=pltpu.HBM)
    acc, top, q_near, limits = pl.pallas_call(
        functools.partial(first_kernel, count, window_rows, cache_rows),
        out_shape=[
            *state_shapes(queries),
            jax.ShapeDtypeStruct(queries.shape, queries.dtype),
            jax.ShapeDtypeStruct((-(-count // 8) * 8, HD), jnp.int32),
        ],
        in_specs=[anywhere, anywhere, anywhere, vmem],
        out_specs=[vmem] * 4,
        scratch_shapes=[
            *room(kv_heads, total_keys),
            pltpu.SMEM(valid_counts.shape, jnp.int32),
            pltpu.SMEM(first_block.shape, jnp.int32),
            pltpu.SemaphoreType.DMA((3,)),
        ],
        name="attend_first",
        **kernel_options(queries, total_keys, kv_heads),
    )(valid_counts, first_block, queries, packed)
    return (acc, top), q_near, limits


def attend_next(pieces, keys, values, state, last, window_rows, cache_rows, queries, limits):
    kv_heads = keys[0].shape[1] // HD
    total_keys = -(-len(pieces) * (window_rows + cache_rows) // HD) * HD
    vmem = pl.BlockSpec(memory_space=pltpu.VMEM)
    operands = [queries, limits, *keys, *values, *state]
    shapes = [jax.ShapeDtypeStruct(queries.shape, queries.dtype)] if last else state_shapes(queries)
    scratch = room(kv_heads, total_keys)
    if last:
        chunk_count = queries.shape[1] // HD // CHUNK_HEADS
        scratch += [pltpu.VMEM(queries.shape, queries.dtype), pltpu.SemaphoreType.DMA((chunk_count,))]
    outs = pl.pallas_call(
        functools.partial(next_kernel, tuple(pieces), last, window_rows, cache_rows),
        out_shape=shapes,
        in_specs=[vmem] * len(operands),
        out_specs=[pl.BlockSpec(memory_space=pltpu.HBM)] if last else [vmem] * len(shapes),
        scratch_shapes=scratch,
        name="attend_last" if last else "attend_next",
        **kernel_options(queries, total_keys, kv_heads),
    )(*operands)
    return outs[0] if last else tuple(outs)


def ring_pairs(count, cores, flip):
    ring = [place_at(p, count) for p in range(count)]
    pairs = []
    for core in range(cores):
        step = -1 if (core + flip) % 2 else 1
        for p in range(count):
            pairs.append((ring[p] * cores + core, ring[(p + step) % count] * cores + core))
    return pairs


def shards(count, cores, queries, win_keys, win_values, cache_keys, cache_values, valid_counts, first_block):
    window_rows, cache_rows = win_keys.shape[0], cache_keys.shape[0]
    stride = window_rows + cache_rows
    half = count // 2
    sizes = (window_rows, cache_rows)
    send_a = functools.partial(lax.ppermute, axis_name=("ctx", "tp"), perm=ring_pairs(count, cores, 0))
    send_b = functools.partial(lax.ppermute, axis_name=("ctx", "tp"), perm=ring_pairs(count, cores, 1))

    win_keys, win_values, cache_keys, cache_values, valid_counts, first_block, queries = [
        pltpu.with_memory_space_constraint(x, pltpu.HBM)
        for x in (win_keys, win_values, cache_keys, cache_values, valid_counts, first_block, queries)
    ]
    packed = pack(win_keys, win_values, cache_keys, cache_values)
    a = send_a(packed)
    state, near, limits = attend_first(count, *sizes, valid_counts, first_block, queries, packed)
    packed, top = lax.optimization_barrier((packed, state[1]))
    state = (state[0], top)
    b = send_b(packed) if half > 1 else None
    for step in range(1, half):
        a, top = lax.optimization_barrier((a, state[1]))
        next_a = send_a(a)
        next_b = send_b(b) if step + 1 < half else None
        row = 2 * (step - 1)
        pieces = [(row, 0, stride), (row + 1, 0, stride)]
        state = attend_next(pieces, [a, b], [a, b], (state[0], top), False, *sizes, near, limits)
        a, b = next_a, next_b
    return attend_next([(2 * (half - 1), 0, stride)], [a], [a], state, True, *sizes, near, limits)


def solution(mesh):
    in_specs = (
        P(("groups", "ctx"), "tp"),
        P(("groups", "ctx"), "tp"),
        P(("groups", "ctx"), "tp"),
        P(("groups", "ctx"), "tp"),
        P(("groups", "ctx"), "tp"),
        P("groups"),
        P("groups"),
    )
    out_specs = P(("groups", "ctx"), "tp")
    return jax.shard_map(
        functools.partial(shards, mesh.shape["ctx"], mesh.shape["tp"]),
        mesh=mesh,
        in_specs=in_specs,
        out_specs=out_specs,
        check_vma=False,
    )
```

```python
import functools
import math

import jax
import jax.numpy as jnp
from jax import lax
from jax.experimental import pallas as pl
from jax.experimental.pallas import tpu as pltpu
from jax.sharding import PartitionSpec as P

HD = 128
EXP_SCALE = HD**-0.5 * math.log2(math.e)
HIDDEN = -1.0e30
CHUNK_HEADS = 4
LARGEST_TOTAL = 2.0**100


def ring_width(count):
    width = round(count ** (1 / 3))
    if width > 1 and count % width == 0 and (count // width) % 2 == 0:
        return width
    return 1


def place_at(position, count):
    width = ring_width(count)
    if width == 1:
        return position
    rows = count // width
    row, step = position // (width - 1), position % (width - 1)
    forth = row * width + 1 + step
    back = row * width + width - 1 - step
    home = (rows - 1 - (position - rows * (width - 1))) * width
    if isinstance(position, int):
        return home if position >= rows * (width - 1) else (back if row % 2 else forth)
    return jnp.where(position >= rows * (width - 1), home, jnp.where(row % 2 == 1, back, forth))


def position_of(place, count):
    width = ring_width(count)
    if width == 1:
        return place
    rows = count // width
    row, column = place // width, place % width
    snake = row * (width - 1) + jnp.where(row % 2 == 1, width - 1 - column, column - 1)
    return jnp.where(column == 0, rows * (width - 1) + rows - 1 - row, snake)


def pack_kernel(win_keys, win_values, cache_keys, cache_values, packed, sems):
    start = 0
    copies = []
    for index, piece in enumerate((win_keys, cache_keys, win_values, cache_values)):
        rows = piece.shape[0]
        copies.append(pltpu.make_async_copy(piece, packed.at[start : start + rows], sems.at[index]))
        start += rows
    for copy in copies:
        copy.start()
    for copy in copies:
        copy.wait()


def pack(win_keys, win_values, cache_keys, cache_values):
    rows = 2 * (win_keys.shape[0] + cache_keys.shape[0])
    return pl.pallas_call(
        pack_kernel,
        out_shape=jax.ShapeDtypeStruct((rows, win_keys.shape[1]), win_keys.dtype),
        in_specs=[pl.BlockSpec(memory_space=pltpu.HBM)] * 4,
        out_specs=pl.BlockSpec(memory_space=pltpu.VMEM),
        scratch_shapes=[pltpu.SemaphoreType.DMA((4,))],
        compiler_params=pltpu.CompilerParams(vmem_limit_bytes=4 * 1024 * 1024),
        cost_estimate=pl.CostEstimate(flops=0, bytes_accessed=4 * rows * win_keys.shape[1], transcendentals=0),
        name="pack",
    )(win_keys, win_values, cache_keys, cache_values)


def ring_offsets(count):
    half = count // 2
    offsets = []
    for step in range(1, half):
        side = 1 if step % 2 else -1
        offsets += [side * step, -side * step]
    return offsets + [half]


def place_pieces(pieces, own, window_rows, cache_rows, limits, key_refs, value_refs, keys, values):
    stride = window_rows + cache_rows
    kv_heads, total_keys = keys.shape[:2]
    cache_at = len(pieces) * window_rows
    row_iota = lax.broadcasted_iota(jnp.int32, (window_rows, HD), 0)
    for index, (limit_row, key_base, value_base) in enumerate(pieces):
        key, value = key_refs[index], value_refs[index]
        if not own:
            shown = row_iota < limits[limit_row : limit_row + 1, :]
        for head in range(kv_heads):
            lanes = slice(head * HD, (head + 1) * HD)
            at = slice(index * window_rows, (index + 1) * window_rows)
            win_key = key[key_base : key_base + window_rows, lanes]
            win_value = value[value_base : value_base + window_rows, lanes]
            if own:
                keys[head, at, :] = win_key
                values[head, at, :HD] = win_value
                values[head, at, HD:] = jnp.ones((window_rows, HD), jnp.bfloat16)
            else:
                fill = key[key_base + window_rows : key_base + window_rows + 1, lanes].astype(jnp.float32)
                keys[head, at, :] = jnp.where(shown, win_key.astype(jnp.float32), fill).astype(jnp.bfloat16)
                values[head, at, :HD] = jnp.where(shown, win_value.astype(jnp.float32), 0.0).astype(jnp.bfloat16)
                values[head, at, HD:] = jnp.where(shown, 1.0, 0.0).astype(jnp.bfloat16)
            at = slice(cache_at + index * cache_rows, cache_at + (index + 1) * cache_rows)
            keys[head, at, :] = key[key_base + window_rows : key_base + stride, lanes]
            values[head, at, :HD] = value[value_base + window_rows : value_base + stride, lanes]
            values[head, at, HD:] = jnp.ones((cache_rows, HD), jnp.bfloat16)
    filled = len(pieces) * stride
    if filled < total_keys:
        key_base = pieces[0][1] + window_rows
        for head in range(kv_heads):
            row = key_refs[0][key_base : key_base + 1, head * HD : (head + 1) * HD].astype(jnp.float32)
            keys[head, filled:, :] = jnp.broadcast_to(row, (total_keys - filled, HD)).astype(jnp.bfloat16)
            values[head, filled:, :] = jnp.zeros((total_keys - filled, 2 * HD), jnp.bfloat16)


def scores(query, keys):
    return lax.dot_general(query, keys, (((1,), (1,)), ((), ())), preferred_element_type=jnp.float32)


def weigh(score, top, values):
    lanes = score.shape[1] // HD
    weight = jnp.exp2(score * EXP_SCALE - jnp.concatenate([top] * lanes, axis=1)).astype(jnp.bfloat16)
    return jnp.dot(weight, values, preferred_element_type=jnp.float32)


def wide_top(score):
    return jnp.broadcast_to(jnp.max(score, axis=1, keepdims=True) * EXP_SCALE, (score.shape[0], HD))


def normalised(acc):
    total = acc[:, HD:]
    inverse = pl.reciprocal(total, approx=True)
    return (acc[:, :HD] * (inverse * (2.0 - total * inverse))).astype(jnp.bfloat16)


def chunks(q_ref, kv_heads):
    rows = q_ref.shape[0]
    group = q_ref.shape[1] // HD // kv_heads
    for head in range(kv_heads):
        for start in range(0, group, CHUNK_HEADS):
            base = head * group + start
            query = jnp.concatenate(
                [q_ref[:, (base + i) * HD : (base + i + 1) * HD] for i in range(CHUNK_HEADS)], axis=0
            )
            yield head, slice(base * rows, (base + CHUNK_HEADS) * rows), query, base


def first_kernel(
    count, window_rows, cache_rows, valid_hbm, first_hbm, q_hbm, packed, acc_out, top_out, q_ref, limits,
    keys, values, valid_ref, first_ref, sems,
):
    copies = [
        pltpu.make_async_copy(valid_hbm, valid_ref, sems.at[0]),
        pltpu.make_async_copy(first_hbm, first_ref, sems.at[1]),
        pltpu.make_async_copy(q_hbm, q_ref, sems.at[2]),
    ]
    for copy in copies:
        copy.start()
    stride = window_rows + cache_rows
    place_pieces(((0, 0, stride),), True, window_rows, cache_rows, None, (packed,), (packed,), keys, values)
    for copy in copies:
        copy.wait()

    me = lax.axis_index("ctx")
    position = position_of(me, count)
    first = first_ref[me]
    sign = 2 * lax.rem(position, 2) - 1
    for row, offset in enumerate(ring_offsets(count)):
        place = place_at(lax.rem(position + sign * offset + count, count), count)
        limit = jnp.where((place >= first) & (place <= me), valid_ref[place], 0)
        limits[row : row + 1, :] = jnp.full((1, HD), limit, jnp.int32)

    rows = q_ref.shape[0]
    key_iota = lax.broadcasted_iota(jnp.int32, (rows, window_rows), 1)
    query_iota = lax.broadcasted_iota(jnp.int32, (rows, window_rows), 0)
    seen = (key_iota <= query_iota) & (key_iota < valid_ref[me])
    bias = jnp.concatenate([jnp.where(seen, 0.0, HIDDEN)] * CHUNK_HEADS, axis=0)
    for head, at, query, _ in chunks(q_ref, keys.shape[0]):
        score = scores(query, keys[head])
        score = jnp.concatenate([score[:, :window_rows] + bias, score[:, window_rows:]], axis=1)
        top = wide_top(score)
        acc_out[at, :] = weigh(score, top, values[head])
        top_out[at, :] = top


def next_kernel(pieces, last, window_rows, cache_rows, q_ref, limits, *refs):
    number = len(pieces)
    key_refs, value_refs = refs[:number], refs[number : 2 * number]
    if last:
        acc_in, top_in, out, keys, values, result, sems = refs[2 * number :]
    else:
        acc_in, top_in, acc_out, top_out, keys, values = refs[2 * number :]
    place_pieces(pieces, False, window_rows, cache_rows, limits, key_refs, value_refs, keys, values)
    rows = q_ref.shape[0]
    kv_heads = keys.shape[0]

    def sent(base):
        lanes = slice(base * HD, (base + CHUNK_HEADS) * HD)
        return pltpu.make_async_copy(result.at[:, lanes], out.at[:, lanes], sems.at[base // CHUNK_HEADS])

    def settle(base, acc):
        done = normalised(acc)
        for i in range(CHUNK_HEADS):
            result[:, (base + i) * HD : (base + i + 1) * HD] = done[i * rows : (i + 1) * rows]
        sent(base).start()

    fine = jnp.ones((8, HD), jnp.float32)
    for head, at, query, base in chunks(q_ref, kv_heads):
        top = top_in[at, :]
        acc = acc_in[at, :] + weigh(scores(query, keys[head]), top, values[head])
        safe = jnp.where(acc[:, HD:] < LARGEST_TOTAL, 1.0, 0.0).reshape(-1, 8, HD)
        fine = jnp.minimum(fine, jnp.min(safe, axis=0))
        if last:
            settle(base, acc)
        else:
            acc_out[at, :] = acc
            top_out[at, :] = top
    if last:
        for base in range(0, kv_heads * (q_ref.shape[1] // HD // kv_heads), CHUNK_HEADS):
            sent(base).wait()

    @pl.when(jnp.min(fine) < 0.5)
    def _():
        for head, at, query, base in chunks(q_ref, kv_heads):
            score = scores(query, keys[head])
            before = top_in[at, :]
            top = jnp.maximum(before, wide_top(score))
            fade = jnp.exp2(before - top)
            acc = acc_in[at, :] * jnp.concatenate([fade, fade], axis=1) + weigh(score, top, values[head])
            if last:
                settle(base, acc)
                sent(base).wait()
            else:
                acc_out[at, :] = acc
                top_out[at, :] = top


def kernel_options(queries, total_keys, kv_heads):
    rows, width = queries.shape
    return {
        "compiler_params": pltpu.CompilerParams(vmem_limit_bytes=40 * 1024 * 1024),
        "cost_estimate": pl.CostEstimate(
            flops=6 * rows * width * total_keys,
            bytes_accessed=2 * rows * width,
            transcendentals=rows * (width // HD) * total_keys,
        ),
    }


def room(kv_heads, total_keys):
    return [
        pltpu.VMEM((kv_heads, total_keys, HD), jnp.bfloat16),
        pltpu.VMEM((kv_heads, total_keys, 2 * HD), jnp.bfloat16),
    ]


def state_shapes(queries):
    rows = queries.shape[0] * queries.shape[1] // HD
    return [jax.ShapeDtypeStruct((rows, 2 * HD), jnp.float32), jax.ShapeDtypeStruct((rows, HD), jnp.float32)]


def attend_first(count, window_rows, cache_rows, valid_counts, first_block, queries, packed):
    kv_heads = packed.shape[1] // HD
    total_keys = -(-(window_rows + cache_rows) // HD) * HD
    vmem, anywhere = pl.BlockSpec(memory_space=pltpu.VMEM), pl.BlockSpec(memory_space=pltpu.HBM)
    acc, top, q_near, limits = pl.pallas_call(
        functools.partial(first_kernel, count, window_rows, cache_rows),
        out_shape=[
            *state_shapes(queries),
            jax.ShapeDtypeStruct(queries.shape, queries.dtype),
            jax.ShapeDtypeStruct((-(-count // 8) * 8, HD), jnp.int32),
        ],
        in_specs=[anywhere, anywhere, anywhere, vmem],
        out_specs=[vmem] * 4,
        scratch_shapes=[
            *room(kv_heads, total_keys),
            pltpu.SMEM(valid_counts.shape, jnp.int32),
            pltpu.SMEM(first_block.shape, jnp.int32),
            pltpu.SemaphoreType.DMA((3,)),
        ],
        name="attend_first",
        **kernel_options(queries, total_keys, kv_heads),
    )(valid_counts, first_block, queries, packed)
    return (acc, top), q_near, limits


def attend_next(pieces, keys, values, state, last, window_rows, cache_rows, queries, limits):
    kv_heads = keys[0].shape[1] // HD
    total_keys = -(-len(pieces) * (window_rows + cache_rows) // HD) * HD
    vmem = pl.BlockSpec(memory_space=pltpu.VMEM)
    operands = [queries, limits, *keys, *values, *state]
    shapes = [jax.ShapeDtypeStruct(queries.shape, queries.dtype)] if last else state_shapes(queries)
    scratch = room(kv_heads, total_keys)
    if last:
        chunk_count = queries.shape[1] // HD // CHUNK_HEADS
        scratch += [pltpu.VMEM(queries.shape, queries.dtype), pltpu.SemaphoreType.DMA((chunk_count,))]
    outs = pl.pallas_call(
        functools.partial(next_kernel, tuple(pieces), last, window_rows, cache_rows),
        out_shape=shapes,
        in_specs=[vmem] * len(operands),
        out_specs=[pl.BlockSpec(memory_space=pltpu.HBM)] if last else [vmem] * len(shapes),
        scratch_shapes=scratch,
        name="attend_last" if last else "attend_next",
        **kernel_options(queries, total_keys, kv_heads),
    )(*operands)
    return outs[0] if last else tuple(outs)


def swap_pairs(count, distance, parity):
    ring = [place_at(p, count) for p in range(count)]
    pairs = []
    for p in range(parity, count, 2):
        first, second = ring[p], ring[(p + distance) % count]
        pairs += [(first, second), (second, first)]
    return pairs


def shards(count, queries, win_keys, win_values, cache_keys, cache_values, valid_counts, first_block):
    window_rows, cache_rows = win_keys.shape[0], cache_keys.shape[0]
    stride = window_rows + cache_rows
    half = count // 2
    sizes = (window_rows, cache_rows)
    odd = functools.partial(lax.ppermute, axis_name="ctx", perm=swap_pairs(count, 1, 1))
    even = functools.partial(lax.ppermute, axis_name="ctx", perm=swap_pairs(count, 1, 0))
    across = functools.partial(lax.ppermute, axis_name="ctx", perm=swap_pairs(count, half - 1, 0))

    win_keys, win_values, cache_keys, cache_values, valid_counts, first_block, queries = [
        pltpu.with_memory_space_constraint(x, pltpu.HBM)
        for x in (win_keys, win_values, cache_keys, cache_values, valid_counts, first_block, queries)
    ]
    p = q = pack(win_keys, win_values, cache_keys, cache_values)
    opposite = None
    state, near, limits = attend_first(count, *sizes, valid_counts, first_block, queries, p)
    for step in range(1, half):
        next_p = (odd if step % 2 else even)(p)
        next_q = (even if step % 2 else odd)(q)
        if step == 2:
            opposite = across(p)
        if step > 1:
            row = 2 * (step - 2)
            pieces, arrived = [(row, 0, stride), (row + 1, 0, stride)], [p, q]
            if step == half - 1:
                pieces.append((2 * (half - 1), 0, stride))
                arrived.append(opposite)
            state = attend_next(pieces, arrived, arrived, state, False, *sizes, near, limits)
        if step < half - 1:
            p, top = lax.optimization_barrier((next_p, state[1]))
            q, top = lax.optimization_barrier((next_q, top))
            state = (state[0], top)
        else:
            p, q = next_p, next_q
    row = 2 * (half - 2)
    return attend_next([(row, 0, stride), (row + 1, 0, stride)], [p, q], [p, q], state, True, *sizes, near, limits)


def solution(mesh):
    in_specs = (
        P(("groups", "ctx"), "tp"),
        P(("groups", "ctx"), "tp"),
        P(("groups", "ctx"), "tp"),
        P(("groups", "ctx"), "tp"),
        P(("groups", "ctx"), "tp"),
        P("groups"),
        P("groups"),
    )
    out_specs = P(("groups", "ctx"), "tp")
    return jax.shard_map(
        functools.partial(shards, mesh.shape["ctx"]),
        mesh=mesh,
        in_specs=in_specs,
        out_specs=out_specs,
        check_vma=False,
    )
```

```python
import functools
import math

import jax
import jax.numpy as jnp
from jax import lax
from jax.experimental import pallas as pl
from jax.experimental.pallas import tpu as pltpu
from jax.sharding import PartitionSpec as P

HD = 128
EXP_SCALE = HD**-0.5 * math.log2(math.e)
HIDDEN = -1.0e30
CHUNK_HEADS = 2
LARGEST_TOTAL = 2.0**100


def ring_width(count):
    width = round(count ** (1 / 3))
    if width > 1 and count % width == 0 and (count // width) % 2 == 0:
        return width
    return 1


def place_at(position, count):
    width = ring_width(count)
    if width == 1:
        return position
    rows = count // width
    row, step = position // (width - 1), position % (width - 1)
    forth = row * width + 1 + step
    back = row * width + width - 1 - step
    home = (rows - 1 - (position - rows * (width - 1))) * width
    if isinstance(position, int):
        return home if position >= rows * (width - 1) else (back if row % 2 else forth)
    return jnp.where(position >= rows * (width - 1), home, jnp.where(row % 2 == 1, back, forth))


def position_of(place, count):
    width = ring_width(count)
    if width == 1:
        return place
    rows = count // width
    row, column = place // width, place % width
    snake = row * (width - 1) + jnp.where(row % 2 == 1, width - 1 - column, column - 1)
    return jnp.where(column == 0, rows * (width - 1) + rows - 1 - row, snake)


def pack_kernel(win_keys, win_values, cache_keys, cache_values, packed, sems):
    start = 0
    copies = []
    for index, piece in enumerate((win_keys, cache_keys, win_values, cache_values)):
        rows = piece.shape[0]
        copies.append(pltpu.make_async_copy(piece, packed.at[start : start + rows], sems.at[index]))
        start += rows
    for copy in copies:
        copy.start()
    for copy in copies:
        copy.wait()


def pack(win_keys, win_values, cache_keys, cache_values):
    rows = 2 * (win_keys.shape[0] + cache_keys.shape[0])
    return pl.pallas_call(
        pack_kernel,
        out_shape=jax.ShapeDtypeStruct((rows, win_keys.shape[1]), win_keys.dtype),
        in_specs=[pl.BlockSpec(memory_space=pltpu.HBM)] * 4,
        out_specs=pl.BlockSpec(memory_space=pltpu.VMEM),
        scratch_shapes=[pltpu.SemaphoreType.DMA((4,))],
        compiler_params=pltpu.CompilerParams(vmem_limit_bytes=4 * 1024 * 1024),
        cost_estimate=pl.CostEstimate(flops=0, bytes_accessed=4 * rows * win_keys.shape[1], transcendentals=0),
        name="pack",
    )(win_keys, win_values, cache_keys, cache_values)


def ring_offsets(count):
    half = count // 2
    return [sign * step for step in range(1, half) for sign in (-1, 1)] + [half]


def place_pieces(pieces, own, window_rows, cache_rows, limits, key_refs, value_refs, keys, values):
    stride = window_rows + cache_rows
    kv_heads, total_keys = keys.shape[:2]
    cache_at = len(pieces) * window_rows
    row_iota = lax.broadcasted_iota(jnp.int32, (window_rows, HD), 0)
    for index, (limit_row, key_base, value_base) in enumerate(pieces):
        key, value = key_refs[0], value_refs[0]
        if not own:
            shown = row_iota < limits[limit_row : limit_row + 1, :]
        for head in range(kv_heads):
            lanes = slice(head * HD, (head + 1) * HD)
            at = slice(index * window_rows, (index + 1) * window_rows)
            win_key = key[key_base : key_base + window_rows, lanes]
            win_value = value[value_base : value_base + window_rows, lanes]
            if own:
                keys[head, at, :] = win_key
                values[head, at, :HD] = win_value
                values[head, at, HD:] = jnp.ones((window_rows, HD), jnp.bfloat16)
            else:
                fill = key[key_base + window_rows : key_base + window_rows + 1, lanes].astype(jnp.float32)
                keys[head, at, :] = jnp.where(shown, win_key.astype(jnp.float32), fill).astype(jnp.bfloat16)
                values[head, at, :HD] = jnp.where(shown, win_value.astype(jnp.float32), 0.0).astype(jnp.bfloat16)
                values[head, at, HD:] = jnp.where(shown, 1.0, 0.0).astype(jnp.bfloat16)
            at = slice(cache_at + index * cache_rows, cache_at + (index + 1) * cache_rows)
            keys[head, at, :] = key[key_base + window_rows : key_base + stride, lanes]
            cache_value = value[value_base + window_rows : value_base + stride, lanes]
            if own:
                values[head, at, :HD] = cache_value
                values[head, at, HD:] = jnp.ones((cache_rows, HD), jnp.bfloat16)
            else:
                shown_cache = row_iota[:cache_rows] < limits[limits.shape[0] // 2 + limit_row : limits.shape[0] // 2 + limit_row + 1, :]
                values[head, at, :HD] = jnp.where(shown_cache, cache_value.astype(jnp.float32), 0.0).astype(jnp.bfloat16)
                values[head, at, HD:] = jnp.where(shown_cache, 1.0, 0.0).astype(jnp.bfloat16)
    filled = len(pieces) * stride
    if filled < total_keys:
        key_base = pieces[0][1] + window_rows
        for head in range(kv_heads):
            row = key_refs[0][key_base : key_base + 1, head * HD : (head + 1) * HD].astype(jnp.float32)
            keys[head, filled:, :] = jnp.broadcast_to(row, (total_keys - filled, HD)).astype(jnp.bfloat16)
            values[head, filled:, :] = jnp.zeros((total_keys - filled, 2 * HD), jnp.bfloat16)


def scores(query, keys):
    return lax.dot_general(query, keys, (((1,), (1,)), ((), ())), preferred_element_type=jnp.float32)


def weigh(score, top, values):
    lanes = score.shape[1] // HD
    weight = jnp.exp2(score * EXP_SCALE - jnp.concatenate([top] * lanes, axis=1)).astype(jnp.bfloat16)
    return jnp.dot(weight, values, preferred_element_type=jnp.float32)


def wide_top(score):
    return jnp.broadcast_to(jnp.max(score, axis=1, keepdims=True) * EXP_SCALE, (score.shape[0], HD))


def normalised(acc):
    total = acc[:, HD:]
    inverse = pl.reciprocal(total, approx=True)
    return (acc[:, :HD] * (inverse * (2.0 - total * inverse))).astype(jnp.bfloat16)


def chunks(q_ref, kv_heads):
    rows = q_ref.shape[0]
    group = q_ref.shape[1] // HD // kv_heads
    for head in range(kv_heads):
        for start in range(0, group, CHUNK_HEADS):
            base = head * group + start
            query = jnp.concatenate(
                [q_ref[:, (base + i) * HD : (base + i + 1) * HD] for i in range(CHUNK_HEADS)], axis=0
            )
            yield head, slice(base * rows, (base + CHUNK_HEADS) * rows), query, base


def first_kernel(
    count, window_rows, cache_rows, valid_hbm, first_hbm, q_hbm, packed, acc_out, top_out, q_ref, limits,
    keys, values, valid_ref, first_ref, sems,
):
    copies = [
        pltpu.make_async_copy(valid_hbm, valid_ref, sems.at[0]),
        pltpu.make_async_copy(first_hbm, first_ref, sems.at[1]),
        pltpu.make_async_copy(q_hbm, q_ref, sems.at[2]),
    ]
    for copy in copies:
        copy.start()
    stride = window_rows + cache_rows
    place_pieces(((0, 0, stride),), True, window_rows, cache_rows, None, (packed,), (packed,), keys, values)
    for copy in copies:
        copy.wait()

    me = lax.axis_index("ctx")
    first = first_ref[me]
    for place in range(count):
        limit = jnp.where((place >= first) & (place < me), valid_ref[place], 0)
        limits[place : place + 1, :] = jnp.full((1, HD), limit, jnp.int32)
        others = jnp.where(place == me, 0, cache_rows)
        limits[count + place : count + place + 1, :] = jnp.full((1, HD), others, jnp.int32)

    rows = q_ref.shape[0]
    key_iota = lax.broadcasted_iota(jnp.int32, (rows, window_rows), 1)
    query_iota = lax.broadcasted_iota(jnp.int32, (rows, window_rows), 0)
    seen = (key_iota <= query_iota) & (key_iota < valid_ref[me])
    bias = jnp.concatenate([jnp.where(seen, 0.0, HIDDEN)] * CHUNK_HEADS, axis=0)
    for head, at, query, _ in chunks(q_ref, keys.shape[0]):
        score = scores(query, keys[head])
        score = jnp.concatenate([score[:, :window_rows] + bias, score[:, window_rows:]], axis=1)
        top = wide_top(score)
        acc_out[at, :] = weigh(score, top, values[head])
        top_out[at, :] = top


def next_kernel(pieces, last, window_rows, cache_rows, q_ref, limits, *refs):
    key_refs = value_refs = refs[:1]
    if last:
        acc_in, top_in, out, keys, values, result, sems = refs[1:]
    else:
        acc_in, top_in, acc_out, top_out, keys, values = refs[1:]
    place_pieces(pieces, False, window_rows, cache_rows, limits, key_refs, value_refs, keys, values)
    rows = q_ref.shape[0]
    kv_heads = keys.shape[0]

    def sent(base):
        lanes = slice(base * HD, (base + CHUNK_HEADS) * HD)
        return pltpu.make_async_copy(result.at[:, lanes], out.at[:, lanes], sems.at[base // CHUNK_HEADS])

    def settle(base, acc):
        done = normalised(acc)
        for i in range(CHUNK_HEADS):
            result[:, (base + i) * HD : (base + i + 1) * HD] = done[i * rows : (i + 1) * rows]
        sent(base).start()

    fine = jnp.ones((8, HD), jnp.float32)
    for head, at, query, base in chunks(q_ref, kv_heads):
        top = top_in[at, :]
        acc = acc_in[at, :] + weigh(scores(query, keys[head]), top, values[head])
        safe = jnp.where(acc[:, HD:] < LARGEST_TOTAL, 1.0, 0.0).reshape(-1, 8, HD)
        fine = jnp.minimum(fine, jnp.min(safe, axis=0))
        if last:
            settle(base, acc)
        else:
            acc_out[at, :] = acc
            top_out[at, :] = top
    if last:
        for base in range(0, kv_heads * (q_ref.shape[1] // HD // kv_heads), CHUNK_HEADS):
            sent(base).wait()

    @pl.when(jnp.min(fine) < 0.5)
    def _():
        for head, at, query, base in chunks(q_ref, kv_heads):
            score = scores(query, keys[head])
            before = top_in[at, :]
            top = jnp.maximum(before, wide_top(score))
            fade = jnp.exp2(before - top)
            acc = acc_in[at, :] * jnp.concatenate([fade, fade], axis=1) + weigh(score, top, values[head])
            if last:
                settle(base, acc)
                sent(base).wait()
            else:
                acc_out[at, :] = acc
                top_out[at, :] = top


def kernel_options(queries, total_keys, kv_heads):
    rows, width = queries.shape
    return {
        "compiler_params": pltpu.CompilerParams(vmem_limit_bytes=40 * 1024 * 1024),
        "cost_estimate": pl.CostEstimate(
            flops=6 * rows * width * total_keys,
            bytes_accessed=2 * rows * width,
            transcendentals=rows * (width // HD) * total_keys,
        ),
    }


def room(kv_heads, total_keys):
    return [
        pltpu.VMEM((kv_heads, total_keys, HD), jnp.bfloat16),
        pltpu.VMEM((kv_heads, total_keys, 2 * HD), jnp.bfloat16),
    ]


def state_shapes(queries):
    rows = queries.shape[0] * queries.shape[1] // HD
    return [jax.ShapeDtypeStruct((rows, 2 * HD), jnp.float32), jax.ShapeDtypeStruct((rows, HD), jnp.float32)]


def attend_first(count, window_rows, cache_rows, valid_counts, first_block, queries, packed):
    kv_heads = packed.shape[1] // HD
    total_keys = -(-(window_rows + cache_rows) // HD) * HD
    vmem, anywhere = pl.BlockSpec(memory_space=pltpu.VMEM), pl.BlockSpec(memory_space=pltpu.HBM)
    acc, top, q_near, limits = pl.pallas_call(
        functools.partial(first_kernel, count, window_rows, cache_rows),
        out_shape=[
            *state_shapes(queries),
            jax.ShapeDtypeStruct(queries.shape, queries.dtype),
            jax.ShapeDtypeStruct((-(-2 * count // 8) * 8, HD), jnp.int32),
        ],
        in_specs=[anywhere, anywhere, anywhere, vmem],
        out_specs=[vmem] * 4,
        scratch_shapes=[
            *room(kv_heads, total_keys),
            pltpu.SMEM(valid_counts.shape, jnp.int32),
            pltpu.SMEM(first_block.shape, jnp.int32),
            pltpu.SemaphoreType.DMA((3,)),
        ],
        name="attend_first",
        **kernel_options(queries, total_keys, kv_heads),
    )(valid_counts, first_block, queries, packed)
    return (acc, top), q_near, limits


def attend_next(pieces, keys, values, state, last, window_rows, cache_rows, queries, limits):
    kv_heads = keys[0].shape[1] // HD
    total_keys = -(-len(pieces) * (window_rows + cache_rows) // HD) * HD
    vmem = pl.BlockSpec(memory_space=pltpu.VMEM)
    operands = [queries, limits, *keys, *state]
    shapes = [jax.ShapeDtypeStruct(queries.shape, queries.dtype)] if last else state_shapes(queries)
    scratch = room(kv_heads, total_keys)
    if last:
        chunk_count = queries.shape[1] // HD // CHUNK_HEADS
        scratch += [pltpu.VMEM(queries.shape, queries.dtype), pltpu.SemaphoreType.DMA((chunk_count,))]
    outs = pl.pallas_call(
        functools.partial(next_kernel, tuple(pieces), last, window_rows, cache_rows),
        out_shape=shapes,
        in_specs=[vmem] * len(operands),
        out_specs=[pl.BlockSpec(memory_space=pltpu.HBM)] if last else [vmem] * len(shapes),
        scratch_shapes=scratch,
        name="attend_last" if last else "attend_next",
        **kernel_options(queries, total_keys, kv_heads),
    )(*operands)
    return outs[0] if last else tuple(outs)


def shards(count, queries, win_keys, win_values, cache_keys, cache_values, valid_counts, first_block):
    window_rows, cache_rows = win_keys.shape[0], cache_keys.shape[0]
    stride = window_rows + cache_rows
    win_keys, win_values, cache_keys, cache_values, valid_counts, first_block, queries = [
        pltpu.with_memory_space_constraint(x, pltpu.HBM)
        for x in (win_keys, win_values, cache_keys, cache_values, valid_counts, first_block, queries)
    ]
    packed = pack(win_keys, win_values, cache_keys, cache_values)
    gathered = lax.all_gather(packed, "ctx", axis=0, tiled=True)
    state, near, limits = attend_first(count, window_rows, cache_rows, valid_counts, first_block, queries, packed)
    for start in range(0, count, 8):
        stop = min(start + 8, count)
        pieces = [(i, 2 * stride * i, 2 * stride * i + stride) for i in range(start, stop)]
        state = attend_next(
            pieces, [gathered], [gathered], state, stop == count, window_rows, cache_rows, near, limits
        )
    return state


def solution(mesh):
    in_specs = (
        P(("groups", "ctx"), "tp"),
        P(("groups", "ctx"), "tp"),
        P(("groups", "ctx"), "tp"),
        P(("groups", "ctx"), "tp"),
        P(("groups", "ctx"), "tp"),
        P("groups"),
        P("groups"),
    )
    out_specs = P(("groups", "ctx"), "tp")
    return jax.shard_map(
        functools.partial(shards, mesh.shape["ctx"]),
        mesh=mesh,
        in_specs=in_specs,
        out_specs=out_specs,
        check_vma=False,
    )
```

```python
import functools
import math

import jax
import jax.numpy as jnp
from jax import lax
from jax.experimental import pallas as pl
from jax.experimental.pallas import tpu as pltpu
from jax.sharding import PartitionSpec as P

HD = 128
EXP_SCALE = HD**-0.5 * math.log2(math.e)
HIDDEN = -1.0e30
CHUNK_HEADS = 4
LARGEST_TOTAL = 2.0**100


def ring_width(count):
    width = round(count ** (1 / 3))
    if width > 1 and count % width == 0 and (count // width) % 2 == 0:
        return width
    return 1


def place_at(position, count):
    width = ring_width(count)
    if width == 1:
        return position
    rows = count // width
    row, step = position // (width - 1), position % (width - 1)
    forth = row * width + 1 + step
    back = row * width + width - 1 - step
    home = (rows - 1 - (position - rows * (width - 1))) * width
    if isinstance(position, int):
        return home if position >= rows * (width - 1) else (back if row % 2 else forth)
    return jnp.where(position >= rows * (width - 1), home, jnp.where(row % 2 == 1, back, forth))


def position_of(place, count):
    width = ring_width(count)
    if width == 1:
        return place
    rows = count // width
    row, column = place // width, place % width
    snake = row * (width - 1) + jnp.where(row % 2 == 1, width - 1 - column, column - 1)
    return jnp.where(column == 0, rows * (width - 1) + rows - 1 - row, snake)


def pack_kernel(win_keys, win_values, cache_keys, cache_values, packed, sems):
    start = 0
    copies = []
    for index, piece in enumerate((win_keys, cache_keys, win_values, cache_values)):
        rows = piece.shape[0]
        copies.append(pltpu.make_async_copy(piece, packed.at[start : start + rows], sems.at[index]))
        start += rows
    for copy in copies:
        copy.start()
    for copy in copies:
        copy.wait()


def pack(win_keys, win_values, cache_keys, cache_values):
    rows = 2 * (win_keys.shape[0] + cache_keys.shape[0])
    return pl.pallas_call(
        pack_kernel,
        out_shape=jax.ShapeDtypeStruct((rows, win_keys.shape[1]), win_keys.dtype),
        in_specs=[pl.BlockSpec(memory_space=pltpu.HBM)] * 4,
        out_specs=pl.BlockSpec(memory_space=pltpu.VMEM),
        scratch_shapes=[pltpu.SemaphoreType.DMA((4,))],
        compiler_params=pltpu.CompilerParams(vmem_limit_bytes=4 * 1024 * 1024),
        cost_estimate=pl.CostEstimate(flops=0, bytes_accessed=4 * rows * win_keys.shape[1], transcendentals=0),
        name="pack",
    )(win_keys, win_values, cache_keys, cache_values)


def ring_offsets(count):
    half = count // 2
    offsets = []
    for step in range(1, half):
        side = 1 if step % 2 else -1
        offsets += [side * step, -side * step]
    return offsets + [half]


def place_piece(index, number, limit_row, own, sizes, limits, key, key_base, value, value_base, keys, values):
    window_rows, cache_rows = sizes
    stride = window_rows + cache_rows
    cache_at = number * window_rows + index * cache_rows
    if not own:
        row_iota = lax.broadcasted_iota(jnp.int32, (window_rows, HD), 0)
        shown = row_iota < limits[limit_row : limit_row + 1, :]
    for head in range(keys.shape[0]):
        lanes = slice(head * HD, (head + 1) * HD)
        at = slice(index * window_rows, (index + 1) * window_rows)
        win_key = key[key_base : key_base + window_rows, lanes]
        win_value = value[value_base : value_base + window_rows, lanes]
        if own:
            keys[head, at, :] = win_key
            values[head, at, :HD] = win_value
            values[head, at, HD:] = jnp.ones((window_rows, HD), jnp.bfloat16)
        else:
            fill = key[key_base + window_rows : key_base + window_rows + 1, lanes].astype(jnp.float32)
            keys[head, at, :] = jnp.where(shown, win_key.astype(jnp.float32), fill).astype(jnp.bfloat16)
            values[head, at, :HD] = jnp.where(shown, win_value.astype(jnp.float32), 0.0).astype(jnp.bfloat16)
            values[head, at, HD:] = jnp.where(shown, 1.0, 0.0).astype(jnp.bfloat16)
        at = slice(cache_at, cache_at + cache_rows)
        keys[head, at, :] = key[key_base + window_rows : key_base + stride, lanes]
        values[head, at, :HD] = value[value_base + window_rows : value_base + stride, lanes]
        values[head, at, HD:] = jnp.ones((cache_rows, HD), jnp.bfloat16)


def fill_up(filled, keys, values):
    spare = keys.shape[1] - filled
    if spare:
        for head in range(keys.shape[0]):
            row = keys[head, filled - 1 : filled, :].astype(jnp.float32)
            keys[head, filled:, :] = jnp.broadcast_to(row, (spare, HD)).astype(jnp.bfloat16)
            values[head, filled:, :] = jnp.zeros((spare, 2 * HD), jnp.bfloat16)


def scores(query, keys):
    return lax.dot_general(query, keys, (((1,), (1,)), ((), ())), preferred_element_type=jnp.float32)


def weigh(score, top, values):
    lanes = score.shape[1] // HD
    weight = jnp.exp2(score * EXP_SCALE - jnp.concatenate([top] * lanes, axis=1)).astype(jnp.bfloat16)
    return jnp.dot(weight, values, preferred_element_type=jnp.float32)


def wide_top(score):
    return jnp.broadcast_to(jnp.max(score, axis=1, keepdims=True) * EXP_SCALE, (score.shape[0], HD))


def normalised(acc):
    total = acc[:, HD:]
    inverse = pl.reciprocal(total, approx=True)
    return (acc[:, :HD] * (inverse * (2.0 - total * inverse))).astype(jnp.bfloat16)


def chunks(q_ref, kv_heads):
    rows = q_ref.shape[0]
    group = q_ref.shape[1] // HD // kv_heads
    for head in range(kv_heads):
        for start in range(0, group, CHUNK_HEADS):
            base = head * group + start
            query = jnp.concatenate(
                [q_ref[:, (base + i) * HD : (base + i + 1) * HD] for i in range(CHUNK_HEADS)], axis=0
            )
            yield head, slice(base * rows, (base + CHUNK_HEADS) * rows), query, base


def first_kernel(
    count, window_rows, cache_rows, valid_hbm, first_hbm, q_hbm, packed, acc_out, top_out, q_ref, limits,
    keys, values, valid_ref, first_ref, sems,
):
    copies = [
        pltpu.make_async_copy(valid_hbm, valid_ref, sems.at[0]),
        pltpu.make_async_copy(first_hbm, first_ref, sems.at[1]),
        pltpu.make_async_copy(q_hbm, q_ref, sems.at[2]),
    ]
    for copy in copies:
        copy.start()
    stride = window_rows + cache_rows
    place_piece(0, 1, 0, True, (window_rows, cache_rows), None, packed, 0, packed, stride, keys, values)
    fill_up(stride, keys, values)
    for copy in copies:
        copy.wait()

    me = lax.axis_index("ctx")
    position = position_of(me, count)
    first = first_ref[me]
    sign = 2 * lax.rem(position, 2) - 1
    for row, offset in enumerate(ring_offsets(count)):
        place = place_at(lax.rem(position + sign * offset + count, count), count)
        limit = jnp.where((place >= first) & (place <= me), valid_ref[place], 0)
        limits[row : row + 1, :] = jnp.full((1, HD), limit, jnp.int32)

    rows = q_ref.shape[0]
    key_iota = lax.broadcasted_iota(jnp.int32, (rows, window_rows), 1)
    query_iota = lax.broadcasted_iota(jnp.int32, (rows, window_rows), 0)
    seen = (key_iota <= query_iota) & (key_iota < valid_ref[me])
    bias = jnp.concatenate([jnp.where(seen, 0.0, HIDDEN)] * CHUNK_HEADS, axis=0)
    for head, at, query, _ in chunks(q_ref, keys.shape[0]):
        score = scores(query, keys[head])
        score = jnp.concatenate([score[:, :window_rows] + bias, score[:, window_rows:]], axis=1)
        top = wide_top(score)
        acc_out[at, :] = weigh(score, top, values[head])
        top_out[at, :] = top


def next_kernel(rows_of, split, last, count, sizes, q_ref, limits, *refs):
    number = len(rows_of)
    whole = number - split
    blocks, halves = refs[:whole], refs[whole : whole + 2 * split]
    refs = refs[whole + 2 * split :]
    if last:
        acc_in, top_in, out, keys, values, result, sems = refs
    else:
        acc_in, top_in, acc_out, top_out, keys, values = refs
    stride = sum(sizes)
    for index, block in enumerate(blocks):
        place_piece(index, number, rows_of[index], False, sizes, limits, block, 0, block, stride, keys, values)
    if split:
        place = functools.partial(place_piece, whole, number, rows_of[whole], False, sizes, limits)
        if halves[0].shape[0] == stride:
            place(halves[0], 0, halves[1], 0, keys, values)
        else:
            me = lax.axis_index("ctx")
            corner = (me < 2) | (me >= count - 2)

            @pl.when(corner)
            def _():
                place(halves[0], 0, halves[0], stride, keys, values)

            @pl.when(jnp.logical_not(corner))
            def _():
                place(halves[1], 0, halves[1], stride, keys, values)

    fill_up(number * stride, keys, values)
    rows = q_ref.shape[0]
    kv_heads = keys.shape[0]

    def sent(base):
        lanes = slice(base * HD, (base + CHUNK_HEADS) * HD)
        return pltpu.make_async_copy(result.at[:, lanes], out.at[:, lanes], sems.at[base // CHUNK_HEADS])

    def settle(base, acc):
        done = normalised(acc)
        for i in range(CHUNK_HEADS):
            result[:, (base + i) * HD : (base + i + 1) * HD] = done[i * rows : (i + 1) * rows]
        sent(base).start()

    fine = jnp.ones((8, HD), jnp.float32)
    for head, at, query, base in chunks(q_ref, kv_heads):
        top = top_in[at, :]
        acc = acc_in[at, :] + weigh(scores(query, keys[head]), top, values[head])
        safe = jnp.where(acc[:, HD:] < LARGEST_TOTAL, 1.0, 0.0).reshape(-1, 8, HD)
        fine = jnp.minimum(fine, jnp.min(safe, axis=0))
        if last:
            settle(base, acc)
        else:
            acc_out[at, :] = acc
            top_out[at, :] = top
    if last:
        for base in range(0, kv_heads * (q_ref.shape[1] // HD // kv_heads), CHUNK_HEADS):
            sent(base).wait()

    @pl.when(jnp.min(fine) < 0.5)
    def _():
        for head, at, query, base in chunks(q_ref, kv_heads):
            score = scores(query, keys[head])
            before = top_in[at, :]
            top = jnp.maximum(before, wide_top(score))
            fade = jnp.exp2(before - top)
            acc = acc_in[at, :] * jnp.concatenate([fade, fade], axis=1) + weigh(score, top, values[head])
            if last:
                settle(base, acc)
                sent(base).wait()
            else:
                acc_out[at, :] = acc
                top_out[at, :] = top


def kernel_options(queries, total_keys, kv_heads):
    rows, width = queries.shape
    return {
        "compiler_params": pltpu.CompilerParams(vmem_limit_bytes=40 * 1024 * 1024),
        "cost_estimate": pl.CostEstimate(
            flops=6 * rows * width * total_keys,
            bytes_accessed=2 * rows * width,
            transcendentals=rows * (width // HD) * total_keys,
        ),
    }


def room(kv_heads, total_keys):
    return [
        pltpu.VMEM((kv_heads, total_keys, HD), jnp.bfloat16),
        pltpu.VMEM((kv_heads, total_keys, 2 * HD), jnp.bfloat16),
    ]


def state_shapes(queries):
    rows = queries.shape[0] * queries.shape[1] // HD
    return [jax.ShapeDtypeStruct((rows, 2 * HD), jnp.float32), jax.ShapeDtypeStruct((rows, HD), jnp.float32)]


def attend_first(count, window_rows, cache_rows, valid_counts, first_block, queries, packed):
    kv_heads = packed.shape[1] // HD
    total_keys = -(-(window_rows + cache_rows) // HD) * HD
    vmem, anywhere = pl.BlockSpec(memory_space=pltpu.VMEM), pl.BlockSpec(memory_space=pltpu.HBM)
    acc, top, q_near, limits = pl.pallas_call(
        functools.partial(first_kernel, count, window_rows, cache_rows),
        out_shape=[
            *state_shapes(queries),
            jax.ShapeDtypeStruct(queries.shape, queries.dtype),
            jax.ShapeDtypeStruct((-(-count // 8) * 8, HD), jnp.int32),
        ],
        in_specs=[anywhere, anywhere, anywhere, vmem],
        out_specs=[vmem] * 4,
        scratch_shapes=[
            *room(kv_heads, total_keys),
            pltpu.SMEM(valid_counts.shape, jnp.int32),
            pltpu.SMEM(first_block.shape, jnp.int32),
            pltpu.SemaphoreType.DMA((3,)),
        ],
        name="attend_first",
        **kernel_options(queries, total_keys, kv_heads),
    )(valid_counts, first_block, queries, packed)
    return (acc, top), q_near, limits


def attend_next(rows_of, blocks, halves, state, last, count, window_rows, cache_rows, queries, limits):
    kv_heads = blocks[0].shape[1] // HD
    total_keys = -(-len(rows_of) * (window_rows + cache_rows) // HD) * HD
    vmem = pl.BlockSpec(memory_space=pltpu.VMEM)
    operands = [queries, limits, *blocks, *halves, *state]
    shapes = [jax.ShapeDtypeStruct(queries.shape, queries.dtype)] if last else state_shapes(queries)
    scratch = room(kv_heads, total_keys)
    if last:
        chunk_count = queries.shape[1] // HD // CHUNK_HEADS
        scratch += [pltpu.VMEM(queries.shape, queries.dtype), pltpu.SemaphoreType.DMA((chunk_count,))]
    outs = pl.pallas_call(
        functools.partial(next_kernel, tuple(rows_of), bool(halves), last, count, (window_rows, cache_rows)),
        out_shape=shapes,
        in_specs=[vmem] * len(operands),
        out_specs=[pl.BlockSpec(memory_space=pltpu.HBM)] if last else [vmem] * len(shapes),
        scratch_shapes=scratch,
        name="attend_last" if last else "attend_next",
        **kernel_options(queries, total_keys, kv_heads),
    )(*operands)
    return outs[0] if last else tuple(outs)


def swap_pairs(count, parity):
    pairs = []
    for p in range(parity, count, 2):
        first, second = place_at(p, count), place_at((p + 1) % count, count)
        pairs += [(first, second), (second, first)]
    return pairs


def shards(count, queries, win_keys, win_values, cache_keys, cache_values, valid_counts, first_block):
    window_rows, cache_rows = win_keys.shape[0], cache_keys.shape[0]
    stride = window_rows + cache_rows
    half = count // 2
    sizes = (window_rows, cache_rows)
    send = functools.partial(lax.ppermute, axis_name="ctx")
    odd, even = swap_pairs(count, 1), swap_pairs(count, 0)
    short = ring_width(count) == 2 and count == 8
    corners = [(0, 7), (7, 0), (1, 6), (6, 1)]
    rungs = [(2, 3), (3, 2), (4, 5), (5, 4)]

    win_keys, win_values, cache_keys, cache_values, valid_counts, first_block, queries = [
        pltpu.with_memory_space_constraint(x, pltpu.HBM)
        for x in (win_keys, win_values, cache_keys, cache_values, valid_counts, first_block, queries)
    ]
    p = q = own = pack(win_keys, win_values, cache_keys, cache_values)
    state, near, limits = attend_first(count, *sizes, valid_counts, first_block, queries, own)
    common = (count, *sizes, near, limits)
    opposite = []
    for step in range(1, half):
        next_p = send(p, perm=odd if step % 2 else even)
        next_q = send(q, perm=even if step % 2 else odd)
        row = 2 * (step - 2)
        rows_of = [row, row + 1]
        if short and step == 3:
            state = attend_next([*rows_of, 2 * (half - 1)], [p, q], opposite, state, False, *common)
        elif step > 1:
            state = attend_next(rows_of, [p, q], [], state, False, *common)
        acc, top = state
        if short and step == 1:
            own, top = lax.optimization_barrier((own, top))
            opposite = [send(own, perm=corners)]
        elif short and step == 2:
            p, top = lax.optimization_barrier((p, top))
            opposite.append(send(p, perm=rungs))
        if step < half - 1:
            if short and step == 2:
                opposite[0], next_p = lax.optimization_barrier((opposite[0], next_p))
            p, top = lax.optimization_barrier((next_p, top))
            q, top = lax.optimization_barrier((next_q, top))
        else:
            p, q = next_p, next_q
        state = (acc, top)
    row = 2 * (half - 2)
    if short:
        state = attend_next([row], [p], [], state, False, *common)
        return attend_next([row + 1], [q], [], state, True, *common)
    key_half = send(p[:stride], perm=even if half % 2 == 0 else odd)
    value_half = send(q[stride:], perm=odd if half % 2 == 0 else even)
    return attend_next([row, row + 1, row + 2], [p, q], [key_half, value_half], state, True, *common)


def solution(mesh):
    in_specs = (
        P(("groups", "ctx"), "tp"),
        P(("groups", "ctx"), "tp"),
        P(("groups", "ctx"), "tp"),
        P(("groups", "ctx"), "tp"),
        P(("groups", "ctx"), "tp"),
        P("groups"),
        P("groups"),
    )
    out_specs = P(("groups", "ctx"), "tp")
    return jax.shard_map(
        functools.partial(shards, mesh.shape["ctx"]),
        mesh=mesh,
        in_specs=in_specs,
        out_specs=out_specs,
        check_vma=False,
    )
```

```python
import functools
import math

import jax
import jax.numpy as jnp
from jax import lax
from jax.experimental import pallas as pl
from jax.experimental.pallas import tpu as pltpu
from jax.sharding import PartitionSpec as P

HD = 128
EXP_SCALE = HD**-0.5 * math.log2(math.e)
HIDDEN = -1.0e30
CHUNK_HEADS = 4
LARGEST_TOTAL = 2.0**100


def ring_width(count):
    width = round(count ** (1 / 3))
    if width > 1 and count % width == 0 and (count // width) % 2 == 0:
        return width
    return 1


def place_at(position, count):
    width = ring_width(count)
    if width == 1:
        return position
    rows = count // width
    row, step = position // (width - 1), position % (width - 1)
    forth = row * width + 1 + step
    back = row * width + width - 1 - step
    home = (rows - 1 - (position - rows * (width - 1))) * width
    if isinstance(position, int):
        return home if position >= rows * (width - 1) else (back if row % 2 else forth)
    return jnp.where(position >= rows * (width - 1), home, jnp.where(row % 2 == 1, back, forth))


def position_of(place, count):
    width = ring_width(count)
    if width == 1:
        return place
    rows = count // width
    row, column = place // width, place % width
    snake = row * (width - 1) + jnp.where(row % 2 == 1, width - 1 - column, column - 1)
    return jnp.where(column == 0, rows * (width - 1) + rows - 1 - row, snake)


def pack_kernel(win_keys, win_values, cache_keys, cache_values, keys, values, sems):
    window_rows = win_keys.shape[0]
    copies = [
        pltpu.make_async_copy(win_keys, keys.at[:window_rows], sems.at[0]),
        pltpu.make_async_copy(cache_keys, keys.at[window_rows:], sems.at[1]),
        pltpu.make_async_copy(win_values, values.at[:window_rows], sems.at[2]),
        pltpu.make_async_copy(cache_values, values.at[window_rows:], sems.at[3]),
    ]
    for copy in copies:
        copy.start()
    for copy in copies:
        copy.wait()


def pack(win_keys, win_values, cache_keys, cache_values):
    rows, width = win_keys.shape[0] + cache_keys.shape[0], win_keys.shape[1]
    return pl.pallas_call(
        pack_kernel,
        out_shape=[jax.ShapeDtypeStruct((rows, width), win_keys.dtype)] * 2,
        in_specs=[pl.BlockSpec(memory_space=pltpu.HBM)] * 4,
        out_specs=[pl.BlockSpec(memory_space=pltpu.VMEM)] * 2,
        scratch_shapes=[pltpu.SemaphoreType.DMA((4,))],
        compiler_params=pltpu.CompilerParams(vmem_limit_bytes=4 * 1024 * 1024),
        cost_estimate=pl.CostEstimate(flops=0, bytes_accessed=8 * rows * width, transcendentals=0),
        name="pack",
    )(win_keys, win_values, cache_keys, cache_values)


def ring_offsets(count):
    half = count // 2
    return [sign * step for step in range(1, half) for sign in (-1, 1)] + [half]


def place_piece(index, number, limit_row, own, sizes, limits, key, value, keys, values):
    window_rows, cache_rows = sizes
    cache_at = number * window_rows + index * cache_rows
    if not own:
        row_iota = lax.broadcasted_iota(jnp.int32, (window_rows, HD), 0)
        shown = row_iota < limits[limit_row : limit_row + 1, :]
    for head in range(keys.shape[0]):
        lanes = slice(head * HD, (head + 1) * HD)
        at = slice(index * window_rows, (index + 1) * window_rows)
        win_key, win_value = key[:window_rows, lanes], value[:window_rows, lanes]
        if own:
            keys[head, at, :] = win_key
            values[head, at, :HD] = win_value
            values[head, at, HD:] = jnp.ones((window_rows, HD), jnp.bfloat16)
        else:
            fill = key[window_rows : window_rows + 1, lanes].astype(jnp.float32)
            keys[head, at, :] = jnp.where(shown, win_key.astype(jnp.float32), fill).astype(jnp.bfloat16)
            values[head, at, :HD] = jnp.where(shown, win_value.astype(jnp.float32), 0.0).astype(jnp.bfloat16)
            values[head, at, HD:] = jnp.where(shown, 1.0, 0.0).astype(jnp.bfloat16)
        at = slice(cache_at, cache_at + cache_rows)
        keys[head, at, :] = key[window_rows:, lanes]
        values[head, at, :HD] = value[window_rows:, lanes]
        values[head, at, HD:] = jnp.ones((cache_rows, HD), jnp.bfloat16)


def fill_up(filled, keys, values):
    spare = keys.shape[1] - filled
    if spare:
        for head in range(keys.shape[0]):
            row = keys[head, filled - 1 : filled, :].astype(jnp.float32)
            keys[head, filled:, :] = jnp.broadcast_to(row, (spare, HD)).astype(jnp.bfloat16)
            values[head, filled:, :] = jnp.zeros((spare, 2 * HD), jnp.bfloat16)


def scores(query, keys):
    return lax.dot_general(query, keys, (((1,), (1,)), ((), ())), preferred_element_type=jnp.float32)


def weigh(score, top, values):
    lanes = score.shape[1] // HD
    weight = jnp.exp2(score * EXP_SCALE - jnp.concatenate([top] * lanes, axis=1)).astype(jnp.bfloat16)
    return jnp.dot(weight, values, preferred_element_type=jnp.float32)


def wide_top(score):
    return jnp.broadcast_to(jnp.max(score, axis=1, keepdims=True) * EXP_SCALE, (score.shape[0], HD))


def normalised(acc):
    total = acc[:, HD:]
    inverse = pl.reciprocal(total, approx=True)
    return (acc[:, :HD] * (inverse * (2.0 - total * inverse))).astype(jnp.bfloat16)


def chunks(q_ref, kv_heads):
    rows = q_ref.shape[0]
    group = q_ref.shape[1] // HD // kv_heads
    for head in range(kv_heads):
        for start in range(0, group, CHUNK_HEADS):
            base = head * group + start
            query = jnp.concatenate(
                [q_ref[:, (base + i) * HD : (base + i + 1) * HD] for i in range(CHUNK_HEADS)], axis=0
            )
            yield head, slice(base * rows, (base + CHUNK_HEADS) * rows), query, base


def first_kernel(
    count, window_rows, cache_rows, valid_hbm, first_hbm, q_hbm, own_keys, own_values, acc_out, top_out, q_ref, limits,
    keys, values, valid_ref, first_ref, sems,
):
    copies = [
        pltpu.make_async_copy(valid_hbm, valid_ref, sems.at[0]),
        pltpu.make_async_copy(first_hbm, first_ref, sems.at[1]),
        pltpu.make_async_copy(q_hbm, q_ref, sems.at[2]),
    ]
    for copy in copies:
        copy.start()
    place_piece(0, 1, 0, True, (window_rows, cache_rows), None, own_keys, own_values, keys, values)
    fill_up(window_rows + cache_rows, keys, values)
    for copy in copies:
        copy.wait()

    me = lax.axis_index("ctx")
    position = position_of(me, count)
    first = first_ref[me]
    for row, offset in enumerate(ring_offsets(count)):
        place = place_at(lax.rem(position + offset + count, count), count)
        limit = jnp.where((place >= first) & (place <= me), valid_ref[place], 0)
        limits[row : row + 1, :] = jnp.full((1, HD), limit, jnp.int32)

    rows = q_ref.shape[0]
    key_iota = lax.broadcasted_iota(jnp.int32, (rows, window_rows), 1)
    query_iota = lax.broadcasted_iota(jnp.int32, (rows, window_rows), 0)
    seen = (key_iota <= query_iota) & (key_iota < valid_ref[me])
    bias = jnp.concatenate([jnp.where(seen, 0.0, HIDDEN)] * CHUNK_HEADS, axis=0)
    for head, at, query, _ in chunks(q_ref, keys.shape[0]):
        score = scores(query, keys[head])
        score = jnp.concatenate([score[:, :window_rows] + bias, score[:, window_rows:]], axis=1)
        top = wide_top(score)
        acc_out[at, :] = weigh(score, top, values[head])
        top_out[at, :] = top


def next_kernel(rows_of, last, sizes, q_ref, limits, *refs):
    number = len(rows_of)
    key_refs, value_refs = refs[:number], refs[number : 2 * number]
    if last:
        acc_in, top_in, out, keys, values, result, sems = refs[2 * number :]
    else:
        acc_in, top_in, acc_out, top_out, keys, values = refs[2 * number :]
    for index, row in enumerate(rows_of):
        place_piece(index, number, row, False, sizes, limits, key_refs[index], value_refs[index], keys, values)
    fill_up(number * sum(sizes), keys, values)
    rows = q_ref.shape[0]
    kv_heads = keys.shape[0]

    def sent(base):
        lanes = slice(base * HD, (base + CHUNK_HEADS) * HD)
        return pltpu.make_async_copy(result.at[:, lanes], out.at[:, lanes], sems.at[base // CHUNK_HEADS])

    def settle(base, acc):
        done = normalised(acc)
        for i in range(CHUNK_HEADS):
            result[:, (base + i) * HD : (base + i + 1) * HD] = done[i * rows : (i + 1) * rows]
        sent(base).start()

    fine = jnp.ones((8, HD), jnp.float32)
    for head, at, query, base in chunks(q_ref, kv_heads):
        top = top_in[at, :]
        acc = acc_in[at, :] + weigh(scores(query, keys[head]), top, values[head])
        safe = jnp.where(acc[:, HD:] < LARGEST_TOTAL, 1.0, 0.0).reshape(-1, 8, HD)
        fine = jnp.minimum(fine, jnp.min(safe, axis=0))
        if last:
            settle(base, acc)
        else:
            acc_out[at, :] = acc
            top_out[at, :] = top
    if last:
        for base in range(0, kv_heads * (q_ref.shape[1] // HD // kv_heads), CHUNK_HEADS):
            sent(base).wait()

    @pl.when(jnp.min(fine) < 0.5)
    def _():
        for head, at, query, base in chunks(q_ref, kv_heads):
            score = scores(query, keys[head])
            before = top_in[at, :]
            top = jnp.maximum(before, wide_top(score))
            fade = jnp.exp2(before - top)
            acc = acc_in[at, :] * jnp.concatenate([fade, fade], axis=1) + weigh(score, top, values[head])
            if last:
                settle(base, acc)
                sent(base).wait()
            else:
                acc_out[at, :] = acc
                top_out[at, :] = top


def kernel_options(queries, total_keys, kv_heads):
    rows, width = queries.shape
    return {
        "compiler_params": pltpu.CompilerParams(vmem_limit_bytes=40 * 1024 * 1024),
        "cost_estimate": pl.CostEstimate(
            flops=6 * rows * width * total_keys,
            bytes_accessed=2 * rows * width,
            transcendentals=rows * (width // HD) * total_keys,
        ),
    }


def room(kv_heads, total_keys):
    return [
        pltpu.VMEM((kv_heads, total_keys, HD), jnp.bfloat16),
        pltpu.VMEM((kv_heads, total_keys, 2 * HD), jnp.bfloat16),
    ]


def state_shapes(queries):
    rows = queries.shape[0] * queries.shape[1] // HD
    return [jax.ShapeDtypeStruct((rows, 2 * HD), jnp.float32), jax.ShapeDtypeStruct((rows, HD), jnp.float32)]


def attend_first(count, window_rows, cache_rows, valid_counts, first_block, queries, own_keys, own_values):
    kv_heads = own_keys.shape[1] // HD
    total_keys = -(-(window_rows + cache_rows) // HD) * HD
    vmem, anywhere = pl.BlockSpec(memory_space=pltpu.VMEM), pl.BlockSpec(memory_space=pltpu.HBM)
    acc, top, q_near, limits = pl.pallas_call(
        functools.partial(first_kernel, count, window_rows, cache_rows),
        out_shape=[
            *state_shapes(queries),
            jax.ShapeDtypeStruct(queries.shape, queries.dtype),
            jax.ShapeDtypeStruct((-(-count // 8) * 8, HD), jnp.int32),
        ],
        in_specs=[anywhere, anywhere, anywhere, vmem, vmem],
        out_specs=[vmem] * 4,
        scratch_shapes=[
            *room(kv_heads, total_keys),
            pltpu.SMEM(valid_counts.shape, jnp.int32),
            pltpu.SMEM(first_block.shape, jnp.int32),
            pltpu.SemaphoreType.DMA((3,)),
        ],
        name="attend_first",
        **kernel_options(queries, total_keys, kv_heads),
    )(valid_counts, first_block, queries, own_keys, own_values)
    return (acc, top), q_near, limits


def attend_next(pieces, state, last, sizes, queries, limits):
    rows_of, key_blocks, value_blocks = zip(*pieces)
    kv_heads = key_blocks[0].shape[1] // HD
    total_keys = -(-len(pieces) * sum(sizes) // HD) * HD
    vmem = pl.BlockSpec(memory_space=pltpu.VMEM)
    operands = [queries, limits, *key_blocks, *value_blocks, *state]
    shapes = [jax.ShapeDtypeStruct(queries.shape, queries.dtype)] if last else state_shapes(queries)
    scratch = room(kv_heads, total_keys)
    if last:
        chunk_count = queries.shape[1] // HD // CHUNK_HEADS
        scratch += [pltpu.VMEM(queries.shape, queries.dtype), pltpu.SemaphoreType.DMA((chunk_count,))]
    outs = pl.pallas_call(
        functools.partial(next_kernel, rows_of, last, sizes),
        out_shape=shapes,
        in_specs=[vmem] * len(operands),
        out_specs=[pl.BlockSpec(memory_space=pltpu.HBM)] if last else [vmem] * len(shapes),
        scratch_shapes=scratch,
        name="attend_last" if last else "attend_next",
        **kernel_options(queries, total_keys, kv_heads),
    )(*operands)
    return outs[0] if last else tuple(outs)


def shards(count, queries, win_keys, win_values, cache_keys, cache_values, valid_counts, first_block):
    sizes = (win_keys.shape[0], cache_keys.shape[0])
    half = count // 2
    ring = [place_at(p, count) for p in range(count)]
    onward = [(ring[p], ring[(p + 1) % count]) for p in range(count)]
    backward = [(b, a) for a, b in onward]

    win_keys, win_values, cache_keys, cache_values, valid_counts, first_block, queries = [
        pltpu.with_memory_space_constraint(x, pltpu.HBM)
        for x in (win_keys, win_values, cache_keys, cache_values, valid_counts, first_block, queries)
    ]
    own_keys, own_values = pack(win_keys, win_values, cache_keys, cache_values)
    key_on = key_back = own_keys
    value_on = value_back = own_values
    state, near, limits = attend_first(count, *sizes, valid_counts, first_block, queries, own_keys, own_values)
    arrived = []
    for step in range(1, half + 1):
        key_on = lax.ppermute(key_on, "ctx", onward)
        value_back = lax.ppermute(value_back, "ctx", backward)
        if step < half:
            value_on = lax.ppermute(value_on, "ctx", onward)
            key_back = lax.ppermute(key_back, "ctx", backward)
            row = 2 * (step - 1)
            arrived.append([(row, key_on, value_on), (row + 1, key_back, value_back)])
        else:
            arrived.append([(2 * (half - 1), key_on, value_back)])
        if step == 1:
            key_on, top = lax.optimization_barrier((key_on, state[1]))
            state = (state[0], top)
    for begin in range(0, half - 2, 2):
        pieces = [piece for step in arrived[begin : min(begin + 2, half - 2)] for piece in step]
        state = attend_next(pieces, state, False, sizes, near, limits)
    state = attend_next(arrived[half - 2], state, False, sizes, near, limits)
    return attend_next(arrived[half - 1], state, True, sizes, near, limits)


def solution(mesh):
    in_specs = (
        P(("groups", "ctx"), "tp"),
        P(("groups", "ctx"), "tp"),
        P(("groups", "ctx"), "tp"),
        P(("groups", "ctx"), "tp"),
        P(("groups", "ctx"), "tp"),
        P("groups"),
        P("groups"),
    )
    out_specs = P(("groups", "ctx"), "tp")
    return jax.shard_map(
        functools.partial(shards, mesh.shape["ctx"]),
        mesh=mesh,
        in_specs=in_specs,
        out_specs=out_specs,
        check_vma=False,
    )
```

```python
import functools
import math

import jax
import jax.numpy as jnp
from jax import lax
from jax.experimental import pallas as pl
from jax.experimental.pallas import tpu as pltpu
from jax.sharding import PartitionSpec as P

HD = 128
EXP_SCALE = HD**-0.5 * math.log2(math.e)
HIDDEN = -1.0e30
CHUNK_HEADS = 4
LARGEST_TOTAL = 2.0**100


def ring_width(count):
    width = round(count ** (1 / 3))
    if width > 1 and count % width == 0 and (count // width) % 2 == 0:
        return width
    return 1


def place_at(position, count):
    width = ring_width(count)
    if width == 1:
        return position
    rows = count // width
    row, step = position // (width - 1), position % (width - 1)
    forth = row * width + 1 + step
    back = row * width + width - 1 - step
    home = (rows - 1 - (position - rows * (width - 1))) * width
    if isinstance(position, int):
        return home if position >= rows * (width - 1) else (back if row % 2 else forth)
    return jnp.where(position >= rows * (width - 1), home, jnp.where(row % 2 == 1, back, forth))


def position_of(place, count):
    width = ring_width(count)
    if width == 1:
        return place
    rows = count // width
    row, column = place // width, place % width
    snake = row * (width - 1) + jnp.where(row % 2 == 1, width - 1 - column, column - 1)
    return jnp.where(column == 0, rows * (width - 1) + rows - 1 - row, snake)


def load_kernel(count, win_keys, win_values, cache_keys, cache_values, q_hbm, valid_hbm, first_hbm, *refs):
    keys, values, q_ref, limits, valid_ref, first_ref, sems = refs
    window_rows = win_keys.shape[0]
    pairs = [
        (valid_hbm, valid_ref),
        (first_hbm, first_ref),
        (win_keys, keys.at[:window_rows]),
        (cache_keys, keys.at[window_rows:]),
        (win_values, values.at[:window_rows]),
        (cache_values, values.at[window_rows:]),
        (q_hbm, q_ref),
    ]
    copies = [pltpu.make_async_copy(*pair, sems.at[index]) for index, pair in enumerate(pairs)]
    for copy in copies:
        copy.start()
    for copy in copies[:2]:
        copy.wait()
    me = lax.axis_index("ctx")
    position = position_of(me, count)
    first = first_ref[me]
    for row, offset in enumerate(ring_offsets(count)):
        place = place_at(lax.rem(position + offset + count, count), count)
        limit = jnp.where((place >= first) & (place <= me), valid_ref[place], 0)
        limits[row : row + 1, :] = jnp.full((1, HD), limit, jnp.int32)
    limits[count - 1 : count, :] = jnp.full((1, HD), valid_ref[me], jnp.int32)
    for copy in copies[2:]:
        copy.wait()


def load(count, win_keys, win_values, cache_keys, cache_values, queries, valid_counts, first_block):
    rows, width = win_keys.shape[0] + cache_keys.shape[0], win_keys.shape[1]
    return pl.pallas_call(
        functools.partial(load_kernel, count),
        out_shape=[
            jax.ShapeDtypeStruct((rows, width), win_keys.dtype),
            jax.ShapeDtypeStruct((rows, width), win_keys.dtype),
            jax.ShapeDtypeStruct(queries.shape, queries.dtype),
            jax.ShapeDtypeStruct((-(-count // 8) * 8, HD), jnp.int32),
        ],
        in_specs=[pl.BlockSpec(memory_space=pltpu.HBM)] * 7,
        out_specs=[pl.BlockSpec(memory_space=pltpu.VMEM)] * 4,
        scratch_shapes=[
            pltpu.SMEM(valid_counts.shape, jnp.int32),
            pltpu.SMEM(first_block.shape, jnp.int32),
            pltpu.SemaphoreType.DMA((7,)),
        ],
        compiler_params=pltpu.CompilerParams(vmem_limit_bytes=4 * 1024 * 1024),
        cost_estimate=pl.CostEstimate(flops=0, bytes_accessed=8 * rows * width, transcendentals=0),
        name="load",
    )(win_keys, win_values, cache_keys, cache_values, queries, valid_counts, first_block)


def ring_offsets(count):
    half = count // 2
    return [sign * step for step in range(1, half) for sign in (-1, 1)] + [half]


def place_piece(index, number, limit_row, own, sizes, limits, key, value, keys, values):
    window_rows, cache_rows = sizes
    cache_at = number * window_rows + index * cache_rows
    if not own:
        row_iota = lax.broadcasted_iota(jnp.int32, (window_rows, HD), 0)
        shown = row_iota < limits[limit_row : limit_row + 1, :]
    for head in range(keys.shape[0]):
        lanes = slice(head * HD, (head + 1) * HD)
        at = slice(index * window_rows, (index + 1) * window_rows)
        win_key, win_value = key[:window_rows, lanes], value[:window_rows, lanes]
        if own:
            keys[head, at, :] = win_key
            values[head, at, :HD] = win_value
            values[head, at, HD:] = jnp.ones((window_rows, HD), jnp.bfloat16)
        else:
            fill = key[window_rows : window_rows + 1, lanes].astype(jnp.float32)
            keys[head, at, :] = jnp.where(shown, win_key.astype(jnp.float32), fill).astype(jnp.bfloat16)
            values[head, at, :HD] = jnp.where(shown, win_value.astype(jnp.float32), 0.0).astype(jnp.bfloat16)
            values[head, at, HD:] = jnp.where(shown, 1.0, 0.0).astype(jnp.bfloat16)
        at = slice(cache_at, cache_at + cache_rows)
        keys[head, at, :] = key[window_rows:, lanes]
        values[head, at, :HD] = value[window_rows:, lanes]
        values[head, at, HD:] = jnp.ones((cache_rows, HD), jnp.bfloat16)


def fill_up(filled, keys, values):
    spare = keys.shape[1] - filled
    if spare:
        for head in range(keys.shape[0]):
            row = keys[head, filled - 1 : filled, :].astype(jnp.float32)
            keys[head, filled:, :] = jnp.broadcast_to(row, (spare, HD)).astype(jnp.bfloat16)
            values[head, filled:, :] = jnp.zeros((spare, 2 * HD), jnp.bfloat16)


def scores(query, keys):
    return lax.dot_general(query, keys, (((1,), (1,)), ((), ())), preferred_element_type=jnp.float32)


def weigh(score, top, values):
    lanes = score.shape[1] // HD
    weight = jnp.exp2(score * EXP_SCALE - jnp.concatenate([top] * lanes, axis=1)).astype(jnp.bfloat16)
    return jnp.dot(weight, values, preferred_element_type=jnp.float32)


def wide_top(score):
    return jnp.broadcast_to(jnp.max(score, axis=1, keepdims=True) * EXP_SCALE, (score.shape[0], HD))


def normalised(acc):
    total = acc[:, HD:]
    inverse = pl.reciprocal(total, approx=True)
    return (acc[:, :HD] * (inverse * (2.0 - total * inverse))).astype(jnp.bfloat16)


def chunks(q_ref, kv_heads):
    rows = q_ref.shape[0]
    group = q_ref.shape[1] // HD // kv_heads
    for head in range(kv_heads):
        for start in range(0, group, CHUNK_HEADS):
            base = head * group + start
            query = jnp.concatenate(
                [q_ref[:, (base + i) * HD : (base + i + 1) * HD] for i in range(CHUNK_HEADS)], axis=0
            )
            yield head, slice(base * rows, (base + CHUNK_HEADS) * rows), query, base


def first_kernel(count, sizes, q_ref, limits, own_keys, own_values, acc_out, top_out, keys, values):
    window_rows = sizes[0]
    place_piece(0, 1, 0, True, sizes, None, own_keys, own_values, keys, values)
    fill_up(sum(sizes), keys, values)
    rows = q_ref.shape[0]
    key_iota = lax.broadcasted_iota(jnp.int32, (rows, window_rows), 1)
    query_iota = lax.broadcasted_iota(jnp.int32, (rows, window_rows), 0)
    seen = (key_iota <= query_iota) & (key_iota < limits[count - 1 : count, :])
    bias = jnp.concatenate([jnp.where(seen, 0.0, HIDDEN)] * CHUNK_HEADS, axis=0)
    for head, at, query, _ in chunks(q_ref, keys.shape[0]):
        score = scores(query, keys[head])
        score = jnp.concatenate([score[:, :window_rows] + bias, score[:, window_rows:]], axis=1)
        top = wide_top(score)
        acc_out[at, :] = weigh(score, top, values[head])
        top_out[at, :] = top


def next_kernel(rows_of, last, sizes, q_ref, limits, *refs):
    number = len(rows_of)
    key_refs, value_refs = refs[: 2 * number : 2], refs[1 : 2 * number : 2]
    if last:
        acc_in, top_in, out, keys, values, result, sems = refs[2 * number :]
    else:
        acc_in, top_in, acc_out, top_out, keys, values = refs[2 * number :]
    for index, row in enumerate(rows_of):
        place_piece(index, number, row, False, sizes, limits, key_refs[index], value_refs[index], keys, values)
    fill_up(number * sum(sizes), keys, values)
    rows = q_ref.shape[0]
    kv_heads = keys.shape[0]

    def sent(base):
        lanes = slice(base * HD, (base + CHUNK_HEADS) * HD)
        return pltpu.make_async_copy(result.at[:, lanes], out.at[:, lanes], sems.at[base // CHUNK_HEADS])

    def settle(base, acc):
        done = normalised(acc)
        for i in range(CHUNK_HEADS):
            result[:, (base + i) * HD : (base + i + 1) * HD] = done[i * rows : (i + 1) * rows]
        sent(base).start()

    fine = jnp.ones((8, HD), jnp.float32)
    for head, at, query, base in chunks(q_ref, kv_heads):
        top = top_in[at, :]
        acc = acc_in[at, :] + weigh(scores(query, keys[head]), top, values[head])
        safe = jnp.where(acc[:, HD:] < LARGEST_TOTAL, 1.0, 0.0).reshape(-1, 8, HD)
        fine = jnp.minimum(fine, jnp.min(safe, axis=0))
        if last:
            settle(base, acc)
        else:
            acc_out[at, :] = acc
            top_out[at, :] = top
    if last:
        for base in range(0, kv_heads * (q_ref.shape[1] // HD // kv_heads), CHUNK_HEADS):
            sent(base).wait()

    @pl.when(jnp.min(fine) < 0.5)
    def _():
        for head, at, query, base in chunks(q_ref, kv_heads):
            score = scores(query, keys[head])
            before = top_in[at, :]
            top = jnp.maximum(before, wide_top(score))
            fade = jnp.exp2(before - top)
            acc = acc_in[at, :] * jnp.concatenate([fade, fade], axis=1) + weigh(score, top, values[head])
            if last:
                settle(base, acc)
                sent(base).wait()
            else:
                acc_out[at, :] = acc
                top_out[at, :] = top


def kernel_options(queries, total_keys, kv_heads):
    rows, width = queries.shape
    return {
        "compiler_params": pltpu.CompilerParams(vmem_limit_bytes=40 * 1024 * 1024),
        "cost_estimate": pl.CostEstimate(
            flops=6 * rows * width * total_keys,
            bytes_accessed=2 * rows * width,
            transcendentals=rows * (width // HD) * total_keys,
        ),
    }


def room(kv_heads, total_keys):
    return [
        pltpu.VMEM((kv_heads, total_keys, HD), jnp.bfloat16),
        pltpu.VMEM((kv_heads, total_keys, 2 * HD), jnp.bfloat16),
    ]


def state_shapes(queries):
    rows = queries.shape[0] * queries.shape[1] // HD
    return [jax.ShapeDtypeStruct((rows, 2 * HD), jnp.float32), jax.ShapeDtypeStruct((rows, HD), jnp.float32)]


def attend_first(count, sizes, queries, limits, own_keys, own_values):
    kv_heads = own_keys.shape[1] // HD
    total_keys = -(-sum(sizes) // HD) * HD
    vmem = pl.BlockSpec(memory_space=pltpu.VMEM)
    return tuple(
        pl.pallas_call(
            functools.partial(first_kernel, count, sizes),
            out_shape=state_shapes(queries),
            in_specs=[vmem] * 4,
            out_specs=[vmem] * 2,
            scratch_shapes=room(kv_heads, total_keys),
            name="attend_first",
            **kernel_options(queries, total_keys, kv_heads),
        )(queries, limits, own_keys, own_values)
    )


def attend_next(pieces, state, last, sizes, queries, limits):
    rows_of = tuple(piece[0] for piece in pieces)
    blocks = [block for piece in pieces for block in piece[1:]]
    kv_heads = blocks[0].shape[1] // HD
    total_keys = -(-len(pieces) * sum(sizes) // HD) * HD
    vmem = pl.BlockSpec(memory_space=pltpu.VMEM)
    operands = [queries, limits, *blocks, *state]
    shapes = [jax.ShapeDtypeStruct(queries.shape, queries.dtype)] if last else state_shapes(queries)
    scratch = room(kv_heads, total_keys)
    if last:
        chunk_count = queries.shape[1] // HD // CHUNK_HEADS
        scratch += [pltpu.VMEM(queries.shape, queries.dtype), pltpu.SemaphoreType.DMA((chunk_count,))]
    outs = pl.pallas_call(
        functools.partial(next_kernel, rows_of, last, sizes),
        out_shape=shapes,
        in_specs=[vmem] * len(operands),
        out_specs=[pl.BlockSpec(memory_space=pltpu.HBM)] if last else [vmem] * len(shapes),
        scratch_shapes=scratch,
        name="attend_last" if last else "attend_next",
        **kernel_options(queries, total_keys, kv_heads),
    )(*operands)
    return outs[0] if last else tuple(outs)


def shards(count, queries, win_keys, win_values, cache_keys, cache_values, valid_counts, first_block):
    sizes = (win_keys.shape[0], cache_keys.shape[0])
    half = count // 2
    ring = [place_at(p, count) for p in range(count)]
    onward = [(ring[p], ring[(p + 1) % count]) for p in range(count)]
    backward = [(b, a) for a, b in onward]

    win_keys, win_values, cache_keys, cache_values, valid_counts, first_block, queries = [
        pltpu.with_memory_space_constraint(x, pltpu.HBM)
        for x in (win_keys, win_values, cache_keys, cache_values, valid_counts, first_block, queries)
    ]
    own_keys, own_values, near, limits = load(
        count, win_keys, win_values, cache_keys, cache_values, queries, valid_counts, first_block
    )
    key_on = key_back = own_keys
    value_on = value_back = own_values
    state = attend_first(count, sizes, near, limits, own_keys, own_values)
    arrived = []
    for step in range(1, half + 1):
        key_on = lax.ppermute(key_on, "ctx", onward)
        value_back = lax.ppermute(value_back, "ctx", backward)
        if step < half:
            value_on = lax.ppermute(value_on, "ctx", onward)
            key_back = lax.ppermute(key_back, "ctx", backward)
            row = 2 * (step - 1)
            arrived.append([(row, key_on, value_on), (row + 1, key_back, value_back)])
        else:
            arrived.append([(2 * (half - 1), key_on, value_back)])
        if step == 1:
            key_on, top = lax.optimization_barrier((key_on, state[1]))
            state = (state[0], top)
    for begin in range(0, half - 2, 2):
        pieces = [piece for step in arrived[begin : min(begin + 2, half - 2)] for piece in step]
        state = attend_next(pieces, state, False, sizes, near, limits)
    state = attend_next(arrived[half - 2], state, False, sizes, near, limits)
    return attend_next(arrived[half - 1], state, True, sizes, near, limits)


def solution(mesh):
    in_specs = (
        P(("groups", "ctx"), "tp"),
        P(("groups", "ctx"), "tp"),
        P(("groups", "ctx"), "tp"),
        P(("groups", "ctx"), "tp"),
        P(("groups", "ctx"), "tp"),
        P("groups"),
        P("groups"),
    )
    out_specs = P(("groups", "ctx"), "tp")
    return jax.shard_map(
        functools.partial(shards, mesh.shape["ctx"]),
        mesh=mesh,
        in_specs=in_specs,
        out_specs=out_specs,
        check_vma=False,
    )
```

```python
import functools
import math

import jax
import jax.numpy as jnp
from jax import lax
from jax.experimental import pallas as pl
from jax.experimental.pallas import tpu as pltpu
from jax.sharding import PartitionSpec as P

HD = 128
EXP_SCALE = HD**-0.5 * math.log2(math.e)
HIDDEN = -1.0e30
CHUNK_HEADS = 4
QUERY_COPIES = 4
LARGEST_TOTAL = 2.0**100


def ring_width(count):
    width = round(count ** (1 / 3))
    if width > 1 and count % width == 0 and (count // width) % 2 == 0:
        return width
    return 1


def place_at(position, count):
    width = ring_width(count)
    if width == 1:
        return position
    rows = count // width
    row, step = position // (width - 1), position % (width - 1)
    forth = row * width + 1 + step
    back = row * width + width - 1 - step
    home = (rows - 1 - (position - rows * (width - 1))) * width
    if isinstance(position, int):
        return home if position >= rows * (width - 1) else (back if row % 2 else forth)
    return jnp.where(position >= rows * (width - 1), home, jnp.where(row % 2 == 1, back, forth))


def position_of(place, count):
    width = ring_width(count)
    if width == 1:
        return place
    rows = count // width
    row, column = place // width, place % width
    snake = row * (width - 1) + jnp.where(row % 2 == 1, width - 1 - column, column - 1)
    return jnp.where(column == 0, rows * (width - 1) + rows - 1 - row, snake)


def load_kernel(count, win_keys, win_values, cache_keys, cache_values, q_hbm, valid_hbm, first_hbm, *refs):
    keys, values, q_ref, limits, valid_ref, first_ref, sems = refs
    window_rows = win_keys.shape[0]
    rows = q_ref.shape[0] // QUERY_COPIES
    pairs = [
        (valid_hbm, valid_ref),
        (first_hbm, first_ref),
        (win_keys, keys.at[:window_rows]),
        (cache_keys, keys.at[window_rows:]),
        (win_values, values.at[:window_rows]),
        (cache_values, values.at[window_rows:]),
    ] + [(q_hbm.at[i * rows : (i + 1) * rows], q_ref.at[i * rows : (i + 1) * rows]) for i in range(QUERY_COPIES)]
    copies = [pltpu.make_async_copy(*pair, sems.at[index]) for index, pair in enumerate(pairs)]
    for copy in copies:
        copy.start()
    for copy in copies[:2]:
        copy.wait()
    me = lax.axis_index("ctx")
    position = position_of(me, count)
    first = first_ref[me]
    for row, offset in enumerate(ring_offsets(count)):
        place = place_at(lax.rem(position + offset + count, count), count)
        limit = jnp.where((place >= first) & (place <= me), valid_ref[place], 0)
        limits[row : row + 1, :] = jnp.full((1, HD), limit, jnp.int32)
    limits[count - 1 : count, :] = jnp.full((1, HD), valid_ref[me], jnp.int32)
    for copy in copies[2:]:
        copy.wait()


def load(count, win_keys, win_values, cache_keys, cache_values, queries, valid_counts, first_block):
    rows, width = win_keys.shape[0] + cache_keys.shape[0], win_keys.shape[1]
    return pl.pallas_call(
        functools.partial(load_kernel, count),
        out_shape=[
            jax.ShapeDtypeStruct((rows, width), win_keys.dtype),
            jax.ShapeDtypeStruct((rows, width), win_keys.dtype),
            jax.ShapeDtypeStruct(queries.shape, queries.dtype),
            jax.ShapeDtypeStruct((-(-count // 8) * 8, HD), jnp.int32),
        ],
        in_specs=[pl.BlockSpec(memory_space=pltpu.HBM)] * 7,
        out_specs=[pl.BlockSpec(memory_space=pltpu.VMEM)] * 4,
        scratch_shapes=[
            pltpu.SMEM(valid_counts.shape, jnp.int32),
            pltpu.SMEM(first_block.shape, jnp.int32),
            pltpu.SemaphoreType.DMA((6 + QUERY_COPIES,)),
        ],
        compiler_params=pltpu.CompilerParams(vmem_limit_bytes=4 * 1024 * 1024),
        cost_estimate=pl.CostEstimate(flops=0, bytes_accessed=8 * rows * width, transcendentals=0),
        name="load",
    )(win_keys, win_values, cache_keys, cache_values, queries, valid_counts, first_block)


def ring_offsets(count):
    half = count // 2
    return [sign * step for step in range(1, half) for sign in (-1, 1)] + [half]


def place_piece(index, number, limit_row, own, sizes, limits, key, value, keys, values):
    window_rows, cache_rows = sizes
    cache_at = number * window_rows + index * cache_rows
    if not own:
        row_iota = lax.broadcasted_iota(jnp.int32, (window_rows, HD), 0)
        shown = row_iota < limits[limit_row : limit_row + 1, :]
    for head in range(keys.shape[0]):
        lanes = slice(head * HD, (head + 1) * HD)
        at = slice(index * window_rows, (index + 1) * window_rows)
        win_key, win_value = key[:window_rows, lanes], value[:window_rows, lanes]
        if own:
            keys[head, at, :] = win_key
            values[head, at, :HD] = win_value
            values[head, at, HD:] = jnp.ones((window_rows, HD), jnp.bfloat16)
        else:
            fill = key[window_rows : window_rows + 1, lanes].astype(jnp.float32)
            keys[head, at, :] = jnp.where(shown, win_key.astype(jnp.float32), fill).astype(jnp.bfloat16)
            values[head, at, :HD] = jnp.where(shown, win_value.astype(jnp.float32), 0.0).astype(jnp.bfloat16)
            values[head, at, HD:] = jnp.where(shown, 1.0, 0.0).astype(jnp.bfloat16)
        at = slice(cache_at, cache_at + cache_rows)
        keys[head, at, :] = key[window_rows:, lanes]
        values[head, at, :HD] = value[window_rows:, lanes]
        values[head, at, HD:] = jnp.ones((cache_rows, HD), jnp.bfloat16)


def fill_up(filled, keys, values):
    spare = keys.shape[1] - filled
    if spare:
        for head in range(keys.shape[0]):
            row = keys[head, filled - 1 : filled, :].astype(jnp.float32)
            keys[head, filled:, :] = jnp.broadcast_to(row, (spare, HD)).astype(jnp.bfloat16)
            values[head, filled:, :] = jnp.zeros((spare, 2 * HD), jnp.bfloat16)


def scores(query, keys):
    return lax.dot_general(query, keys, (((1,), (1,)), ((), ())), preferred_element_type=jnp.float32)


def weigh(score, top, values):
    lanes = score.shape[1] // HD
    weight = jnp.exp2(score * EXP_SCALE - jnp.concatenate([top] * lanes, axis=1)).astype(jnp.bfloat16)
    return jnp.dot(weight, values, preferred_element_type=jnp.float32)


def wide_top(score):
    return jnp.broadcast_to(jnp.max(score, axis=1, keepdims=True) * EXP_SCALE, (score.shape[0], HD))


def head_lanes(head, heads, rows):
    width = HD // heads
    lane = lax.broadcasted_iota(jnp.int32, (rows, HD), 1)
    return (lane >= head * width) & (lane < (head + 1) * width)


def pack_totals(packed, sums, base, heads):
    rows = packed.shape[0]
    for i in range(CHUNK_HEADS):
        packed = jnp.where(head_lanes(base + i, heads, rows), sums[i * rows : (i + 1) * rows], packed)
    return packed


def by_row(packed, base, heads):
    rows, width = packed.shape[0], HD // heads
    columns = [packed[:, (base + i) * width : (base + i) * width + 1] for i in range(CHUNK_HEADS)]
    return jnp.concatenate([jnp.broadcast_to(column, (rows, HD)) for column in columns], axis=0)


def chunks(q_ref, kv_heads):
    rows = q_ref.shape[0]
    group = q_ref.shape[1] // HD // kv_heads
    for head in range(kv_heads):
        for start in range(0, group, CHUNK_HEADS):
            base = head * group + start
            query = jnp.concatenate(
                [q_ref[:, (base + i) * HD : (base + i + 1) * HD] for i in range(CHUNK_HEADS)], axis=0
            )
            yield head, slice(base * rows, (base + CHUNK_HEADS) * rows), query, base


def first_kernel(count, sizes, q_ref, limits, own_keys, own_values, acc_out, total_out, flag_out, top_out, keys, values):
    window_rows = sizes[0]
    place_piece(0, 1, 0, True, sizes, None, own_keys, own_values, keys, values)
    fill_up(sum(sizes), keys, values)
    rows, heads = q_ref.shape[0], q_ref.shape[1] // HD
    key_iota = lax.broadcasted_iota(jnp.int32, (rows, window_rows), 1)
    query_iota = lax.broadcasted_iota(jnp.int32, (rows, window_rows), 0)
    seen = (key_iota <= query_iota) & (key_iota < limits[count - 1 : count, :])
    bias = jnp.concatenate([jnp.where(seen, 0.0, HIDDEN)] * CHUNK_HEADS, axis=0)
    packed = jnp.zeros((rows, HD), jnp.float32)
    for head, at, query, base in chunks(q_ref, keys.shape[0]):
        score = scores(query, keys[head])
        score = jnp.concatenate([score[:, :window_rows] + bias, score[:, window_rows:]], axis=1)
        top = wide_top(score)
        added = weigh(score, top, values[head])
        acc_out[at, :] = added[:, :HD]
        top_out[at, :] = top
        packed = pack_totals(packed, added[:, HD:], base, heads)
    total_out[...] = packed
    flag_out[...] = jnp.zeros(flag_out.shape, jnp.float32)


def next_kernel(rows_of, last, sizes, q_ref, limits, top_ref, *refs):
    number = len(rows_of)
    key_refs, value_refs = refs[: 2 * number : 2], refs[1 : 2 * number : 2]
    acc_in, total_in, flag_in, other_in, *refs = refs[2 * number :]
    if last:
        out, keys, values, before_ref, result, sems = refs
    else:
        acc_out, total_out, flag_out, other_out, keys, values, before_ref = refs
    for index, row in enumerate(rows_of):
        place_piece(index, number, row, False, sizes, limits, key_refs[index], value_refs[index], keys, values)
    fill_up(number * sum(sizes), keys, values)
    rows, heads = q_ref.shape[0], q_ref.shape[1] // HD
    kv_heads = keys.shape[0]

    def sent(head):
        lanes = slice(head * HD, (head + 2) * HD)
        return pltpu.make_async_copy(result.at[:, lanes], out.at[:, lanes], sems.at[head // 2])

    def settle(base, acc, total):
        inverse = pl.reciprocal(total, approx=True)
        inverse = inverse * (2.0 - total * inverse)
        done = (acc * by_row(inverse, base, heads)).astype(jnp.bfloat16)
        for i in range(CHUNK_HEADS):
            result[:, (base + i) * HD : (base + i + 1) * HD] = done[i * rows : (i + 1) * rows]
            if i % 2:
                sent(base + i - 1).start()

    def wait_all():
        for head in range(0, heads, 2):
            sent(head).wait()

    packed = jnp.zeros((rows, HD), jnp.float32)
    for head, at, query, base in chunks(q_ref, kv_heads):
        added = weigh(scores(query, keys[head]), top_ref[at, :], values[head])
        acc = acc_in[at, :] + added[:, :HD]
        packed = pack_totals(packed, added[:, HD:], base, heads)
        if last:
            settle(base, acc, total_in[...] + packed)
        else:
            acc_out[at, :] = acc
    total = total_in[...] + packed
    large = jnp.where(total < LARGEST_TOTAL, 0.0, 1.0).reshape(-1, 8, HD)
    large = jnp.maximum(jnp.max(large, axis=0), flag_in[...])
    again = jnp.max(large) > 0.5
    if last:
        wait_all()
    else:
        total_out[...] = total
        flag_out[...] = jnp.broadcast_to(jnp.where(again, 1.0, 0.0), flag_out.shape)

    @pl.when(again)
    def _():
        moved = jnp.max(flag_in[...]) > 0.5

        @pl.when(moved)
        def _():
            before_ref[...] = other_in[...]

        @pl.when(jnp.logical_not(moved))
        def _():
            before_ref[...] = top_ref[...]

        packed = jnp.zeros((rows, HD), jnp.float32)
        for head, at, query, base in chunks(q_ref, kv_heads):
            score = scores(query, keys[head])
            before = before_ref[at, :]
            top = jnp.maximum(before, wide_top(score))
            fade = jnp.exp2(before - top)
            added = weigh(score, top, values[head])
            acc = acc_in[at, :] * fade + added[:, :HD]
            total = by_row(total_in[...], base, heads) * fade + added[:, HD:]
            packed = pack_totals(packed, total, base, heads)
            if last:
                settle(base, acc, packed)
            else:
                acc_out[at, :] = acc
                other_out[at, :] = top
        if last:
            wait_all()
        else:
            total_out[...] = packed


def kernel_options(queries, total_keys, kv_heads):
    rows, width = queries.shape
    return {
        "compiler_params": pltpu.CompilerParams(vmem_limit_bytes=40 * 1024 * 1024),
        "cost_estimate": pl.CostEstimate(
            flops=6 * rows * width * total_keys,
            bytes_accessed=2 * rows * width,
            transcendentals=rows * (width // HD) * total_keys,
        ),
    }


def room(kv_heads, total_keys):
    return [
        pltpu.VMEM((kv_heads, total_keys, HD), jnp.bfloat16),
        pltpu.VMEM((kv_heads, total_keys, 2 * HD), jnp.bfloat16),
    ]


def state_shapes(queries):
    rows = queries.shape[0] * queries.shape[1] // HD
    shapes = [(rows, HD), (queries.shape[0], HD), (8, HD), (rows, HD)]
    return [jax.ShapeDtypeStruct(shape, jnp.float32) for shape in shapes]


def attend_first(count, sizes, queries, limits, own_keys, own_values):
    kv_heads = own_keys.shape[1] // HD
    total_keys = -(-sum(sizes) // HD) * HD
    vmem = pl.BlockSpec(memory_space=pltpu.VMEM)
    return tuple(
        pl.pallas_call(
            functools.partial(first_kernel, count, sizes),
            out_shape=state_shapes(queries),
            in_specs=[vmem] * 4,
            out_specs=[vmem] * 4,
            scratch_shapes=room(kv_heads, total_keys),
            name="attend_first",
            **kernel_options(queries, total_keys, kv_heads),
        )(queries, limits, own_keys, own_values)
    )


def attend_next(pieces, state, last, sizes, queries, limits, top):
    rows_of = tuple(piece[0] for piece in pieces)
    blocks = [block for piece in pieces for block in piece[1:]]
    kv_heads = blocks[0].shape[1] // HD
    total_keys = -(-len(pieces) * sum(sizes) // HD) * HD
    vmem = pl.BlockSpec(memory_space=pltpu.VMEM)
    operands = [queries, limits, top, *blocks, *state]
    shapes = [jax.ShapeDtypeStruct(queries.shape, queries.dtype)] if last else state_shapes(queries)
    scratch = [*room(kv_heads, total_keys), pltpu.VMEM(top.shape, top.dtype)]
    if last:
        pairs_of_heads = queries.shape[1] // HD // 2
        scratch += [pltpu.VMEM(queries.shape, queries.dtype), pltpu.SemaphoreType.DMA((pairs_of_heads,))]
    outs = pl.pallas_call(
        functools.partial(next_kernel, rows_of, last, sizes),
        out_shape=shapes,
        in_specs=[vmem] * len(operands),
        out_specs=[pl.BlockSpec(memory_space=pltpu.HBM)] if last else [vmem] * len(shapes),
        scratch_shapes=scratch,
        name="attend_last" if last else "attend_next",
        **kernel_options(queries, total_keys, kv_heads),
    )(*operands)
    return outs[0] if last else tuple(outs)


def shards(count, queries, win_keys, win_values, cache_keys, cache_values, valid_counts, first_block):
    sizes = (win_keys.shape[0], cache_keys.shape[0])
    half = count // 2
    ring = [place_at(p, count) for p in range(count)]
    onward = [(ring[p], ring[(p + 1) % count]) for p in range(count)]
    backward = [(b, a) for a, b in onward]

    win_keys, win_values, cache_keys, cache_values, valid_counts, first_block, queries = [
        pltpu.with_memory_space_constraint(x, pltpu.HBM)
        for x in (win_keys, win_values, cache_keys, cache_values, valid_counts, first_block, queries)
    ]
    own_keys, own_values, near, limits = load(
        count, win_keys, win_values, cache_keys, cache_values, queries, valid_counts, first_block
    )
    key_on = key_back = own_keys
    value_on = value_back = own_values
    state = attend_first(count, sizes, near, limits, own_keys, own_values)
    arrived = []
    for step in range(1, half + 1):
        key_on = lax.ppermute(key_on, "ctx", onward)
        value_back = lax.ppermute(value_back, "ctx", backward)
        if step < half:
            value_on = lax.ppermute(value_on, "ctx", onward)
            key_back = lax.ppermute(key_back, "ctx", backward)
            row = 2 * (step - 1)
            arrived.append([(row, key_on, value_on), (row + 1, key_back, value_back)])
        else:
            arrived.append([(2 * (half - 1), key_on, value_back)])
        if step == 1:
            key_on, *state = lax.optimization_barrier((key_on, *state))
    top = state[3]
    for begin in range(0, half - 2, 2):
        pieces = [piece for step in arrived[begin : min(begin + 2, half - 2)] for piece in step]
        state = attend_next(pieces, state, False, sizes, near, limits, top)
    state = attend_next(arrived[half - 2], state, False, sizes, near, limits, top)
    return attend_next(arrived[half - 1], state, True, sizes, near, limits, top)


def solution(mesh):
    in_specs = (
        P(("groups", "ctx"), "tp"),
        P(("groups", "ctx"), "tp"),
        P(("groups", "ctx"), "tp"),
        P(("groups", "ctx"), "tp"),
        P(("groups", "ctx"), "tp"),
        P("groups"),
        P("groups"),
    )
    out_specs = P(("groups", "ctx"), "tp")
    return jax.shard_map(
        functools.partial(shards, mesh.shape["ctx"]),
        mesh=mesh,
        in_specs=in_specs,
        out_specs=out_specs,
        check_vma=False,
    )
```

```python
import functools
import math

import jax
import jax.numpy as jnp
from jax import lax
from jax.experimental import pallas as pl
from jax.experimental.pallas import tpu as pltpu
from jax.sharding import PartitionSpec as P

HD = 128
EXP_SCALE = HD**-0.5 * math.log2(math.e)
HIDDEN = -1.0e30
CHUNK_HEADS = 4
LARGEST_TOTAL = 2.0**100


def ring_width(count):
    width = round(count ** (1 / 3))
    if width > 1 and count % width == 0 and (count // width) % 2 == 0:
        return width
    return 1


def place_at(position, count):
    width = ring_width(count)
    if width == 1:
        return position
    rows = count // width
    row, step = position // (width - 1), position % (width - 1)
    forth = row * width + 1 + step
    back = row * width + width - 1 - step
    home = (rows - 1 - (position - rows * (width - 1))) * width
    if isinstance(position, int):
        return home if position >= rows * (width - 1) else (back if row % 2 else forth)
    return jnp.where(position >= rows * (width - 1), home, jnp.where(row % 2 == 1, back, forth))


def position_of(place, count):
    width = ring_width(count)
    if width == 1:
        return place
    rows = count // width
    row, column = place // width, place % width
    snake = row * (width - 1) + jnp.where(row % 2 == 1, width - 1 - column, column - 1)
    return jnp.where(column == 0, rows * (width - 1) + rows - 1 - row, snake)


def load_kernel(count, win_keys, win_values, cache_keys, cache_values, q_hbm, valid_hbm, first_hbm, *refs):
    keys, values, q_ref, limits, valid_ref, first_ref, sems = refs
    window_rows = win_keys.shape[0]
    pairs = [
        (valid_hbm, valid_ref),
        (first_hbm, first_ref),
        (win_keys, keys.at[:window_rows]),
        (cache_keys, keys.at[window_rows:]),
        (win_values, values.at[:window_rows]),
        (cache_values, values.at[window_rows:]),
        (q_hbm, q_ref),
    ]
    copies = [pltpu.make_async_copy(*pair, sems.at[index]) for index, pair in enumerate(pairs)]
    for copy in copies:
        copy.start()
    for copy in copies[:2]:
        copy.wait()
    me = lax.axis_index("ctx")
    position = position_of(me, count)
    first = first_ref[me]
    for row, offset in enumerate(ring_offsets(count)):
        place = place_at(lax.rem(position + offset + count, count), count)
        limit = jnp.where((place >= first) & (place <= me), valid_ref[place], 0)
        limits[row : row + 1, :] = jnp.full((1, HD), limit, jnp.int32)
    limits[count - 1 : count, :] = jnp.full((1, HD), valid_ref[me], jnp.int32)
    for copy in copies[2:]:
        copy.wait()


def load(count, win_keys, win_values, cache_keys, cache_values, queries, valid_counts, first_block):
    rows, width = win_keys.shape[0] + cache_keys.shape[0], win_keys.shape[1]
    return pl.pallas_call(
        functools.partial(load_kernel, count),
        out_shape=[
            jax.ShapeDtypeStruct((rows, width), win_keys.dtype),
            jax.ShapeDtypeStruct((rows, width), win_keys.dtype),
            jax.ShapeDtypeStruct(queries.shape, queries.dtype),
            jax.ShapeDtypeStruct((-(-count // 8) * 8, HD), jnp.int32),
        ],
        in_specs=[pl.BlockSpec(memory_space=pltpu.HBM)] * 7,
        out_specs=[pl.BlockSpec(memory_space=pltpu.VMEM)] * 4,
        scratch_shapes=[
            pltpu.SMEM(valid_counts.shape, jnp.int32),
            pltpu.SMEM(first_block.shape, jnp.int32),
            pltpu.SemaphoreType.DMA((7,)),
        ],
        compiler_params=pltpu.CompilerParams(vmem_limit_bytes=4 * 1024 * 1024),
        cost_estimate=pl.CostEstimate(flops=0, bytes_accessed=8 * rows * width, transcendentals=0),
        name="load",
    )(win_keys, win_values, cache_keys, cache_values, queries, valid_counts, first_block)


def ring_offsets(count):
    half = count // 2
    return [sign * step for step in range(1, half) for sign in (-1, 1)] + [half]


def place_window(index, limit_row, own, sizes, limits, key, value, keys, values):
    window_rows = sizes[0]
    if not own:
        row_iota = lax.broadcasted_iota(jnp.int32, (window_rows, HD), 0)
        shown = row_iota < limits[limit_row : limit_row + 1, :]
    at = slice(index * window_rows, (index + 1) * window_rows)
    for head in range(keys.shape[0]):
        lanes = slice(head * HD, (head + 1) * HD)
        win_key, win_value = key[:window_rows, lanes], value[:window_rows, lanes]
        if own:
            keys[head, at, :] = win_key
            values[head, at, :HD] = win_value
            values[head, at, HD:] = jnp.ones((window_rows, HD), jnp.bfloat16)
        else:
            fill = key[window_rows : window_rows + 1, lanes].astype(jnp.float32)
            keys[head, at, :] = jnp.where(shown, win_key.astype(jnp.float32), fill).astype(jnp.bfloat16)
            values[head, at, :HD] = jnp.where(shown, win_value.astype(jnp.float32), 0.0).astype(jnp.bfloat16)
            values[head, at, HD:] = jnp.where(shown, 1.0, 0.0).astype(jnp.bfloat16)


def place_cache(index, number, sizes, key, value, keys, values):
    window_rows, cache_rows = sizes
    start = number * window_rows + index * cache_rows
    at = slice(start, start + cache_rows)
    for head in range(keys.shape[0]):
        lanes = slice(head * HD, (head + 1) * HD)
        keys[head, at, :] = key[window_rows:, lanes]
        values[head, at, :HD] = value[window_rows:, lanes]
        values[head, at, HD:] = jnp.ones((cache_rows, HD), jnp.bfloat16)


def fill_up(filled, keys, values):
    spare = keys.shape[1] - filled
    if spare:
        for head in range(keys.shape[0]):
            row = keys[head, filled - 1 : filled, :].astype(jnp.float32)
            keys[head, filled:, :] = jnp.broadcast_to(row, (spare, HD)).astype(jnp.bfloat16)
            values[head, filled:, :] = jnp.zeros((spare, 2 * HD), jnp.bfloat16)


def scores(query, keys):
    return lax.dot_general(query, keys, (((1,), (1,)), ((), ())), preferred_element_type=jnp.float32)


def weigh(score, top, values):
    lanes = score.shape[1] // HD
    weight = jnp.exp2(score * EXP_SCALE - jnp.concatenate([top] * lanes, axis=1)).astype(jnp.bfloat16)
    return jnp.dot(weight, values, preferred_element_type=jnp.float32)


def wide_top(score):
    return jnp.broadcast_to(jnp.max(score, axis=1, keepdims=True) * EXP_SCALE, (score.shape[0], HD))


def normalised(acc):
    total = acc[:, HD:]
    inverse = pl.reciprocal(total, approx=True)
    return (acc[:, :HD] * (inverse * (2.0 - total * inverse))).astype(jnp.bfloat16)


def chunks(q_ref, kv_heads):
    rows = q_ref.shape[0]
    group = q_ref.shape[1] // HD // kv_heads
    for head in range(kv_heads):
        for start in range(0, group, CHUNK_HEADS):
            base = head * group + start
            query = jnp.concatenate(
                [q_ref[:, (base + i) * HD : (base + i + 1) * HD] for i in range(CHUNK_HEADS)], axis=0
            )
            yield head, slice(base * rows, (base + CHUNK_HEADS) * rows), query, base


def first_kernel(count, sizes, q_ref, limits, own_keys, own_values, acc_out, top_out, keys, values):
    window_rows = sizes[0]
    place_window(0, 0, True, sizes, None, own_keys, own_values, keys, values)
    place_cache(0, 1, sizes, own_keys, own_values, keys, values)
    fill_up(sum(sizes), keys, values)
    rows = q_ref.shape[0]
    key_iota = lax.broadcasted_iota(jnp.int32, (rows, window_rows), 1)
    query_iota = lax.broadcasted_iota(jnp.int32, (rows, window_rows), 0)
    seen = (key_iota <= query_iota) & (key_iota < limits[count - 1 : count, :])
    bias = jnp.concatenate([jnp.where(seen, 0.0, HIDDEN)] * CHUNK_HEADS, axis=0)
    for head, at, query, _ in chunks(q_ref, keys.shape[0]):
        score = scores(query, keys[head])
        score = jnp.concatenate([score[:, :window_rows] + bias, score[:, window_rows:]], axis=1)
        top = wide_top(score)
        acc_out[at, :] = weigh(score, top, values[head])
        top_out[at, :] = top


def next_kernel(rows_of, last, count, sizes, q_ref, limits, *refs):
    number = len(rows_of)
    key_refs, value_refs = refs[: 2 * number : 2], refs[1 : 2 * number : 2]
    if last:
        acc_in, top_in, out, keys, values, result, sems = refs[2 * number :]
    else:
        acc_in, top_in, acc_out, top_out, keys, values = refs[2 * number :]
    rows, heads = q_ref.shape[0], q_ref.shape[1] // HD
    kv_heads = keys.shape[0]

    def sent(base):
        lanes = slice(base * HD, (base + CHUNK_HEADS) * HD)
        return pltpu.make_async_copy(result.at[:, lanes], out.at[:, lanes], sems.at[base // CHUNK_HEADS])

    def settle(base, acc):
        done = normalised(acc)
        for i in range(CHUNK_HEADS):
            result[:, (base + i) * HD : (base + i + 1) * HD] = done[i * rows : (i + 1) * rows]
        sent(base).start()

    def take_in(begin):
        fine = jnp.ones((8, HD), jnp.float32)
        for head, at, query, base in chunks(q_ref, kv_heads):
            top = top_in[at, :]
            acc = acc_in[at, :] + weigh(scores(query, keys[head, begin:]), top, values[head, begin:])
            safe = jnp.where(acc[:, HD:] < LARGEST_TOTAL, 1.0, 0.0).reshape(-1, 8, HD)
            fine = jnp.minimum(fine, jnp.min(safe, axis=0))
            if last:
                settle(base, acc)
            else:
                acc_out[at, :] = acc
                top_out[at, :] = top
        if last:
            for base in range(0, heads, CHUNK_HEADS):
                sent(base).wait()

        @pl.when(jnp.min(fine) < 0.5)
        def _():
            for head, at, query, base in chunks(q_ref, kv_heads):
                score = scores(query, keys[head, begin:])
                before = top_in[at, :]
                top = jnp.maximum(before, wide_top(score))
                fade = jnp.exp2(before - top)
                acc = acc_in[at, :] * jnp.concatenate([fade, fade], axis=1)
                acc = acc + weigh(score, top, values[head, begin:])
                if last:
                    settle(base, acc)
                    sent(base).wait()
                else:
                    acc_out[at, :] = acc
                    top_out[at, :] = top

    for index in range(number):
        place_cache(index, number, sizes, key_refs[index], value_refs[index], keys, values)
    fill_up(number * sum(sizes), keys, values)
    me = lax.axis_index("ctx")
    position = position_of(me, count)
    offsets = ring_offsets(count)
    places = [place_at(lax.rem(position + offsets[row] + count, count), count) for row in rows_of]
    earlier = functools.reduce(jnp.logical_or, [place < me for place in places])

    @pl.when(earlier)
    def _():
        for index, row in enumerate(rows_of):
            place_window(index, row, False, sizes, limits, key_refs[index], value_refs[index], keys, values)
        take_in(0)

    @pl.when(jnp.logical_not(earlier))
    def _():
        take_in(number * sizes[0])


def kernel_options(queries, total_keys, kv_heads):
    rows, width = queries.shape
    return {
        "compiler_params": pltpu.CompilerParams(vmem_limit_bytes=40 * 1024 * 1024),
        "cost_estimate": pl.CostEstimate(
            flops=6 * rows * width * total_keys,
            bytes_accessed=2 * rows * width,
            transcendentals=rows * (width // HD) * total_keys,
        ),
    }


def room(kv_heads, total_keys):
    return [
        pltpu.VMEM((kv_heads, total_keys, HD), jnp.bfloat16),
        pltpu.VMEM((kv_heads, total_keys, 2 * HD), jnp.bfloat16),
    ]


def state_shapes(queries):
    rows = queries.shape[0] * queries.shape[1] // HD
    return [jax.ShapeDtypeStruct((rows, 2 * HD), jnp.float32), jax.ShapeDtypeStruct((rows, HD), jnp.float32)]


def attend_first(count, sizes, queries, limits, own_keys, own_values):
    kv_heads = own_keys.shape[1] // HD
    total_keys = -(-sum(sizes) // HD) * HD
    vmem = pl.BlockSpec(memory_space=pltpu.VMEM)
    return tuple(
        pl.pallas_call(
            functools.partial(first_kernel, count, sizes),
            out_shape=state_shapes(queries),
            in_specs=[vmem] * 4,
            out_specs=[vmem] * 2,
            scratch_shapes=room(kv_heads, total_keys),
            name="attend_first",
            **kernel_options(queries, total_keys, kv_heads),
        )(queries, limits, own_keys, own_values)
    )


def attend_next(pieces, state, last, count, sizes, queries, limits):
    rows_of = tuple(piece[0] for piece in pieces)
    blocks = [block for piece in pieces for block in piece[1:]]
    kv_heads = blocks[0].shape[1] // HD
    total_keys = -(-len(pieces) * sum(sizes) // HD) * HD
    vmem = pl.BlockSpec(memory_space=pltpu.VMEM)
    operands = [queries, limits, *blocks, *state]
    shapes = [jax.ShapeDtypeStruct(queries.shape, queries.dtype)] if last else state_shapes(queries)
    scratch = room(kv_heads, total_keys)
    if last:
        chunk_count = queries.shape[1] // HD // CHUNK_HEADS
        scratch += [pltpu.VMEM(queries.shape, queries.dtype), pltpu.SemaphoreType.DMA((chunk_count,))]
    outs = pl.pallas_call(
        functools.partial(next_kernel, rows_of, last, count, sizes),
        out_shape=shapes,
        in_specs=[vmem] * len(operands),
        out_specs=[pl.BlockSpec(memory_space=pltpu.HBM)] if last else [vmem] * len(shapes),
        scratch_shapes=scratch,
        name="attend_last" if last else "attend_next",
        **kernel_options(queries, total_keys, kv_heads),
    )(*operands)
    return outs[0] if last else tuple(outs)


def shards(count, queries, win_keys, win_values, cache_keys, cache_values, valid_counts, first_block):
    sizes = (win_keys.shape[0], cache_keys.shape[0])
    half = count // 2
    ring = [place_at(p, count) for p in range(count)]
    onward = [(ring[p], ring[(p + 1) % count]) for p in range(count)]
    backward = [(b, a) for a, b in onward]

    win_keys, win_values, cache_keys, cache_values, valid_counts, first_block, queries = [
        pltpu.with_memory_space_constraint(x, pltpu.HBM)
        for x in (win_keys, win_values, cache_keys, cache_values, valid_counts, first_block, queries)
    ]
    own_keys, own_values, near, limits = load(
        count, win_keys, win_values, cache_keys, cache_values, queries, valid_counts, first_block
    )
    key_on = key_back = own_keys
    value_on = value_back = own_values
    state = attend_first(count, sizes, near, limits, own_keys, own_values)
    arrived = []
    for step in range(1, half + 1):
        key_on = lax.ppermute(key_on, "ctx", onward)
        value_back = lax.ppermute(value_back, "ctx", backward)
        if step < half:
            value_on = lax.ppermute(value_on, "ctx", onward)
            key_back = lax.ppermute(key_back, "ctx", backward)
            row = 2 * (step - 1)
            arrived.append([(row, key_on, value_on), (row + 1, key_back, value_back)])
        else:
            arrived.append([(2 * (half - 1), key_on, value_back)])
        if step == 1:
            key_on, top = lax.optimization_barrier((key_on, state[1]))
            state = (state[0], top)
    for begin in range(0, half - 2, 2):
        pieces = [piece for step in arrived[begin : min(begin + 2, half - 2)] for piece in step]
        state = attend_next(pieces, state, False, count, sizes, near, limits)
    state = attend_next(arrived[half - 2], state, False, count, sizes, near, limits)
    return attend_next(arrived[half - 1], state, True, count, sizes, near, limits)


def solution(mesh):
    in_specs = (
        P(("groups", "ctx"), "tp"),
        P(("groups", "ctx"), "tp"),
        P(("groups", "ctx"), "tp"),
        P(("groups", "ctx"), "tp"),
        P(("groups", "ctx"), "tp"),
        P("groups"),
        P("groups"),
    )
    out_specs = P(("groups", "ctx"), "tp")
    return jax.shard_map(
        functools.partial(shards, mesh.shape["ctx"]),
        mesh=mesh,
        in_specs=in_specs,
        out_specs=out_specs,
        check_vma=False,
    )
```

```python
import functools
import math

import jax
import jax.numpy as jnp
from jax import lax
from jax.experimental import pallas as pl
from jax.experimental.pallas import tpu as pltpu
from jax.sharding import PartitionSpec as P

HD = 128
EXP_SCALE = HD**-0.5 * math.log2(math.e)
HIDDEN = -1.0e30
CHUNK_HEADS = 8
LAST_CHUNK_HEADS = 4
LARGEST_TOTAL = 2.0**100


def ring_width(count):
    width = round(count ** (1 / 3))
    if width > 1 and count % width == 0 and (count // width) % 2 == 0:
        return width
    return 1


def place_at(position, count):
    width = ring_width(count)
    if width == 1:
        return position
    rows = count // width
    row, step = position // (width - 1), position % (width - 1)
    forth = row * width + 1 + step
    back = row * width + width - 1 - step
    home = (rows - 1 - (position - rows * (width - 1))) * width
    if isinstance(position, int):
        return home if position >= rows * (width - 1) else (back if row % 2 else forth)
    return jnp.where(position >= rows * (width - 1), home, jnp.where(row % 2 == 1, back, forth))


def position_of(place, count):
    width = ring_width(count)
    if width == 1:
        return place
    rows = count // width
    row, column = place // width, place % width
    snake = row * (width - 1) + jnp.where(row % 2 == 1, width - 1 - column, column - 1)
    return jnp.where(column == 0, rows * (width - 1) + rows - 1 - row, snake)


def load_kernel(count, win_keys, win_values, cache_keys, cache_values, q_hbm, valid_hbm, first_hbm, *refs):
    keys, values, q_ref, limits, valid_ref, first_ref, sems = refs
    window_rows = win_keys.shape[0]
    pairs = [
        (valid_hbm, valid_ref),
        (first_hbm, first_ref),
        (q_hbm, q_ref),
        (win_keys, keys.at[:window_rows]),
        (cache_keys, keys.at[window_rows:]),
        (win_values, values.at[:window_rows]),
        (cache_values, values.at[window_rows:]),
    ]
    copies = [pltpu.make_async_copy(*pair, sems.at[index]) for index, pair in enumerate(pairs)]
    for copy in copies:
        copy.start()
    for copy in copies[:2]:
        copy.wait()
    me = lax.axis_index("ctx")
    position = position_of(me, count)
    first = first_ref[me]
    for row, offset in enumerate(ring_offsets(count)):
        place = place_at(lax.rem(position + offset + count, count), count)
        limit = jnp.where((place >= first) & (place <= me), valid_ref[place], 0)
        limits[row : row + 1, :] = jnp.full((1, HD), limit, jnp.int32)
    limits[count - 1 : count, :] = jnp.full((1, HD), valid_ref[me], jnp.int32)
    for copy in copies[2:]:
        copy.wait()


def load(count, win_keys, win_values, cache_keys, cache_values, queries, valid_counts, first_block):
    rows, width = win_keys.shape[0] + cache_keys.shape[0], win_keys.shape[1]
    return pl.pallas_call(
        functools.partial(load_kernel, count),
        out_shape=[
            jax.ShapeDtypeStruct((rows, width), win_keys.dtype),
            jax.ShapeDtypeStruct((rows, width), win_keys.dtype),
            jax.ShapeDtypeStruct(queries.shape, queries.dtype),
            jax.ShapeDtypeStruct((-(-count // 8) * 8, HD), jnp.int32),
        ],
        in_specs=[pl.BlockSpec(memory_space=pltpu.HBM)] * 7,
        out_specs=[pl.BlockSpec(memory_space=pltpu.VMEM)] * 4,
        scratch_shapes=[
            pltpu.SMEM(valid_counts.shape, jnp.int32),
            pltpu.SMEM(first_block.shape, jnp.int32),
            pltpu.SemaphoreType.DMA((7,)),
        ],
        compiler_params=pltpu.CompilerParams(vmem_limit_bytes=4 * 1024 * 1024),
        cost_estimate=pl.CostEstimate(flops=0, bytes_accessed=8 * rows * width, transcendentals=0),
        name="load",
    )(win_keys, win_values, cache_keys, cache_values, queries, valid_counts, first_block)


def ring_offsets(count):
    half = count // 2
    return [sign * step for step in range(1, half) for sign in (-1, 1)] + [half]


def place_window(index, limit_row, own, sizes, limits, key, value, keys, values):
    window_rows = sizes[0]
    if not own:
        row_iota = lax.broadcasted_iota(jnp.int32, (window_rows, HD), 0)
        shown = row_iota < limits[limit_row : limit_row + 1, :]
    at = slice(index * window_rows, (index + 1) * window_rows)
    for head in range(keys.shape[0]):
        lanes = slice(head * HD, (head + 1) * HD)
        win_key, win_value = key[:window_rows, lanes], value[:window_rows, lanes]
        if own:
            keys[head, at, :] = win_key
            values[head, at, :HD] = win_value
            values[head, at, HD:] = jnp.ones((window_rows, HD), jnp.bfloat16)
        else:
            fill = key[window_rows : window_rows + 1, lanes].astype(jnp.float32)
            keys[head, at, :] = jnp.where(shown, win_key.astype(jnp.float32), fill).astype(jnp.bfloat16)
            values[head, at, :HD] = jnp.where(shown, win_value.astype(jnp.float32), 0.0).astype(jnp.bfloat16)
            values[head, at, HD:] = jnp.where(shown, 1.0, 0.0).astype(jnp.bfloat16)


def place_cache(index, number, sizes, key, value, keys, values):
    window_rows, cache_rows = sizes
    start = number * window_rows + index * cache_rows
    at = slice(start, start + cache_rows)
    for head in range(keys.shape[0]):
        lanes = slice(head * HD, (head + 1) * HD)
        keys[head, at, :] = key[window_rows:, lanes]
        values[head, at, :HD] = value[window_rows:, lanes]
        values[head, at, HD:] = jnp.ones((cache_rows, HD), jnp.bfloat16)


def fill_up(filled, keys, values):
    spare = keys.shape[1] - filled
    if spare:
        for head in range(keys.shape[0]):
            row = keys[head, filled - 1 : filled, :].astype(jnp.float32)
            keys[head, filled:, :] = jnp.broadcast_to(row, (spare, HD)).astype(jnp.bfloat16)
            values[head, filled:, :] = jnp.zeros((spare, 2 * HD), jnp.bfloat16)


def scores(query, keys):
    return lax.dot_general(query, keys, (((1,), (1,)), ((), ())), preferred_element_type=jnp.float32)


def weigh(score, top, values):
    lanes = score.shape[1] // HD
    weight = jnp.exp2(score * EXP_SCALE - jnp.concatenate([top] * lanes, axis=1)).astype(jnp.bfloat16)
    return jnp.dot(weight, values, preferred_element_type=jnp.float32)


def wide_top(score):
    return jnp.broadcast_to(jnp.max(score, axis=1, keepdims=True) * EXP_SCALE, (score.shape[0], HD))


def normalised(acc):
    total = acc[:, HD:]
    inverse = pl.reciprocal(total, approx=True)
    return (acc[:, :HD] * (inverse * (2.0 - total * inverse))).astype(jnp.bfloat16)


def chunks(q_ref, kv_heads, size):
    rows = q_ref.shape[0]
    group = q_ref.shape[1] // HD // kv_heads
    for head in range(kv_heads):
        for start in range(0, group, size):
            base = head * group + start
            query = jnp.concatenate(
                [q_ref[:, (base + i) * HD : (base + i + 1) * HD] for i in range(size)], axis=0
            )
            yield head, slice(base * rows, (base + size) * rows), query, base


def first_kernel(count, sizes, q_ref, limits, own_keys, own_values, acc_out, top_out, keys, values):
    window_rows = sizes[0]
    place_window(0, 0, True, sizes, None, own_keys, own_values, keys, values)
    place_cache(0, 1, sizes, own_keys, own_values, keys, values)
    fill_up(sum(sizes), keys, values)
    rows = q_ref.shape[0]
    key_iota = lax.broadcasted_iota(jnp.int32, (rows, window_rows), 1)
    query_iota = lax.broadcasted_iota(jnp.int32, (rows, window_rows), 0)
    seen = (key_iota <= query_iota) & (key_iota < limits[count - 1 : count, :])
    bias = jnp.concatenate([jnp.where(seen, 0.0, HIDDEN)] * CHUNK_HEADS, axis=0)
    for head, at, query, _ in chunks(q_ref, keys.shape[0], CHUNK_HEADS):
        score = scores(query, keys[head])
        score = jnp.concatenate([score[:, :window_rows] + bias, score[:, window_rows:]], axis=1)
        top = wide_top(score)
        acc_out[at, :] = weigh(score, top, values[head])
        top_out[at, :] = top


def next_kernel(rows_of, last, count, sizes, q_ref, limits, *refs):
    number = len(rows_of)
    key_refs, value_refs = refs[: 2 * number : 2], refs[1 : 2 * number : 2]
    if last:
        acc_in, top_in, out, keys, values, result, sems = refs[2 * number :]
    else:
        acc_in, top_in, acc_out, top_out, keys, values = refs[2 * number :]
    rows, heads = q_ref.shape[0], q_ref.shape[1] // HD
    kv_heads = keys.shape[0]
    size = LAST_CHUNK_HEADS if last else CHUNK_HEADS

    def sent(base):
        lanes = slice(base * HD, (base + size) * HD)
        return pltpu.make_async_copy(result.at[:, lanes], out.at[:, lanes], sems.at[base // size])

    def settle(base, acc):
        done = normalised(acc)
        for i in range(size):
            result[:, (base + i) * HD : (base + i + 1) * HD] = done[i * rows : (i + 1) * rows]
        sent(base).start()

    def take_in(begin):
        fine = jnp.ones((8, HD), jnp.float32)
        for head, at, query, base in chunks(q_ref, kv_heads, size):
            top = top_in[at, :]
            acc = acc_in[at, :] + weigh(scores(query, keys[head, begin:]), top, values[head, begin:])
            safe = jnp.where(acc[:, HD:] < LARGEST_TOTAL, 1.0, 0.0).reshape(-1, 8, HD)
            fine = jnp.minimum(fine, jnp.min(safe, axis=0))
            if last:
                settle(base, acc)
            else:
                acc_out[at, :] = acc
                top_out[at, :] = top
        if last:
            for base in range(0, heads, size):
                sent(base).wait()

        @pl.when(jnp.min(fine) < 0.5)
        def _():
            for head, at, query, base in chunks(q_ref, kv_heads, size):
                score = scores(query, keys[head, begin:])
                before = top_in[at, :]
                top = jnp.maximum(before, wide_top(score))
                fade = jnp.exp2(before - top)
                acc = acc_in[at, :] * jnp.concatenate([fade, fade], axis=1)
                acc = acc + weigh(score, top, values[head, begin:])
                if last:
                    settle(base, acc)
                    sent(base).wait()
                else:
                    acc_out[at, :] = acc
                    top_out[at, :] = top

    for index in range(number):
        place_cache(index, number, sizes, key_refs[index], value_refs[index], keys, values)
    fill_up(number * sum(sizes), keys, values)
    me = lax.axis_index("ctx")
    position = position_of(me, count)
    offsets = ring_offsets(count)
    places = [place_at(lax.rem(position + offsets[row] + count, count), count) for row in rows_of]
    earlier = functools.reduce(jnp.logical_or, [place < me for place in places])

    @pl.when(earlier)
    def _():
        for index, row in enumerate(rows_of):
            place_window(index, row, False, sizes, limits, key_refs[index], value_refs[index], keys, values)
        take_in(0)

    @pl.when(jnp.logical_not(earlier))
    def _():
        take_in(number * sizes[0])


def kernel_options(queries, total_keys, kv_heads):
    rows, width = queries.shape
    return {
        "compiler_params": pltpu.CompilerParams(vmem_limit_bytes=40 * 1024 * 1024),
        "cost_estimate": pl.CostEstimate(
            flops=6 * rows * width * total_keys,
            bytes_accessed=2 * rows * width,
            transcendentals=rows * (width // HD) * total_keys,
        ),
    }


def room(kv_heads, total_keys):
    return [
        pltpu.VMEM((kv_heads, total_keys, HD), jnp.bfloat16),
        pltpu.VMEM((kv_heads, total_keys, 2 * HD), jnp.bfloat16),
    ]


def state_shapes(queries):
    rows = queries.shape[0] * queries.shape[1] // HD
    return [jax.ShapeDtypeStruct((rows, 2 * HD), jnp.float32), jax.ShapeDtypeStruct((rows, HD), jnp.float32)]


def attend_first(count, sizes, queries, limits, own_keys, own_values):
    kv_heads = own_keys.shape[1] // HD
    total_keys = -(-sum(sizes) // HD) * HD
    vmem = pl.BlockSpec(memory_space=pltpu.VMEM)
    return tuple(
        pl.pallas_call(
            functools.partial(first_kernel, count, sizes),
            out_shape=state_shapes(queries),
            in_specs=[vmem] * 4,
            out_specs=[vmem] * 2,
            scratch_shapes=room(kv_heads, total_keys),
            name="attend_first",
            **kernel_options(queries, total_keys, kv_heads),
        )(queries, limits, own_keys, own_values)
    )


def attend_next(pieces, state, last, count, sizes, queries, limits):
    rows_of = tuple(piece[0] for piece in pieces)
    blocks = [block for piece in pieces for block in piece[1:]]
    kv_heads = blocks[0].shape[1] // HD
    total_keys = -(-len(pieces) * sum(sizes) // HD) * HD
    vmem = pl.BlockSpec(memory_space=pltpu.VMEM)
    operands = [queries, limits, *blocks, *state]
    shapes = [jax.ShapeDtypeStruct(queries.shape, queries.dtype)] if last else state_shapes(queries)
    scratch = room(kv_heads, total_keys)
    if last:
        chunk_count = queries.shape[1] // HD // LAST_CHUNK_HEADS
        scratch += [pltpu.VMEM(queries.shape, queries.dtype), pltpu.SemaphoreType.DMA((chunk_count,))]
    outs = pl.pallas_call(
        functools.partial(next_kernel, rows_of, last, count, sizes),
        out_shape=shapes,
        in_specs=[vmem] * len(operands),
        out_specs=[pl.BlockSpec(memory_space=pltpu.HBM)] if last else [vmem] * len(shapes),
        scratch_shapes=scratch,
        name="attend_last" if last else "attend_next",
        **kernel_options(queries, total_keys, kv_heads),
    )(*operands)
    return outs[0] if last else tuple(outs)


def shards(count, queries, win_keys, win_values, cache_keys, cache_values, valid_counts, first_block):
    sizes = (win_keys.shape[0], cache_keys.shape[0])
    half = count // 2
    ring = [place_at(p, count) for p in range(count)]
    onward = [(ring[p], ring[(p + 1) % count]) for p in range(count)]
    backward = [(b, a) for a, b in onward]

    win_keys, win_values, cache_keys, cache_values, valid_counts, first_block, queries = [
        pltpu.with_memory_space_constraint(x, pltpu.HBM)
        for x in (win_keys, win_values, cache_keys, cache_values, valid_counts, first_block, queries)
    ]
    own_keys, own_values, near, limits = load(
        count, win_keys, win_values, cache_keys, cache_values, queries, valid_counts, first_block
    )
    key_on = key_back = own_keys
    value_on = value_back = own_values
    state = attend_first(count, sizes, near, limits, own_keys, own_values)
    arrived = []
    for step in range(1, half + 1):
        key_on = lax.ppermute(key_on, "ctx", onward)
        value_back = lax.ppermute(value_back, "ctx", backward)
        if step < half:
            value_on = lax.ppermute(value_on, "ctx", onward)
            key_back = lax.ppermute(key_back, "ctx", backward)
            row = 2 * (step - 1)
            arrived.append([(row, key_on, value_on), (row + 1, key_back, value_back)])
        else:
            arrived.append([(2 * (half - 1), key_on, value_back)])
        if step == 1:
            key_on, top = lax.optimization_barrier((key_on, state[1]))
            state = (state[0], top)
    for begin in range(0, half - 2, 2):
        pieces = [piece for step in arrived[begin : min(begin + 2, half - 2)] for piece in step]
        state = attend_next(pieces, state, False, count, sizes, near, limits)
    state = attend_next(arrived[half - 2], state, False, count, sizes, near, limits)
    return attend_next(arrived[half - 1], state, True, count, sizes, near, limits)


def solution(mesh):
    in_specs = (
        P(("groups", "ctx"), "tp"),
        P(("groups", "ctx"), "tp"),
        P(("groups", "ctx"), "tp"),
        P(("groups", "ctx"), "tp"),
        P(("groups", "ctx"), "tp"),
        P("groups"),
        P("groups"),
    )
    out_specs = P(("groups", "ctx"), "tp")
    return jax.shard_map(
        functools.partial(shards, mesh.shape["ctx"]),
        mesh=mesh,
        in_specs=in_specs,
        out_specs=out_specs,
        check_vma=False,
    )
```

```python
import functools
import math

import jax
import jax.numpy as jnp
from jax import lax
from jax.experimental import pallas as pl
from jax.experimental.pallas import tpu as pltpu
from jax.sharding import PartitionSpec as P

HD = 128
EXP_SCALE = HD**-0.5 * math.log2(math.e)
HIDDEN = -1.0e30
CHUNK_HEADS = 8
LAST_CHUNK_HEADS = 4
LARGEST_TOTAL = 2.0**100


def ring_width(count):
    width = round(count ** (1 / 3))
    if width > 1 and count % width == 0 and (count // width) % 2 == 0:
        return width
    return 1


def place_at(position, count):
    width = ring_width(count)
    if width == 1:
        return position
    rows = count // width
    row, step = position // (width - 1), position % (width - 1)
    forth = row * width + 1 + step
    back = row * width + width - 1 - step
    home = (rows - 1 - (position - rows * (width - 1))) * width
    if isinstance(position, int):
        return home if position >= rows * (width - 1) else (back if row % 2 else forth)
    return jnp.where(position >= rows * (width - 1), home, jnp.where(row % 2 == 1, back, forth))


def position_of(place, count):
    width = ring_width(count)
    if width == 1:
        return place
    rows = count // width
    row, column = place // width, place % width
    snake = row * (width - 1) + jnp.where(row % 2 == 1, width - 1 - column, column - 1)
    return jnp.where(column == 0, rows * (width - 1) + rows - 1 - row, snake)


def turn():
    return 1 - 2 * lax.rem(lax.axis_index("tp"), 2)


def load_kernel(count, win_keys, win_values, cache_keys, cache_values, q_hbm, valid_hbm, first_hbm, *refs):
    keys, values, q_ref, limits, acc_out, top_out, key_room, value_room, valid_ref, first_ref, sems = refs
    window_rows = win_keys.shape[0]
    pairs = [
        (valid_hbm, valid_ref),
        (first_hbm, first_ref),
        (q_hbm, q_ref),
        (win_keys, keys.at[:window_rows]),
        (cache_keys, keys.at[window_rows:]),
        (win_values, values.at[:window_rows]),
        (cache_values, values.at[window_rows:]),
    ]
    copies = [pltpu.make_async_copy(*pair, sems.at[index]) for index, pair in enumerate(pairs)]
    for copy in copies:
        copy.start()
    for copy in copies[:2]:
        copy.wait()
    me = lax.axis_index("ctx")
    position = position_of(me, count)
    first = first_ref[me]
    for row, offset in enumerate(ring_offsets(count)):
        place = place_at(lax.rem(position + turn() * offset + count, count), count)
        limit = jnp.where((place >= first) & (place <= me), valid_ref[place], 0)
        limits[row : row + 1, :] = jnp.full((1, HD), limit, jnp.int32)
    limits[count - 1 : count, :] = jnp.full((1, HD), valid_ref[me], jnp.int32)
    for copy in copies[2:]:
        copy.wait()

    @pl.when(turn() < 0)
    def _():
        sizes = (window_rows, cache_keys.shape[0])
        take_own(count, sizes, q_ref, limits, keys, values, acc_out, top_out, key_room, value_room)


def load(count, win_keys, win_values, cache_keys, cache_values, queries, valid_counts, first_block):
    rows, width = win_keys.shape[0] + cache_keys.shape[0], win_keys.shape[1]
    return pl.pallas_call(
        functools.partial(load_kernel, count),
        out_shape=[
            jax.ShapeDtypeStruct((rows, width), win_keys.dtype),
            jax.ShapeDtypeStruct((rows, width), win_keys.dtype),
            jax.ShapeDtypeStruct(queries.shape, queries.dtype),
            jax.ShapeDtypeStruct((-(-count // 8) * 8, HD), jnp.int32),
            *state_shapes(queries),
        ],
        in_specs=[pl.BlockSpec(memory_space=pltpu.HBM)] * 7,
        out_specs=[pl.BlockSpec(memory_space=pltpu.VMEM)] * 6,
        scratch_shapes=[
            *room(width // HD, -(-rows // HD) * HD),
            pltpu.SMEM(valid_counts.shape, jnp.int32),
            pltpu.SMEM(first_block.shape, jnp.int32),
            pltpu.SemaphoreType.DMA((7,)),
        ],
        compiler_params=pltpu.CompilerParams(vmem_limit_bytes=24 * 1024 * 1024),
        cost_estimate=pl.CostEstimate(flops=0, bytes_accessed=8 * rows * width, transcendentals=0),
        name="load",
    )(win_keys, win_values, cache_keys, cache_values, queries, valid_counts, first_block)


def ring_offsets(count):
    half = count // 2
    return [sign * step for step in range(1, half) for sign in (-1, 1)] + [half]


def place_window(index, limit_row, own, sizes, limits, key, value, keys, values):
    window_rows = sizes[0]
    if not own:
        row_iota = lax.broadcasted_iota(jnp.int32, (window_rows, HD), 0)
        shown = row_iota < limits[limit_row : limit_row + 1, :]
    at = slice(index * window_rows, (index + 1) * window_rows)
    for head in range(keys.shape[0]):
        lanes = slice(head * HD, (head + 1) * HD)
        win_key, win_value = key[:window_rows, lanes], value[:window_rows, lanes]
        if own:
            keys[head, at, :] = win_key
            values[head, at, :HD] = win_value
            values[head, at, HD:] = jnp.ones((window_rows, HD), jnp.bfloat16)
        else:
            fill = key[window_rows : window_rows + 1, lanes].astype(jnp.float32)
            keys[head, at, :] = jnp.where(shown, win_key.astype(jnp.float32), fill).astype(jnp.bfloat16)
            values[head, at, :HD] = jnp.where(shown, win_value.astype(jnp.float32), 0.0).astype(jnp.bfloat16)
            values[head, at, HD:] = jnp.where(shown, 1.0, 0.0).astype(jnp.bfloat16)


def place_cache(index, number, sizes, key, value, keys, values):
    window_rows, cache_rows = sizes
    start = number * window_rows + index * cache_rows
    at = slice(start, start + cache_rows)
    for head in range(keys.shape[0]):
        lanes = slice(head * HD, (head + 1) * HD)
        keys[head, at, :] = key[window_rows:, lanes]
        values[head, at, :HD] = value[window_rows:, lanes]
        values[head, at, HD:] = jnp.ones((cache_rows, HD), jnp.bfloat16)


def fill_up(filled, keys, values):
    spare = keys.shape[1] - filled
    if spare:
        for head in range(keys.shape[0]):
            row = keys[head, filled - 1 : filled, :].astype(jnp.float32)
            keys[head, filled:, :] = jnp.broadcast_to(row, (spare, HD)).astype(jnp.bfloat16)
            values[head, filled:, :] = jnp.zeros((spare, 2 * HD), jnp.bfloat16)


def scores(query, keys):
    return lax.dot_general(query, keys, (((1,), (1,)), ((), ())), preferred_element_type=jnp.float32)


def weigh(score, top, values):
    lanes = score.shape[1] // HD
    weight = jnp.exp2(score * EXP_SCALE - jnp.concatenate([top] * lanes, axis=1)).astype(jnp.bfloat16)
    return jnp.dot(weight, values, preferred_element_type=jnp.float32)


def wide_top(score):
    return jnp.broadcast_to(jnp.max(score, axis=1, keepdims=True) * EXP_SCALE, (score.shape[0], HD))


def normalised(acc):
    total = acc[:, HD:]
    inverse = pl.reciprocal(total, approx=True)
    return (acc[:, :HD] * (inverse * (2.0 - total * inverse))).astype(jnp.bfloat16)


def chunks(q_ref, kv_heads, size):
    rows = q_ref.shape[0]
    group = q_ref.shape[1] // HD // kv_heads
    for head in range(kv_heads):
        for start in range(0, group, size):
            base = head * group + start
            query = jnp.concatenate(
                [q_ref[:, (base + i) * HD : (base + i + 1) * HD] for i in range(size)], axis=0
            )
            yield head, slice(base * rows, (base + size) * rows), query, base


def take_own(count, sizes, q_ref, limits, own_keys, own_values, acc_out, top_out, keys, values):
    window_rows = sizes[0]
    place_window(0, 0, True, sizes, None, own_keys, own_values, keys, values)
    place_cache(0, 1, sizes, own_keys, own_values, keys, values)
    fill_up(sum(sizes), keys, values)
    rows = q_ref.shape[0]
    key_iota = lax.broadcasted_iota(jnp.int32, (rows, window_rows), 1)
    query_iota = lax.broadcasted_iota(jnp.int32, (rows, window_rows), 0)
    seen = (key_iota <= query_iota) & (key_iota < limits[count - 1 : count, :])
    bias = jnp.concatenate([jnp.where(seen, 0.0, HIDDEN)] * CHUNK_HEADS, axis=0)
    for head, at, query, _ in chunks(q_ref, keys.shape[0], CHUNK_HEADS):
        score = scores(query, keys[head])
        score = jnp.concatenate([score[:, :window_rows] + bias, score[:, window_rows:]], axis=1)
        top = wide_top(score)
        acc_out[at, :] = weigh(score, top, values[head])
        top_out[at, :] = top


def first_kernel(count, sizes, q_ref, limits, own_keys, own_values, acc_in, top_in, acc_out, top_out, keys, values):
    @pl.when(turn() > 0)
    def _():
        take_own(count, sizes, q_ref, limits, own_keys, own_values, acc_out, top_out, keys, values)

    @pl.when(turn() < 0)
    def _():
        acc_out[...] = acc_in[...]
        top_out[...] = top_in[...]


def next_kernel(rows_of, last, count, sizes, q_ref, limits, *refs):
    number = len(rows_of)
    key_refs, value_refs = refs[: 2 * number : 2], refs[1 : 2 * number : 2]
    if last:
        acc_in, top_in, out, keys, values, result, sems = refs[2 * number :]
    else:
        acc_in, top_in, acc_out, top_out, keys, values = refs[2 * number :]
    rows, heads = q_ref.shape[0], q_ref.shape[1] // HD
    kv_heads = keys.shape[0]
    size = LAST_CHUNK_HEADS if last else CHUNK_HEADS

    def sent(base):
        lanes = slice(base * HD, (base + size) * HD)
        return pltpu.make_async_copy(result.at[:, lanes], out.at[:, lanes], sems.at[base // size])

    def settle(base, acc):
        done = normalised(acc)
        for i in range(size):
            result[:, (base + i) * HD : (base + i + 1) * HD] = done[i * rows : (i + 1) * rows]
        sent(base).start()

    def take_in(begin):
        fine = jnp.ones((8, HD), jnp.float32)
        for head, at, query, base in chunks(q_ref, kv_heads, size):
            top = top_in[at, :]
            acc = acc_in[at, :] + weigh(scores(query, keys[head, begin:]), top, values[head, begin:])
            safe = jnp.where(acc[:, HD:] < LARGEST_TOTAL, 1.0, 0.0).reshape(-1, 8, HD)
            fine = jnp.minimum(fine, jnp.min(safe, axis=0))
            if last:
                settle(base, acc)
            else:
                acc_out[at, :] = acc
                top_out[at, :] = top
        if last:
            for base in range(0, heads, size):
                sent(base).wait()

        @pl.when(jnp.min(fine) < 0.5)
        def _():
            for head, at, query, base in chunks(q_ref, kv_heads, size):
                score = scores(query, keys[head, begin:])
                before = top_in[at, :]
                top = jnp.maximum(before, wide_top(score))
                fade = jnp.exp2(before - top)
                acc = acc_in[at, :] * jnp.concatenate([fade, fade], axis=1)
                acc = acc + weigh(score, top, values[head, begin:])
                if last:
                    settle(base, acc)
                    sent(base).wait()
                else:
                    acc_out[at, :] = acc
                    top_out[at, :] = top

    for index in range(number):
        place_cache(index, number, sizes, key_refs[index], value_refs[index], keys, values)
    fill_up(number * sum(sizes), keys, values)
    me = lax.axis_index("ctx")
    position = position_of(me, count)
    offsets = ring_offsets(count)
    places = [place_at(lax.rem(position + turn() * offsets[row] + count, count), count) for row in rows_of]
    earlier = functools.reduce(jnp.logical_or, [place < me for place in places])

    @pl.when(earlier)
    def _():
        for index, row in enumerate(rows_of):
            place_window(index, row, False, sizes, limits, key_refs[index], value_refs[index], keys, values)
        take_in(0)

    @pl.when(jnp.logical_not(earlier))
    def _():
        take_in(number * sizes[0])


def kernel_options(queries, total_keys, kv_heads):
    rows, width = queries.shape
    return {
        "compiler_params": pltpu.CompilerParams(vmem_limit_bytes=40 * 1024 * 1024),
        "cost_estimate": pl.CostEstimate(
            flops=6 * rows * width * total_keys,
            bytes_accessed=2 * rows * width,
            transcendentals=rows * (width // HD) * total_keys,
        ),
    }


def room(kv_heads, total_keys):
    return [
        pltpu.VMEM((kv_heads, total_keys, HD), jnp.bfloat16),
        pltpu.VMEM((kv_heads, total_keys, 2 * HD), jnp.bfloat16),
    ]


def state_shapes(queries):
    rows = queries.shape[0] * queries.shape[1] // HD
    return [jax.ShapeDtypeStruct((rows, 2 * HD), jnp.float32), jax.ShapeDtypeStruct((rows, HD), jnp.float32)]


def attend_first(count, sizes, queries, limits, own_keys, own_values, state):
    kv_heads = own_keys.shape[1] // HD
    total_keys = -(-sum(sizes) // HD) * HD
    vmem = pl.BlockSpec(memory_space=pltpu.VMEM)
    return tuple(
        pl.pallas_call(
            functools.partial(first_kernel, count, sizes),
            out_shape=state_shapes(queries),
            in_specs=[vmem] * 6,
            out_specs=[vmem] * 2,
            scratch_shapes=room(kv_heads, total_keys),
            name="attend_first",
            **kernel_options(queries, total_keys, kv_heads),
        )(queries, limits, own_keys, own_values, *state)
    )


def attend_next(pieces, state, last, count, sizes, queries, limits):
    rows_of = tuple(piece[0] for piece in pieces)
    blocks = [block for piece in pieces for block in piece[1:]]
    kv_heads = blocks[0].shape[1] // HD
    total_keys = -(-len(pieces) * sum(sizes) // HD) * HD
    vmem = pl.BlockSpec(memory_space=pltpu.VMEM)
    operands = [queries, limits, *blocks, *state]
    shapes = [jax.ShapeDtypeStruct(queries.shape, queries.dtype)] if last else state_shapes(queries)
    scratch = room(kv_heads, total_keys)
    if last:
        chunk_count = queries.shape[1] // HD // LAST_CHUNK_HEADS
        scratch += [pltpu.VMEM(queries.shape, queries.dtype), pltpu.SemaphoreType.DMA((chunk_count,))]
    outs = pl.pallas_call(
        functools.partial(next_kernel, rows_of, last, count, sizes),
        out_shape=shapes,
        in_specs=[vmem] * len(operands),
        out_specs=[pl.BlockSpec(memory_space=pltpu.HBM)] if last else [vmem] * len(shapes),
        scratch_shapes=scratch,
        name="attend_last" if last else "attend_next",
        **kernel_options(queries, total_keys, kv_heads),
    )(*operands)
    return outs[0] if last else tuple(outs)


def ring_pairs(count, cores, step):
    ring = [place_at(p, count) for p in range(count)]
    pairs = []
    for core in range(cores):
        way = -step if core % 2 else step
        pairs += [(ring[p] * cores + core, ring[(p + way) % count] * cores + core) for p in range(count)]
    return pairs


def shards(count, cores, queries, win_keys, win_values, cache_keys, cache_values, valid_counts, first_block):
    sizes = (win_keys.shape[0], cache_keys.shape[0])
    half = count // 2
    onward = functools.partial(lax.ppermute, axis_name=("ctx", "tp"), perm=ring_pairs(count, cores, 1))
    backward = functools.partial(lax.ppermute, axis_name=("ctx", "tp"), perm=ring_pairs(count, cores, -1))

    win_keys, win_values, cache_keys, cache_values, valid_counts, first_block, queries = [
        pltpu.with_memory_space_constraint(x, pltpu.HBM)
        for x in (win_keys, win_values, cache_keys, cache_values, valid_counts, first_block, queries)
    ]
    own_keys, own_values, near, limits, *state = load(
        count, win_keys, win_values, cache_keys, cache_values, queries, valid_counts, first_block
    )
    key_on = key_back = own_keys
    value_on = value_back = own_values
    state = attend_first(count, sizes, near, limits, own_keys, own_values, state)
    arrived = []
    for step in range(1, half + 1):
        key_on = onward(key_on)
        value_back = backward(value_back)
        if step < half:
            value_on = onward(value_on)
            key_back = backward(key_back)
            row = 2 * (step - 1)
            arrived.append([(row, key_on, value_on), (row + 1, key_back, value_back)])
        else:
            arrived.append([(2 * (half - 1), key_on, value_back)])
        if step == 1:
            key_on, top = lax.optimization_barrier((key_on, state[1]))
            state = (state[0], top)
    for begin in range(0, half - 2, 2):
        pieces = [piece for step in arrived[begin : min(begin + 2, half - 2)] for piece in step]
        state = attend_next(pieces, state, False, count, sizes, near, limits)
    state = attend_next(arrived[half - 2], state, False, count, sizes, near, limits)
    return attend_next(arrived[half - 1], state, True, count, sizes, near, limits)


def solution(mesh):
    in_specs = (
        P(("groups", "ctx"), "tp"),
        P(("groups", "ctx"), "tp"),
        P(("groups", "ctx"), "tp"),
        P(("groups", "ctx"), "tp"),
        P(("groups", "ctx"), "tp"),
        P("groups"),
        P("groups"),
    )
    out_specs = P(("groups", "ctx"), "tp")
    return jax.shard_map(
        functools.partial(shards, mesh.shape["ctx"], mesh.shape["tp"]),
        mesh=mesh,
        in_specs=in_specs,
        out_specs=out_specs,
        check_vma=False,
    )
```

```python
import functools
import math

import jax
import jax.numpy as jnp
from jax import lax
from jax.experimental import pallas as pl
from jax.experimental.pallas import tpu as pltpu
from jax.sharding import PartitionSpec as P

HD = 128
EXP_SCALE = HD**-0.5 * math.log2(math.e)
HIDDEN = -1.0e30
CHUNK_HEADS = 4
COPY_HEADS = 2
LARGEST_TOTAL = 2.0**100


def ring_width(count):
    width = round(count ** (1 / 3))
    if width > 1 and count % width == 0 and (count // width) % 2 == 0:
        return width
    return 1


def place_at(position, count):
    width = ring_width(count)
    if width == 1:
        return position
    rows = count // width
    row, step = position // (width - 1), position % (width - 1)
    forth = row * width + 1 + step
    back = row * width + width - 1 - step
    home = (rows - 1 - (position - rows * (width - 1))) * width
    if isinstance(position, int):
        return home if position >= rows * (width - 1) else (back if row % 2 else forth)
    return jnp.where(position >= rows * (width - 1), home, jnp.where(row % 2 == 1, back, forth))


def position_of(place, count):
    width = ring_width(count)
    if width == 1:
        return place
    rows = count // width
    row, column = place // width, place % width
    snake = row * (width - 1) + jnp.where(row % 2 == 1, width - 1 - column, column - 1)
    return jnp.where(column == 0, rows * (width - 1) + rows - 1 - row, snake)


def load_kernel(count, win_keys, win_values, cache_keys, cache_values, q_hbm, valid_hbm, first_hbm, *refs):
    keys, values, q_ref, limits, valid_ref, first_ref, sems = refs
    window_rows = win_keys.shape[0]
    pairs = [
        (valid_hbm, valid_ref),
        (first_hbm, first_ref),
        (q_hbm, q_ref),
        (win_keys, keys.at[:window_rows]),
        (cache_keys, keys.at[window_rows:]),
        (win_values, values.at[:window_rows]),
        (cache_values, values.at[window_rows:]),
    ]
    copies = [pltpu.make_async_copy(*pair, sems.at[index]) for index, pair in enumerate(pairs)]
    for copy in copies:
        copy.start()
    for copy in copies[:2]:
        copy.wait()
    me = lax.axis_index("ctx")
    position = position_of(me, count)
    first = first_ref[me]
    for row, offset in enumerate(ring_offsets(count)):
        place = place_at(lax.rem(position + offset + count, count), count)
        limit = jnp.where((place >= first) & (place <= me), valid_ref[place], 0)
        limits[row : row + 1, :] = jnp.full((1, HD), limit, jnp.int32)
    limits[count - 1 : count, :] = jnp.full((1, HD), valid_ref[me], jnp.int32)
    for copy in copies[2:]:
        copy.wait()


def load(count, win_keys, win_values, cache_keys, cache_values, queries, valid_counts, first_block):
    rows, width = win_keys.shape[0] + cache_keys.shape[0], win_keys.shape[1]
    return pl.pallas_call(
        functools.partial(load_kernel, count),
        out_shape=[
            jax.ShapeDtypeStruct((rows, width), win_keys.dtype),
            jax.ShapeDtypeStruct((rows, width), win_keys.dtype),
            jax.ShapeDtypeStruct(queries.shape, queries.dtype),
            jax.ShapeDtypeStruct((-(-count // 8) * 8, HD), jnp.int32),
        ],
        in_specs=[pl.BlockSpec(memory_space=pltpu.HBM)] * 7,
        out_specs=[pl.BlockSpec(memory_space=pltpu.VMEM)] * 4,
        scratch_shapes=[
            pltpu.SMEM(valid_counts.shape, jnp.int32),
            pltpu.SMEM(first_block.shape, jnp.int32),
            pltpu.SemaphoreType.DMA((7,)),
        ],
        compiler_params=pltpu.CompilerParams(vmem_limit_bytes=4 * 1024 * 1024),
        cost_estimate=pl.CostEstimate(flops=0, bytes_accessed=8 * rows * width, transcendentals=0),
        name="load",
    )(win_keys, win_values, cache_keys, cache_values, queries, valid_counts, first_block)


def ring_offsets(count):
    half = count // 2
    return [sign * step for step in range(1, half) for sign in (-1, 1)] + [half]


def place_window(index, limit_row, own, sizes, limits, key, value, keys, values):
    window_rows = sizes[0]
    if not own:
        row_iota = lax.broadcasted_iota(jnp.int32, (window_rows, HD), 0)
        shown = row_iota < limits[limit_row : limit_row + 1, :]
    at = slice(index * window_rows, (index + 1) * window_rows)
    for head in range(keys.shape[0]):
        lanes = slice(head * HD, (head + 1) * HD)
        win_key, win_value = key[:window_rows, lanes], value[:window_rows, lanes]
        if own:
            keys[head, at, :] = win_key
            values[head, at, :HD] = win_value
            values[head, at, HD:] = jnp.ones((window_rows, HD), jnp.bfloat16)
        else:
            fill = key[window_rows : window_rows + 1, lanes].astype(jnp.float32)
            keys[head, at, :] = jnp.where(shown, win_key.astype(jnp.float32), fill).astype(jnp.bfloat16)
            values[head, at, :HD] = jnp.where(shown, win_value.astype(jnp.float32), 0.0).astype(jnp.bfloat16)
            values[head, at, HD:] = jnp.where(shown, 1.0, 0.0).astype(jnp.bfloat16)


def place_cache(index, number, sizes, key, value, keys, values):
    window_rows, cache_rows = sizes
    start = number * window_rows + index * cache_rows
    at = slice(start, start + cache_rows)
    for head in range(keys.shape[0]):
        lanes = slice(head * HD, (head + 1) * HD)
        keys[head, at, :] = key[window_rows:, lanes]
        values[head, at, :HD] = value[window_rows:, lanes]
        values[head, at, HD:] = jnp.ones((cache_rows, HD), jnp.bfloat16)


def fill_up(filled, keys, values):
    spare = keys.shape[1] - filled
    if spare:
        for head in range(keys.shape[0]):
            row = keys[head, filled - 1 : filled, :].astype(jnp.float32)
            keys[head, filled:, :] = jnp.broadcast_to(row, (spare, HD)).astype(jnp.bfloat16)
            values[head, filled:, :] = jnp.zeros((spare, 2 * HD), jnp.bfloat16)


def scores(query, keys):
    return lax.dot_general(query, keys, (((1,), (1,)), ((), ())), preferred_element_type=jnp.float32)


def weigh(score, top, values):
    lanes = score.shape[1] // HD
    weight = jnp.exp2(score * EXP_SCALE - jnp.concatenate([top] * lanes, axis=1)).astype(jnp.bfloat16)
    return jnp.dot(weight, values, preferred_element_type=jnp.float32)


def wide_top(score):
    return jnp.broadcast_to(jnp.max(score, axis=1, keepdims=True) * EXP_SCALE, (score.shape[0], HD))


def normalised(acc):
    total = acc[:, HD:]
    inverse = pl.reciprocal(total, approx=True)
    return (acc[:, :HD] * (inverse * (2.0 - total * inverse))).astype(jnp.bfloat16)


def chunks(q_ref, kv_heads, fine_end=False):
    rows = q_ref.shape[0]
    group = q_ref.shape[1] // HD // kv_heads
    sizes = [CHUNK_HEADS] * (kv_heads * group // CHUNK_HEADS)
    if fine_end:
        sizes[-1:] = [CHUNK_HEADS // 2] * 2
    base = 0
    for size in sizes:
        query = jnp.concatenate([q_ref[:, (base + i) * HD : (base + i + 1) * HD] for i in range(size)], axis=0)
        yield base // group, slice(base * rows, (base + size) * rows), query, base, size
        base += size


def first_kernel(count, sizes, q_ref, limits, own_keys, own_values, acc_out, top_out, keys, values):
    window_rows = sizes[0]
    place_window(0, 0, True, sizes, None, own_keys, own_values, keys, values)
    place_cache(0, 1, sizes, own_keys, own_values, keys, values)
    fill_up(sum(sizes), keys, values)
    rows = q_ref.shape[0]
    key_iota = lax.broadcasted_iota(jnp.int32, (rows, window_rows), 1)
    query_iota = lax.broadcasted_iota(jnp.int32, (rows, window_rows), 0)
    seen = (key_iota <= query_iota) & (key_iota < limits[count - 1 : count, :])
    bias = jnp.concatenate([jnp.where(seen, 0.0, HIDDEN)] * CHUNK_HEADS, axis=0)
    for head, at, query, _, _ in chunks(q_ref, keys.shape[0]):
        score = scores(query, keys[head])
        score = jnp.concatenate([score[:, :window_rows] + bias, score[:, window_rows:]], axis=1)
        top = wide_top(score)
        acc_out[at, :] = weigh(score, top, values[head])
        top_out[at, :] = top


def next_kernel(rows_of, last, count, sizes, q_ref, limits, *refs):
    number = len(rows_of)
    key_refs, value_refs = refs[: 2 * number : 2], refs[1 : 2 * number : 2]
    if last:
        acc_in, top_in, out, keys, values, result, sems = refs[2 * number :]
    else:
        acc_in, top_in, acc_out, top_out, keys, values = refs[2 * number :]
    rows, heads = q_ref.shape[0], q_ref.shape[1] // HD
    kv_heads = keys.shape[0]

    def sent(base):
        lanes = slice(base * HD, (base + COPY_HEADS) * HD)
        return pltpu.make_async_copy(result.at[:, lanes], out.at[:, lanes], sems.at[base // COPY_HEADS])

    def settle(base, size, acc):
        done = normalised(acc)
        for i in range(size):
            result[:, (base + i) * HD : (base + i + 1) * HD] = done[i * rows : (i + 1) * rows]
        for i in range(0, size, COPY_HEADS):
            sent(base + i).start()

    def wait_all():
        for base in range(0, heads, COPY_HEADS):
            sent(base).wait()

    def take_in(begin):
        fine = jnp.ones((8, HD), jnp.float32)
        for head, at, query, base, size in chunks(q_ref, kv_heads, last):
            top = top_in[at, :]
            acc = acc_in[at, :] + weigh(scores(query, keys[head, begin:]), top, values[head, begin:])
            safe = jnp.where(acc[:, HD:] < LARGEST_TOTAL, 1.0, 0.0).reshape(-1, 8, HD)
            fine = jnp.minimum(fine, jnp.min(safe, axis=0))
            if last:
                settle(base, size, acc)
            else:
                acc_out[at, :] = acc
                top_out[at, :] = top
        again = jnp.min(fine) < 0.5
        if last:
            wait_all()

        @pl.when(again)
        def _():
            for head, at, query, base, size in chunks(q_ref, kv_heads, last):
                score = scores(query, keys[head, begin:])
                before = top_in[at, :]
                top = jnp.maximum(before, wide_top(score))
                fade = jnp.exp2(before - top)
                acc = acc_in[at, :] * jnp.concatenate([fade, fade], axis=1)
                acc = acc + weigh(score, top, values[head, begin:])
                if last:
                    settle(base, size, acc)
                else:
                    acc_out[at, :] = acc
                    top_out[at, :] = top
            if last:
                wait_all()

    for index in range(number):
        place_cache(index, number, sizes, key_refs[index], value_refs[index], keys, values)
    fill_up(number * sum(sizes), keys, values)
    if number < 4:
        for index, row in enumerate(rows_of):
            place_window(index, row, False, sizes, limits, key_refs[index], value_refs[index], keys, values)
        take_in(0)
        return
    me = lax.axis_index("ctx")
    position = position_of(me, count)
    offsets = ring_offsets(count)
    places = [place_at(lax.rem(position + offsets[row] + count, count), count) for row in rows_of]
    earlier = functools.reduce(jnp.logical_or, [place < me for place in places])

    @pl.when(earlier)
    def _():
        for index, row in enumerate(rows_of):
            place_window(index, row, False, sizes, limits, key_refs[index], value_refs[index], keys, values)
        take_in(0)

    @pl.when(jnp.logical_not(earlier))
    def _():
        take_in(number * sizes[0])


def kernel_options(queries, total_keys, kv_heads):
    rows, width = queries.shape
    return {
        "compiler_params": pltpu.CompilerParams(vmem_limit_bytes=40 * 1024 * 1024),
        "cost_estimate": pl.CostEstimate(
            flops=6 * rows * width * total_keys,
            bytes_accessed=2 * rows * width,
            transcendentals=rows * (width // HD) * total_keys,
        ),
    }


def room(kv_heads, total_keys):
    return [
        pltpu.VMEM((kv_heads, total_keys, HD), jnp.bfloat16),
        pltpu.VMEM((kv_heads, total_keys, 2 * HD), jnp.bfloat16),
    ]


def state_shapes(queries):
    rows = queries.shape[0] * queries.shape[1] // HD
    return [jax.ShapeDtypeStruct((rows, 2 * HD), jnp.float32), jax.ShapeDtypeStruct((rows, HD), jnp.float32)]


def attend_first(count, sizes, queries, limits, own_keys, own_values):
    kv_heads = own_keys.shape[1] // HD
    total_keys = -(-sum(sizes) // HD) * HD
    vmem = pl.BlockSpec(memory_space=pltpu.VMEM)
    return tuple(
        pl.pallas_call(
            functools.partial(first_kernel, count, sizes),
            out_shape=state_shapes(queries),
            in_specs=[vmem] * 4,
            out_specs=[vmem] * 2,
            scratch_shapes=room(kv_heads, total_keys),
            name="attend_first",
            **kernel_options(queries, total_keys, kv_heads),
        )(queries, limits, own_keys, own_values)
    )


def attend_next(pieces, state, last, count, sizes, queries, limits):
    rows_of = tuple(piece[0] for piece in pieces)
    blocks = [block for piece in pieces for block in piece[1:]]
    kv_heads = blocks[0].shape[1] // HD
    total_keys = -(-len(pieces) * sum(sizes) // HD) * HD
    vmem = pl.BlockSpec(memory_space=pltpu.VMEM)
    operands = [queries, limits, *blocks, *state]
    shapes = [jax.ShapeDtypeStruct(queries.shape, queries.dtype)] if last else state_shapes(queries)
    scratch = room(kv_heads, total_keys)
    if last:
        copies = queries.shape[1] // HD // COPY_HEADS
        scratch += [pltpu.VMEM(queries.shape, queries.dtype), pltpu.SemaphoreType.DMA((copies,))]
    outs = pl.pallas_call(
        functools.partial(next_kernel, rows_of, last, count, sizes),
        out_shape=shapes,
        in_specs=[vmem] * len(operands),
        out_specs=[pl.BlockSpec(memory_space=pltpu.HBM)] if last else [vmem] * len(shapes),
        scratch_shapes=scratch,
        name="attend_last" if last else "attend_next",
        **kernel_options(queries, total_keys, kv_heads),
    )(*operands)
    return outs[0] if last else tuple(outs)


def shards(count, queries, win_keys, win_values, cache_keys, cache_values, valid_counts, first_block):
    sizes = (win_keys.shape[0], cache_keys.shape[0])
    half = count // 2
    ring = [place_at(p, count) for p in range(count)]
    onward = [(ring[p], ring[(p + 1) % count]) for p in range(count)]
    backward = [(b, a) for a, b in onward]

    win_keys, win_values, cache_keys, cache_values, valid_counts, first_block, queries = [
        pltpu.with_memory_space_constraint(x, pltpu.HBM)
        for x in (win_keys, win_values, cache_keys, cache_values, valid_counts, first_block, queries)
    ]
    own_keys, own_values, near, limits = load(
        count, win_keys, win_values, cache_keys, cache_values, queries, valid_counts, first_block
    )
    key_on = key_back = own_keys
    value_on = value_back = own_values
    state = attend_first(count, sizes, near, limits, own_keys, own_values)
    arrived = []
    for step in range(1, half + 1):
        key_on = lax.ppermute(key_on, "ctx", onward)
        value_back = lax.ppermute(value_back, "ctx", backward)
        if step < half:
            value_on = lax.ppermute(value_on, "ctx", onward)
            key_back = lax.ppermute(key_back, "ctx", backward)
            row = 2 * (step - 1)
            arrived.append([(row, key_on, value_on), (row + 1, key_back, value_back)])
        else:
            arrived.append([(2 * (half - 1), key_on, value_back)])
        if step == 1:
            key_on, top = lax.optimization_barrier((key_on, state[1]))
            state = (state[0], top)
    for begin in range(0, half - 2, 2):
        pieces = [piece for step in arrived[begin : min(begin + 2, half - 2)] for piece in step]
        state = attend_next(pieces, state, False, count, sizes, near, limits)
    state = attend_next(arrived[half - 2], state, False, count, sizes, near, limits)
    return attend_next(arrived[half - 1], state, True, count, sizes, near, limits)


def solution(mesh):
    in_specs = (
        P(("groups", "ctx"), "tp"),
        P(("groups", "ctx"), "tp"),
        P(("groups", "ctx"), "tp"),
        P(("groups", "ctx"), "tp"),
        P(("groups", "ctx"), "tp"),
        P("groups"),
        P("groups"),
    )
    out_specs = P(("groups", "ctx"), "tp")
    return jax.shard_map(
        functools.partial(shards, mesh.shape["ctx"]),
        mesh=mesh,
        in_specs=in_specs,
        out_specs=out_specs,
        check_vma=False,
    )
```

```python
import functools
import math

import jax
import jax.numpy as jnp
from jax import lax
from jax.experimental import pallas as pl
from jax.experimental.pallas import tpu as pltpu
from jax.sharding import PartitionSpec as P

HD = 128
EXP_SCALE = HD**-0.5 * math.log2(math.e)
HIDDEN = -1.0e30
CHUNK_HEADS = 4
COPY_HEADS = 2
LARGEST_TOTAL = 2.0**100


def ring_width(count):
    width = round(count ** (1 / 3))
    if width > 1 and count % width == 0 and (count // width) % 2 == 0:
        return width
    return 1


def place_at(position, count):
    width = ring_width(count)
    if width == 1:
        return position
    rows = count // width
    row, step = position // (width - 1), position % (width - 1)
    forth = row * width + 1 + step
    back = row * width + width - 1 - step
    home = (rows - 1 - (position - rows * (width - 1))) * width
    if isinstance(position, int):
        return home if position >= rows * (width - 1) else (back if row % 2 else forth)
    return jnp.where(position >= rows * (width - 1), home, jnp.where(row % 2 == 1, back, forth))


def position_of(place, count):
    width = ring_width(count)
    if width == 1:
        return place
    rows = count // width
    row, column = place // width, place % width
    snake = row * (width - 1) + jnp.where(row % 2 == 1, width - 1 - column, column - 1)
    return jnp.where(column == 0, rows * (width - 1) + rows - 1 - row, snake)


def load_kernel(count, win_keys, win_values, cache_keys, cache_values, q_hbm, valid_hbm, first_hbm, *refs):
    keys, values, q_ref, limits, valid_ref, first_ref, sems = refs
    window_rows = win_keys.shape[0]
    pairs = [
        (valid_hbm, valid_ref),
        (first_hbm, first_ref),
        (q_hbm, q_ref),
        (win_keys, keys.at[:window_rows]),
        (cache_keys, keys.at[window_rows:]),
        (win_values, values.at[:window_rows]),
        (cache_values, values.at[window_rows:]),
    ]
    copies = [pltpu.make_async_copy(*pair, sems.at[index]) for index, pair in enumerate(pairs)]
    for copy in copies:
        copy.start()
    for copy in copies[:2]:
        copy.wait()
    me = lax.axis_index("ctx")
    position = position_of(me, count)
    first = first_ref[me]
    for row, offset in enumerate(ring_offsets(count)):
        place = place_at(lax.rem(position + offset + count, count), count)
        limit = jnp.where((place >= first) & (place <= me), valid_ref[place], 0)
        limits[row : row + 1, :] = jnp.full((1, HD), limit, jnp.int32)
    limits[count - 1 : count, :] = jnp.full((1, HD), valid_ref[me], jnp.int32)
    for copy in copies[2:]:
        copy.wait()


def load(count, win_keys, win_values, cache_keys, cache_values, queries, valid_counts, first_block):
    rows, width = win_keys.shape[0] + cache_keys.shape[0], win_keys.shape[1]
    return pl.pallas_call(
        functools.partial(load_kernel, count),
        out_shape=[
            jax.ShapeDtypeStruct((rows, width), win_keys.dtype),
            jax.ShapeDtypeStruct((rows, width), win_keys.dtype),
            jax.ShapeDtypeStruct(queries.shape, queries.dtype),
            jax.ShapeDtypeStruct((-(-count // 8) * 8, HD), jnp.int32),
        ],
        in_specs=[pl.BlockSpec(memory_space=pltpu.HBM)] * 7,
        out_specs=[pl.BlockSpec(memory_space=pltpu.VMEM)] * 4,
        scratch_shapes=[
            pltpu.SMEM(valid_counts.shape, jnp.int32),
            pltpu.SMEM(first_block.shape, jnp.int32),
            pltpu.SemaphoreType.DMA((7,)),
        ],
        compiler_params=pltpu.CompilerParams(vmem_limit_bytes=4 * 1024 * 1024),
        cost_estimate=pl.CostEstimate(flops=0, bytes_accessed=8 * rows * width, transcendentals=0),
        name="load",
    )(win_keys, win_values, cache_keys, cache_values, queries, valid_counts, first_block)


def ring_offsets(count):
    half = count // 2
    return [sign * step for step in range(1, half) for sign in (-1, 1)] + [half]


def place_window(index, limit_row, own, sizes, limits, key, value, keys, values):
    window_rows = sizes[0]
    if not own:
        row_iota = lax.broadcasted_iota(jnp.int32, (window_rows, HD), 0)
        shown = row_iota < limits[limit_row : limit_row + 1, :]
    at = slice(index * window_rows, (index + 1) * window_rows)
    for head in range(keys.shape[0]):
        lanes = slice(head * HD, (head + 1) * HD)
        win_key, win_value = key[:window_rows, lanes], value[:window_rows, lanes]
        if own:
            keys[head, at, :] = win_key
            values[head, at, :HD] = win_value
            values[head, at, HD:] = jnp.ones((window_rows, HD), jnp.bfloat16)
        else:
            fill = key[window_rows : window_rows + 1, lanes].astype(jnp.float32)
            keys[head, at, :] = jnp.where(shown, win_key.astype(jnp.float32), fill).astype(jnp.bfloat16)
            values[head, at, :HD] = jnp.where(shown, win_value.astype(jnp.float32), 0.0).astype(jnp.bfloat16)
            values[head, at, HD:] = jnp.where(shown, 1.0, 0.0).astype(jnp.bfloat16)


def place_cache(index, number, sizes, key, value, keys, values):
    window_rows, cache_rows = sizes
    start = number * window_rows + index * cache_rows
    at = slice(start, start + cache_rows)
    for head in range(keys.shape[0]):
        lanes = slice(head * HD, (head + 1) * HD)
        keys[head, at, :] = key[window_rows:, lanes]
        values[head, at, :HD] = value[window_rows:, lanes]
        values[head, at, HD:] = jnp.ones((cache_rows, HD), jnp.bfloat16)


def fill_up(filled, keys, values):
    spare = keys.shape[1] - filled
    if spare:
        for head in range(keys.shape[0]):
            row = keys[head, filled - 1 : filled, :].astype(jnp.float32)
            keys[head, filled:, :] = jnp.broadcast_to(row, (spare, HD)).astype(jnp.bfloat16)
            values[head, filled:, :] = jnp.zeros((spare, 2 * HD), jnp.bfloat16)


def scores(query, keys):
    return lax.dot_general(query, keys, (((1,), (1,)), ((), ())), preferred_element_type=jnp.float32)


def weigh(score, top, values):
    lanes = score.shape[1] // HD
    weight = jnp.exp2(score * EXP_SCALE - jnp.concatenate([top] * lanes, axis=1)).astype(jnp.bfloat16)
    return jnp.dot(weight, values, preferred_element_type=jnp.float32)


def wide_top(score):
    return jnp.broadcast_to(jnp.max(score, axis=1, keepdims=True) * EXP_SCALE, (score.shape[0], HD))


def normalised(acc):
    total = acc[:, HD:]
    inverse = pl.reciprocal(total, approx=True)
    return (acc[:, :HD] * (inverse * (2.0 - total * inverse))).astype(jnp.bfloat16)


def chunks(q_ref, kv_heads, fine_end=False):
    rows = q_ref.shape[0]
    group = q_ref.shape[1] // HD // kv_heads
    sizes = [CHUNK_HEADS] * (kv_heads * group // CHUNK_HEADS)
    if fine_end:
        sizes[-1:] = [CHUNK_HEADS // 2] * 2
    base = 0
    for size in sizes:
        query = jnp.concatenate([q_ref[:, (base + i) * HD : (base + i + 1) * HD] for i in range(size)], axis=0)
        yield base // group, slice(base * rows, (base + size) * rows), query, base, size
        base += size


def first_kernel(count, sizes, q_ref, limits, own_keys, own_values, acc_out, top_out, keys, values):
    window_rows = sizes[0]
    place_window(0, 0, True, sizes, None, own_keys, own_values, keys, values)
    place_cache(0, 1, sizes, own_keys, own_values, keys, values)
    fill_up(sum(sizes), keys, values)
    rows = q_ref.shape[0]
    key_iota = lax.broadcasted_iota(jnp.int32, (rows, window_rows), 1)
    query_iota = lax.broadcasted_iota(jnp.int32, (rows, window_rows), 0)
    seen = (key_iota <= query_iota) & (key_iota < limits[count - 1 : count, :])
    bias = jnp.concatenate([jnp.where(seen, 0.0, HIDDEN)] * CHUNK_HEADS, axis=0)
    for head, at, query, _, _ in chunks(q_ref, keys.shape[0]):
        score = scores(query, keys[head])
        score = jnp.concatenate([score[:, :window_rows] + bias, score[:, window_rows:]], axis=1)
        top = wide_top(score)
        acc_out[at, :] = weigh(score, top, values[head])
        top_out[at, :] = top


def next_kernel(rows_of, last, count, sizes, q_ref, limits, *refs):
    number = len(rows_of)
    key_refs, value_refs = refs[: 2 * number : 2], refs[1 : 2 * number : 2]
    if last:
        acc_in, top_in, out, keys, values, result, sems = refs[2 * number :]
    else:
        acc_in, top_in, acc_out, top_out, keys, values = refs[2 * number :]
    rows, heads = q_ref.shape[0], q_ref.shape[1] // HD
    kv_heads = keys.shape[0]

    def sent(base):
        lanes = slice(base * HD, (base + COPY_HEADS) * HD)
        return pltpu.make_async_copy(result.at[:, lanes], out.at[:, lanes], sems.at[base // COPY_HEADS])

    def settle(base, size, acc):
        done = normalised(acc)
        for i in range(size):
            result[:, (base + i) * HD : (base + i + 1) * HD] = done[i * rows : (i + 1) * rows]

    def send(settled):
        for base, size in settled:
            for i in range(0, size, COPY_HEADS):
                sent(base + i).start()

    def wait_all():
        for base in range(0, heads, COPY_HEADS):
            sent(base).wait()

    def take_in(begin):
        fine = jnp.ones((8, HD), jnp.float32)
        settled = []
        for head, at, query, base, size in chunks(q_ref, kv_heads, last):
            top = top_in[at, :]
            acc = acc_in[at, :] + weigh(scores(query, keys[head, begin:]), top, values[head, begin:])
            safe = jnp.where(acc[:, HD:] < LARGEST_TOTAL, 1.0, 0.0).reshape(-1, 8, HD)
            fine = jnp.minimum(fine, jnp.min(safe, axis=0))
            if last:
                settle(base, size, acc)
                send(settled)
                settled = [(base, size)]
            else:
                acc_out[at, :] = acc
                top_out[at, :] = top
        send(settled)
        again = jnp.min(fine) < 0.5
        if last:
            wait_all()

        @pl.when(again)
        def _():
            for head, at, query, base, size in chunks(q_ref, kv_heads, last):
                score = scores(query, keys[head, begin:])
                before = top_in[at, :]
                top = jnp.maximum(before, wide_top(score))
                fade = jnp.exp2(before - top)
                acc = acc_in[at, :] * jnp.concatenate([fade, fade], axis=1)
                acc = acc + weigh(score, top, values[head, begin:])
                if last:
                    settle(base, size, acc)
                    send([(base, size)])
                else:
                    acc_out[at, :] = acc
                    top_out[at, :] = top
            if last:
                wait_all()

    for index in range(number):
        place_cache(index, number, sizes, key_refs[index], value_refs[index], keys, values)
    fill_up(number * sum(sizes), keys, values)
    if number < 4:
        for index, row in enumerate(rows_of):
            place_window(index, row, False, sizes, limits, key_refs[index], value_refs[index], keys, values)
        take_in(0)
        return
    me = lax.axis_index("ctx")
    position = position_of(me, count)
    offsets = ring_offsets(count)
    places = [place_at(lax.rem(position + offsets[row] + count, count), count) for row in rows_of]
    earlier = functools.reduce(jnp.logical_or, [place < me for place in places])

    @pl.when(earlier)
    def _():
        for index, row in enumerate(rows_of):
            place_window(index, row, False, sizes, limits, key_refs[index], value_refs[index], keys, values)
        take_in(0)

    @pl.when(jnp.logical_not(earlier))
    def _():
        take_in(number * sizes[0])


def kernel_options(queries, total_keys, kv_heads):
    rows, width = queries.shape
    return {
        "compiler_params": pltpu.CompilerParams(vmem_limit_bytes=40 * 1024 * 1024),
        "cost_estimate": pl.CostEstimate(
            flops=6 * rows * width * total_keys,
            bytes_accessed=2 * rows * width,
            transcendentals=rows * (width // HD) * total_keys,
        ),
    }


def room(kv_heads, total_keys):
    return [
        pltpu.VMEM((kv_heads, total_keys, HD), jnp.bfloat16),
        pltpu.VMEM((kv_heads, total_keys, 2 * HD), jnp.bfloat16),
    ]


def state_shapes(queries):
    rows = queries.shape[0] * queries.shape[1] // HD
    return [jax.ShapeDtypeStruct((rows, 2 * HD), jnp.float32), jax.ShapeDtypeStruct((rows, HD), jnp.float32)]


def attend_first(count, sizes, queries, limits, own_keys, own_values):
    kv_heads = own_keys.shape[1] // HD
    total_keys = -(-sum(sizes) // HD) * HD
    vmem = pl.BlockSpec(memory_space=pltpu.VMEM)
    return tuple(
        pl.pallas_call(
            functools.partial(first_kernel, count, sizes),
            out_shape=state_shapes(queries),
            in_specs=[vmem] * 4,
            out_specs=[vmem] * 2,
            scratch_shapes=room(kv_heads, total_keys),
            name="attend_first",
            **kernel_options(queries, total_keys, kv_heads),
        )(queries, limits, own_keys, own_values)
    )


def attend_next(pieces, state, last, count, sizes, queries, limits):
    rows_of = tuple(piece[0] for piece in pieces)
    blocks = [block for piece in pieces for block in piece[1:]]
    kv_heads = blocks[0].shape[1] // HD
    total_keys = -(-len(pieces) * sum(sizes) // HD) * HD
    vmem = pl.BlockSpec(memory_space=pltpu.VMEM)
    operands = [queries, limits, *blocks, *state]
    shapes = [jax.ShapeDtypeStruct(queries.shape, queries.dtype)] if last else state_shapes(queries)
    scratch = room(kv_heads, total_keys)
    if last:
        copies = queries.shape[1] // HD // COPY_HEADS
        scratch += [pltpu.VMEM(queries.shape, queries.dtype), pltpu.SemaphoreType.DMA((copies,))]
    outs = pl.pallas_call(
        functools.partial(next_kernel, rows_of, last, count, sizes),
        out_shape=shapes,
        in_specs=[vmem] * len(operands),
        out_specs=[pl.BlockSpec(memory_space=pltpu.HBM)] if last else [vmem] * len(shapes),
        scratch_shapes=scratch,
        name="attend_last" if last else "attend_next",
        **kernel_options(queries, total_keys, kv_heads),
    )(*operands)
    return outs[0] if last else tuple(outs)


def shards(count, queries, win_keys, win_values, cache_keys, cache_values, valid_counts, first_block):
    sizes = (win_keys.shape[0], cache_keys.shape[0])
    half = count // 2
    ring = [place_at(p, count) for p in range(count)]
    onward = [(ring[p], ring[(p + 1) % count]) for p in range(count)]
    backward = [(b, a) for a, b in onward]

    win_keys, win_values, cache_keys, cache_values, valid_counts, first_block, queries = [
        pltpu.with_memory_space_constraint(x, pltpu.HBM)
        for x in (win_keys, win_values, cache_keys, cache_values, valid_counts, first_block, queries)
    ]
    own_keys, own_values, near, limits = load(
        count, win_keys, win_values, cache_keys, cache_values, queries, valid_counts, first_block
    )
    key_on = key_back = own_keys
    value_on = value_back = own_values
    state = attend_first(count, sizes, near, limits, own_keys, own_values)
    arrived = []
    for step in range(1, half + 1):
        key_on = lax.ppermute(key_on, "ctx", onward)
        value_back = lax.ppermute(value_back, "ctx", backward)
        if step < half:
            value_on = lax.ppermute(value_on, "ctx", onward)
            key_back = lax.ppermute(key_back, "ctx", backward)
            row = 2 * (step - 1)
            arrived.append([(row, key_on, value_on), (row + 1, key_back, value_back)])
        else:
            arrived.append([(2 * (half - 1), key_on, value_back)])
        if step == 1:
            key_on, top = lax.optimization_barrier((key_on, state[1]))
            state = (state[0], top)
    for begin in range(0, half - 2, 2):
        pieces = [piece for step in arrived[begin : min(begin + 2, half - 2)] for piece in step]
        state = attend_next(pieces, state, False, count, sizes, near, limits)
    state = attend_next(arrived[half - 2], state, False, count, sizes, near, limits)
    return attend_next(arrived[half - 1], state, True, count, sizes, near, limits)


def solution(mesh):
    in_specs = (
        P(("groups", "ctx"), "tp"),
        P(("groups", "ctx"), "tp"),
        P(("groups", "ctx"), "tp"),
        P(("groups", "ctx"), "tp"),
        P(("groups", "ctx"), "tp"),
        P("groups"),
        P("groups"),
    )
    out_specs = P(("groups", "ctx"), "tp")
    return jax.shard_map(
        functools.partial(shards, mesh.shape["ctx"]),
        mesh=mesh,
        in_specs=in_specs,
        out_specs=out_specs,
        check_vma=False,
    )
```

```python
import functools
import math

import jax
import jax.numpy as jnp
from jax import lax
from jax.experimental import pallas as pl
from jax.experimental.pallas import tpu as pltpu
from jax.sharding import PartitionSpec as P

HD = 128
EXP_SCALE = HD**-0.5 * math.log2(math.e)
HIDDEN = -1.0e30
CHUNK_HEADS = 4
COPY_HEADS = 2
LARGEST_TOTAL = 2.0**100


def ring_width(count):
    width = round(count ** (1 / 3))
    if width > 1 and count % width == 0 and (count // width) % 2 == 0:
        return width
    return 1


def place_at(position, count):
    width = ring_width(count)
    if width == 1:
        return position
    rows = count // width
    row, step = position // (width - 1), position % (width - 1)
    forth = row * width + 1 + step
    back = row * width + width - 1 - step
    home = (rows - 1 - (position - rows * (width - 1))) * width
    if isinstance(position, int):
        return home if position >= rows * (width - 1) else (back if row % 2 else forth)
    return jnp.where(position >= rows * (width - 1), home, jnp.where(row % 2 == 1, back, forth))


def position_of(place, count):
    width = ring_width(count)
    if width == 1:
        return place
    rows = count // width
    row, column = place // width, place % width
    snake = row * (width - 1) + jnp.where(row % 2 == 1, width - 1 - column, column - 1)
    return jnp.where(column == 0, rows * (width - 1) + rows - 1 - row, snake)


def load_kernel(count, win_keys, win_values, cache_keys, cache_values, q_hbm, valid_hbm, first_hbm, *refs):
    keys, values, q_ref, limits, valid_ref, first_ref, sems = refs
    window_rows = win_keys.shape[0]
    pairs = [
        (valid_hbm, valid_ref),
        (first_hbm, first_ref),
        (q_hbm, q_ref),
        (win_keys, keys.at[:window_rows]),
        (cache_keys, keys.at[window_rows:]),
        (win_values, values.at[:window_rows]),
        (cache_values, values.at[window_rows:]),
    ]
    copies = [pltpu.make_async_copy(*pair, sems.at[index]) for index, pair in enumerate(pairs)]
    for copy in copies:
        copy.start()
    for copy in copies[:2]:
        copy.wait()
    me = lax.axis_index("ctx")
    position = position_of(me, count)
    first = first_ref[me]
    for row, offset in enumerate(ring_offsets(count)):
        place = place_at(lax.rem(position + offset + count, count), count)
        limit = jnp.where((place >= first) & (place <= me), valid_ref[place], 0)
        limits[row : row + 1, :] = jnp.full((1, HD), limit, jnp.int32)
    limits[count - 1 : count, :] = jnp.full((1, HD), valid_ref[me], jnp.int32)
    for copy in copies[2:]:
        copy.wait()


def load(count, win_keys, win_values, cache_keys, cache_values, queries, valid_counts, first_block):
    rows, width = win_keys.shape[0] + cache_keys.shape[0], win_keys.shape[1]
    return pl.pallas_call(
        functools.partial(load_kernel, count),
        out_shape=[
            jax.ShapeDtypeStruct((rows, width), win_keys.dtype),
            jax.ShapeDtypeStruct((rows, width), win_keys.dtype),
            jax.ShapeDtypeStruct(queries.shape, queries.dtype),
            jax.ShapeDtypeStruct((-(-count // 8) * 8, HD), jnp.int32),
        ],
        in_specs=[pl.BlockSpec(memory_space=pltpu.HBM)] * 7,
        out_specs=[pl.BlockSpec(memory_space=pltpu.VMEM)] * 4,
        scratch_shapes=[
            pltpu.SMEM(valid_counts.shape, jnp.int32),
            pltpu.SMEM(first_block.shape, jnp.int32),
            pltpu.SemaphoreType.DMA((7,)),
        ],
        compiler_params=pltpu.CompilerParams(vmem_limit_bytes=4 * 1024 * 1024),
        cost_estimate=pl.CostEstimate(flops=0, bytes_accessed=8 * rows * width, transcendentals=0),
        name="load",
    )(win_keys, win_values, cache_keys, cache_values, queries, valid_counts, first_block)


def ring_offsets(count):
    half = count // 2
    return [sign * step for step in range(1, half) for sign in (1, -1)] + [half]


def place_window(index, limit_row, own, sizes, limits, key, value, keys, values):
    window_rows = sizes[0]
    if not own:
        row_iota = lax.broadcasted_iota(jnp.int32, (window_rows, HD), 0)
        shown = row_iota < limits[limit_row : limit_row + 1, :]
    at = slice(index * window_rows, (index + 1) * window_rows)
    for head in range(keys.shape[0]):
        lanes = slice(head * HD, (head + 1) * HD)
        win_key, win_value = key[:window_rows, lanes], value[:window_rows, lanes]
        if own:
            keys[head, at, :] = win_key
            values[head, at, :HD] = win_value
            values[head, at, HD:] = jnp.ones((window_rows, HD), jnp.bfloat16)
        else:
            fill = key[window_rows : window_rows + 1, lanes].astype(jnp.float32)
            keys[head, at, :] = jnp.where(shown, win_key.astype(jnp.float32), fill).astype(jnp.bfloat16)
            values[head, at, :HD] = jnp.where(shown, win_value.astype(jnp.float32), 0.0).astype(jnp.bfloat16)
            values[head, at, HD:] = jnp.where(shown, 1.0, 0.0).astype(jnp.bfloat16)


def place_cache(index, number, sizes, key, value, keys, values):
    window_rows, cache_rows = sizes
    start = number * window_rows + index * cache_rows
    at = slice(start, start + cache_rows)
    for head in range(keys.shape[0]):
        lanes = slice(head * HD, (head + 1) * HD)
        keys[head, at, :] = key[window_rows:, lanes]
        values[head, at, :HD] = value[window_rows:, lanes]
        values[head, at, HD:] = jnp.ones((cache_rows, HD), jnp.bfloat16)


def fill_up(filled, keys, values):
    spare = keys.shape[1] - filled
    if spare:
        for head in range(keys.shape[0]):
            row = keys[head, filled - 1 : filled, :].astype(jnp.float32)
            keys[head, filled:, :] = jnp.broadcast_to(row, (spare, HD)).astype(jnp.bfloat16)
            values[head, filled:, :] = jnp.zeros((spare, 2 * HD), jnp.bfloat16)


def scores(query, keys):
    return lax.dot_general(query, keys, (((1,), (1,)), ((), ())), preferred_element_type=jnp.float32)


def weigh(score, top, values):
    lanes = score.shape[1] // HD
    weight = jnp.exp2(score * EXP_SCALE - jnp.concatenate([top] * lanes, axis=1)).astype(jnp.bfloat16)
    return jnp.dot(weight, values, preferred_element_type=jnp.float32)


def wide_top(score):
    return jnp.broadcast_to(jnp.max(score, axis=1, keepdims=True) * EXP_SCALE, (score.shape[0], HD))


def normalised(acc):
    total = acc[:, HD:]
    inverse = pl.reciprocal(total, approx=True)
    return (acc[:, :HD] * (inverse * (2.0 - total * inverse))).astype(jnp.bfloat16)


def chunks(q_ref, kv_heads, fine_end=False):
    rows = q_ref.shape[0]
    group = q_ref.shape[1] // HD // kv_heads
    sizes = [CHUNK_HEADS] * (kv_heads * group // CHUNK_HEADS)
    if fine_end:
        sizes[-1:] = [CHUNK_HEADS // 2] * 2
    base = 0
    for size in sizes:
        query = jnp.concatenate([q_ref[:, (base + i) * HD : (base + i + 1) * HD] for i in range(size)], axis=0)
        yield base // group, slice(base * rows, (base + size) * rows), query, base, size
        base += size


def first_kernel(count, sizes, q_ref, limits, own_keys, own_values, acc_out, top_out, keys, values):
    window_rows = sizes[0]
    place_window(0, 0, True, sizes, None, own_keys, own_values, keys, values)
    place_cache(0, 1, sizes, own_keys, own_values, keys, values)
    fill_up(sum(sizes), keys, values)
    rows = q_ref.shape[0]
    key_iota = lax.broadcasted_iota(jnp.int32, (rows, window_rows), 1)
    query_iota = lax.broadcasted_iota(jnp.int32, (rows, window_rows), 0)
    seen = (key_iota <= query_iota) & (key_iota < limits[count - 1 : count, :])
    bias = jnp.concatenate([jnp.where(seen, 0.0, HIDDEN)] * CHUNK_HEADS, axis=0)
    for head, at, query, _, _ in chunks(q_ref, keys.shape[0]):
        score = scores(query, keys[head])
        score = jnp.concatenate([score[:, :window_rows] + bias, score[:, window_rows:]], axis=1)
        top = wide_top(score)
        acc_out[at, :] = weigh(score, top, values[head])
        top_out[at, :] = top


def next_kernel(rows_of, last, count, sizes, q_ref, limits, *refs):
    number = len(rows_of)
    key_refs, value_refs = refs[: 2 * number : 2], refs[1 : 2 * number : 2]
    if last:
        acc_in, top_in, out, keys, values, result, sems = refs[2 * number :]
    else:
        acc_in, top_in, acc_out, top_out, keys, values = refs[2 * number :]
    rows, heads = q_ref.shape[0], q_ref.shape[1] // HD
    kv_heads = keys.shape[0]

    def sent(base):
        lanes = slice(base * HD, (base + COPY_HEADS) * HD)
        return pltpu.make_async_copy(result.at[:, lanes], out.at[:, lanes], sems.at[base // COPY_HEADS])

    def settle(base, size, acc):
        done = normalised(acc)
        for i in range(size):
            result[:, (base + i) * HD : (base + i + 1) * HD] = done[i * rows : (i + 1) * rows]
        for i in range(0, size, COPY_HEADS):
            sent(base + i).start()

    def wait_all():
        for base in range(0, heads, COPY_HEADS):
            sent(base).wait()

    def take_in(begin):
        grand_total = jnp.zeros((8, HD), jnp.float32)
        for head, at, query, base, size in chunks(q_ref, kv_heads, last):
            top = top_in[at, :]
            acc = acc_in[at, :] + weigh(scores(query, keys[head, begin:]), top, values[head, begin:])
            grand_total = grand_total + jnp.sum(acc[:, HD:].reshape(-1, 8, HD), axis=0)
            if last:
                settle(base, size, acc)
            else:
                acc_out[at, :] = acc
                top_out[at, :] = top
        again = jnp.min(jnp.where(grand_total < LARGEST_TOTAL, 1.0, 0.0)) < 0.5
        if last:
            wait_all()

        @pl.when(again)
        def _():
            for head, at, query, base, size in chunks(q_ref, kv_heads, last):
                score = scores(query, keys[head, begin:])
                before = top_in[at, :]
                top = jnp.maximum(before, wide_top(score))
                fade = jnp.exp2(before - top)
                acc = acc_in[at, :] * jnp.concatenate([fade, fade], axis=1)
                acc = acc + weigh(score, top, values[head, begin:])
                if last:
                    settle(base, size, acc)
                else:
                    acc_out[at, :] = acc
                    top_out[at, :] = top
            if last:
                wait_all()

    for index in range(number):
        place_cache(index, number, sizes, key_refs[index], value_refs[index], keys, values)
    fill_up(number * sum(sizes), keys, values)
    if number < 4:
        for index, row in enumerate(rows_of):
            place_window(index, row, False, sizes, limits, key_refs[index], value_refs[index], keys, values)
        take_in(0)
        return
    me = lax.axis_index("ctx")
    position = position_of(me, count)
    offsets = ring_offsets(count)
    places = [place_at(lax.rem(position + offsets[row] + count, count), count) for row in rows_of]
    earlier = functools.reduce(jnp.logical_or, [place < me for place in places])

    @pl.when(earlier)
    def _():
        for index, row in enumerate(rows_of):
            place_window(index, row, False, sizes, limits, key_refs[index], value_refs[index], keys, values)
        take_in(0)

    @pl.when(jnp.logical_not(earlier))
    def _():
        take_in(number * sizes[0])


def kernel_options(queries, total_keys, kv_heads):
    rows, width = queries.shape
    return {
        "compiler_params": pltpu.CompilerParams(vmem_limit_bytes=40 * 1024 * 1024),
        "cost_estimate": pl.CostEstimate(
            flops=6 * rows * width * total_keys,
            bytes_accessed=2 * rows * width,
            transcendentals=rows * (width // HD) * total_keys,
        ),
    }


def room(kv_heads, total_keys):
    return [
        pltpu.VMEM((kv_heads, total_keys, HD), jnp.bfloat16),
        pltpu.VMEM((kv_heads, total_keys, 2 * HD), jnp.bfloat16),
    ]


def state_shapes(queries):
    rows = queries.shape[0] * queries.shape[1] // HD
    return [jax.ShapeDtypeStruct((rows, 2 * HD), jnp.float32), jax.ShapeDtypeStruct((rows, HD), jnp.float32)]


def attend_first(count, sizes, queries, limits, own_keys, own_values):
    kv_heads = own_keys.shape[1] // HD
    total_keys = -(-sum(sizes) // HD) * HD
    vmem = pl.BlockSpec(memory_space=pltpu.VMEM)
    return tuple(
        pl.pallas_call(
            functools.partial(first_kernel, count, sizes),
            out_shape=state_shapes(queries),
            in_specs=[vmem] * 4,
            out_specs=[vmem] * 2,
            scratch_shapes=room(kv_heads, total_keys),
            name="attend_first",
            **kernel_options(queries, total_keys, kv_heads),
        )(queries, limits, own_keys, own_values)
    )


def attend_next(pieces, state, last, count, sizes, queries, limits):
    rows_of = tuple(piece[0] for piece in pieces)
    blocks = [block for piece in pieces for block in piece[1:]]
    kv_heads = blocks[0].shape[1] // HD
    total_keys = -(-len(pieces) * sum(sizes) // HD) * HD
    vmem = pl.BlockSpec(memory_space=pltpu.VMEM)
    operands = [queries, limits, *blocks, *state]
    shapes = [jax.ShapeDtypeStruct(queries.shape, queries.dtype)] if last else state_shapes(queries)
    scratch = room(kv_heads, total_keys)
    if last:
        copies = queries.shape[1] // HD // COPY_HEADS
        scratch += [pltpu.VMEM(queries.shape, queries.dtype), pltpu.SemaphoreType.DMA((copies,))]
    outs = pl.pallas_call(
        functools.partial(next_kernel, rows_of, last, count, sizes),
        out_shape=shapes,
        in_specs=[vmem] * len(operands),
        out_specs=[pl.BlockSpec(memory_space=pltpu.HBM)] if last else [vmem] * len(shapes),
        scratch_shapes=scratch,
        name="attend_last" if last else "attend_next",
        **kernel_options(queries, total_keys, kv_heads),
    )(*operands)
    return outs[0] if last else tuple(outs)


def shards(count, queries, win_keys, win_values, cache_keys, cache_values, valid_counts, first_block):
    sizes = (win_keys.shape[0], cache_keys.shape[0])
    half = count // 2
    ring = [place_at(p, count) for p in range(count)]
    onward = [(ring[p], ring[(p - 1) % count]) for p in range(count)]
    backward = [(b, a) for a, b in onward]

    win_keys, win_values, cache_keys, cache_values, valid_counts, first_block, queries = [
        pltpu.with_memory_space_constraint(x, pltpu.HBM)
        for x in (win_keys, win_values, cache_keys, cache_values, valid_counts, first_block, queries)
    ]
    own_keys, own_values, near, limits = load(
        count, win_keys, win_values, cache_keys, cache_values, queries, valid_counts, first_block
    )
    key_on = key_back = own_keys
    value_on = value_back = own_values
    state = attend_first(count, sizes, near, limits, own_keys, own_values)
    arrived = []
    for step in range(1, half + 1):
        key_on = lax.ppermute(key_on, "ctx", onward)
        value_back = lax.ppermute(value_back, "ctx", backward)
        if step < half:
            value_on = lax.ppermute(value_on, "ctx", onward)
            key_back = lax.ppermute(key_back, "ctx", backward)
            row = 2 * (step - 1)
            arrived.append([(row, key_on, value_on), (row + 1, key_back, value_back)])
        else:
            arrived.append([(2 * (half - 1), key_on, value_back)])
        if step == 1:
            key_on, top = lax.optimization_barrier((key_on, state[1]))
            state = (state[0], top)
    for begin in range(0, half - 2, 2):
        pieces = [piece for step in arrived[begin : min(begin + 2, half - 2)] for piece in step]
        state = attend_next(pieces, state, False, count, sizes, near, limits)
    state = attend_next(arrived[half - 2], state, False, count, sizes, near, limits)
    return attend_next(arrived[half - 1], state, True, count, sizes, near, limits)


def solution(mesh):
    in_specs = (
        P(("groups", "ctx"), "tp"),
        P(("groups", "ctx"), "tp"),
        P(("groups", "ctx"), "tp"),
        P(("groups", "ctx"), "tp"),
        P(("groups", "ctx"), "tp"),
        P("groups"),
        P("groups"),
    )
    out_specs = P(("groups", "ctx"), "tp")
    return jax.shard_map(
        functools.partial(shards, mesh.shape["ctx"]),
        mesh=mesh,
        in_specs=in_specs,
        out_specs=out_specs,
        check_vma=False,
    )
```

```python
import functools
import math

import jax
import jax.numpy as jnp
from jax import lax
from jax.experimental import pallas as pl
from jax.experimental.pallas import tpu as pltpu
from jax.sharding import PartitionSpec as P

HD = 128
EXP_SCALE = HD**-0.5 * math.log2(math.e)
HIDDEN = -1.0e30
CHUNK_HEADS = 4
COPY_HEADS = 2
LARGEST_TOTAL = 2.0**100


def ring_width(count):
    width = round(count ** (1 / 3))
    if width > 1 and count % width == 0 and (count // width) % 2 == 0:
        return width
    return 1


def place_at(position, count):
    width = ring_width(count)
    if width == 1:
        return position
    rows = count // width
    row, step = position // (width - 1), position % (width - 1)
    forth = row * width + 1 + step
    back = row * width + width - 1 - step
    home = (rows - 1 - (position - rows * (width - 1))) * width
    if isinstance(position, int):
        return home if position >= rows * (width - 1) else (back if row % 2 else forth)
    return jnp.where(position >= rows * (width - 1), home, jnp.where(row % 2 == 1, back, forth))


def position_of(place, count):
    width = ring_width(count)
    if width == 1:
        return place
    rows = count // width
    row, column = place // width, place % width
    snake = row * (width - 1) + jnp.where(row % 2 == 1, width - 1 - column, column - 1)
    return jnp.where(column == 0, rows * (width - 1) + rows - 1 - row, snake)


def load_kernel(count, win_keys, win_values, cache_keys, cache_values, q_hbm, valid_hbm, first_hbm, *refs):
    keys, values, q_ref, limits, valid_ref, first_ref, sems = refs
    window_rows = win_keys.shape[0]
    pairs = [
        (valid_hbm, valid_ref),
        (first_hbm, first_ref),
        (q_hbm, q_ref),
        (win_keys, keys.at[:window_rows]),
        (cache_keys, keys.at[window_rows:]),
        (win_values, values.at[:window_rows]),
        (cache_values, values.at[window_rows:]),
    ]
    copies = [pltpu.make_async_copy(*pair, sems.at[index]) for index, pair in enumerate(pairs)]
    for copy in copies:
        copy.start()
    for copy in copies[:2]:
        copy.wait()
    me = lax.axis_index("ctx")
    position = position_of(me, count)
    first = first_ref[me]
    for row, offset in enumerate(ring_offsets(count)):
        place = place_at(lax.rem(position + offset + count, count), count)
        limit = jnp.where((place >= first) & (place <= me), valid_ref[place], 0)
        limits[row : row + 1, :] = jnp.full((1, HD), limit, jnp.int32)
    limits[count - 1 : count, :] = jnp.full((1, HD), valid_ref[me], jnp.int32)
    for copy in copies[2:]:
        copy.wait()


def load(count, win_keys, win_values, cache_keys, cache_values, queries, valid_counts, first_block):
    rows, width = win_keys.shape[0] + cache_keys.shape[0], win_keys.shape[1]
    return pl.pallas_call(
        functools.partial(load_kernel, count),
        out_shape=[
            jax.ShapeDtypeStruct((rows, width), win_keys.dtype),
            jax.ShapeDtypeStruct((rows, width), win_keys.dtype),
            jax.ShapeDtypeStruct(queries.shape, queries.dtype),
            jax.ShapeDtypeStruct((-(-count // 8) * 8, HD), jnp.int32),
        ],
        in_specs=[pl.BlockSpec(memory_space=pltpu.HBM)] * 7,
        out_specs=[pl.BlockSpec(memory_space=pltpu.VMEM)] * 4,
        scratch_shapes=[
            pltpu.SMEM(valid_counts.shape, jnp.int32),
            pltpu.SMEM(first_block.shape, jnp.int32),
            pltpu.SemaphoreType.DMA((7,)),
        ],
        compiler_params=pltpu.CompilerParams(vmem_limit_bytes=4 * 1024 * 1024),
        cost_estimate=pl.CostEstimate(flops=0, bytes_accessed=8 * rows * width, transcendentals=0),
        name="load",
    )(win_keys, win_values, cache_keys, cache_values, queries, valid_counts, first_block)


def ring_offsets(count):
    half = count // 2
    return [sign * step for step in range(1, half) for sign in (1, -1)] + [half]


def place_keys(index, number, limit_row, own, sizes, limits, key, keys):
    window_rows, cache_rows = sizes
    at = slice(index * window_rows, (index + 1) * window_rows)
    cache_at = number * window_rows + index * cache_rows
    if not own:
        row_iota = lax.broadcasted_iota(jnp.int32, (window_rows, HD), 0)
        shown = row_iota < limits[limit_row : limit_row + 1, :]
    for head in range(keys.shape[0]):
        lanes = slice(head * HD, (head + 1) * HD)
        win_key = key[:window_rows, lanes]
        if not own:
            fill = key[window_rows : window_rows + 1, lanes].astype(jnp.float32)
            win_key = jnp.where(shown, win_key.astype(jnp.float32), fill).astype(jnp.bfloat16)
        keys[head, at, :] = win_key
        keys[head, cache_at : cache_at + cache_rows, :] = key[window_rows:, lanes]
        spare = keys.shape[1] - number * sum(sizes)
        if spare and index == 0:
            row = key[window_rows : window_rows + 1, lanes].astype(jnp.float32)
            keys[head, keys.shape[1] - spare :, :] = jnp.broadcast_to(row, (spare, HD)).astype(jnp.bfloat16)


def place_values(index, number, limit_row, own, sizes, limits, value, values):
    window_rows, cache_rows = sizes
    at = slice(index * window_rows, (index + 1) * window_rows)
    cache_at = number * window_rows + index * cache_rows
    if not own:
        row_iota = lax.broadcasted_iota(jnp.int32, (window_rows, HD), 0)
        shown = row_iota < limits[limit_row : limit_row + 1, :]
    for head in range(values.shape[0]):
        lanes = slice(head * HD, (head + 1) * HD)
        win_value, ones = value[:window_rows, lanes], jnp.ones((window_rows, HD), jnp.bfloat16)
        if not own:
            win_value = jnp.where(shown, win_value.astype(jnp.float32), 0.0).astype(jnp.bfloat16)
            ones = jnp.where(shown, 1.0, 0.0).astype(jnp.bfloat16)
        values[head, at, :HD] = win_value
        values[head, at, HD:] = ones
        values[head, cache_at : cache_at + cache_rows, :HD] = value[window_rows:, lanes]
        values[head, cache_at : cache_at + cache_rows, HD:] = jnp.ones((cache_rows, HD), jnp.bfloat16)
        spare = values.shape[1] - number * sum(sizes)
        if spare and index == 0:
            values[head, values.shape[1] - spare :, :] = jnp.zeros((spare, 2 * HD), jnp.bfloat16)


def place_block(index, number, limit_row, own, sizes, limits, key, value, keys, values):
    place_keys(index, number, limit_row, own, sizes, limits, key, keys)
    place_values(index, number, limit_row, own, sizes, limits, value, values)


def scores(query, keys):
    return lax.dot_general(query, keys, (((1,), (1,)), ((), ())), preferred_element_type=jnp.float32)


def weights(score, top):
    lanes = score.shape[1] // HD
    return jnp.exp2(score * EXP_SCALE - jnp.concatenate([top] * lanes, axis=1)).astype(jnp.bfloat16)


def weigh(score, top, values):
    return jnp.dot(weights(score, top), values, preferred_element_type=jnp.float32)


def wide_top(score):
    return jnp.broadcast_to(jnp.max(score, axis=1, keepdims=True) * EXP_SCALE, (score.shape[0], HD))


def normalised(acc):
    total = acc[:, HD:]
    inverse = pl.reciprocal(total, approx=True)
    return (acc[:, :HD] * (inverse * (2.0 - total * inverse))).astype(jnp.bfloat16)


def chunks(q_ref, kv_heads, fine_end=False):
    rows = q_ref.shape[0]
    group = q_ref.shape[1] // HD // kv_heads
    sizes = [CHUNK_HEADS] * (kv_heads * group // CHUNK_HEADS)
    if fine_end:
        sizes[-1:] = [CHUNK_HEADS // 2] * 2
    base = 0
    for size in sizes:
        query = jnp.concatenate([q_ref[:, (base + i) * HD : (base + i + 1) * HD] for i in range(size)], axis=0)
        yield base // group, slice(base * rows, (base + size) * rows), query, base, size
        base += size


def first_kernel(count, sizes, q_ref, limits, own_keys, own_values, acc_out, top_out, keys, values):
    window_rows = sizes[0]
    place_block(0, 1, 0, True, sizes, None, own_keys, own_values, keys, values)
    rows = q_ref.shape[0]
    key_iota = lax.broadcasted_iota(jnp.int32, (rows, window_rows), 1)
    query_iota = lax.broadcasted_iota(jnp.int32, (rows, window_rows), 0)
    seen = (key_iota <= query_iota) & (key_iota < limits[count - 1 : count, :])
    bias = jnp.concatenate([jnp.where(seen, 0.0, HIDDEN)] * CHUNK_HEADS, axis=0)
    for head, at, query, _, _ in chunks(q_ref, keys.shape[0]):
        score = scores(query, keys[head])
        score = jnp.concatenate([score[:, :window_rows] + bias, score[:, window_rows:]], axis=1)
        top = wide_top(score)
        acc_out[at, :] = weigh(score, top, values[head])
        top_out[at, :] = top


def too_large(grand_total):
    return jnp.min(jnp.where(grand_total < LARGEST_TOTAL, 1.0, 0.0)) < 0.5


def sum_totals(acc):
    return jnp.sum(acc[:, HD:].reshape(-1, 8, HD), axis=0)


def anew(score, before, acc, values):
    top = jnp.maximum(before, wide_top(score))
    fade = jnp.exp2(before - top)
    return top, acc * jnp.concatenate([fade, fade], axis=1) + weigh(score, top, values)


def next_kernel(rows_of, count, sizes, q_ref, limits, *refs):
    number = len(rows_of)
    key_refs, value_refs = refs[: 2 * number : 2], refs[1 : 2 * number : 2]
    acc_in, top_in, acc_out, top_out, keys, values = refs[2 * number :]
    kv_heads = keys.shape[0]
    for index, row in enumerate(rows_of):
        place_block(index, number, row, False, sizes, limits, key_refs[index], value_refs[index], keys, values)

    def take_in(begin):
        grand_total = jnp.zeros((8, HD), jnp.float32)
        for head, at, query, _, _ in chunks(q_ref, kv_heads):
            top = top_in[at, :]
            acc = acc_in[at, :] + weigh(scores(query, keys[head, begin:]), top, values[head, begin:])
            grand_total = grand_total + sum_totals(acc)
            acc_out[at, :] = acc
            top_out[at, :] = top

        @pl.when(too_large(grand_total))
        def _():
            for head, at, query, _, _ in chunks(q_ref, kv_heads):
                score = scores(query, keys[head, begin:])
                top, acc = anew(score, top_in[at, :], acc_in[at, :], values[head, begin:])
                acc_out[at, :] = acc
                top_out[at, :] = top

    if number < 4:
        take_in(0)
        return
    me = lax.axis_index("ctx")
    position = position_of(me, count)
    offsets = ring_offsets(count)
    places = [place_at(lax.rem(position + offsets[row] + count, count), count) for row in rows_of]
    earlier = functools.reduce(jnp.logical_or, [place < me for place in places])

    @pl.when(earlier)
    def _():
        take_in(0)

    @pl.when(jnp.logical_not(earlier))
    def _():
        take_in(number * sizes[0])


def weights_kernel(row, sizes, q_ref, limits, key, top_in, weight_out, keys):
    place_keys(0, 1, row, False, sizes, limits, key, keys)
    for head, at, query, _, _ in chunks(q_ref, keys.shape[0]):
        weight_out[at, :] = weights(scores(query, keys[head]), top_in[at, :])


def last_kernel(row, sizes, q_ref, limits, key, value, weight_in, acc_in, top_in, out, keys, values, result, sems):
    rows, heads = q_ref.shape[0], q_ref.shape[1] // HD
    kv_heads = keys.shape[0]
    place_values(0, 1, row, False, sizes, limits, value, values)

    def sent(base):
        lanes = slice(base * HD, (base + COPY_HEADS) * HD)
        return pltpu.make_async_copy(result.at[:, lanes], out.at[:, lanes], sems.at[base // COPY_HEADS])

    def settle(base, size, acc):
        done = normalised(acc)
        for i in range(size):
            result[:, (base + i) * HD : (base + i + 1) * HD] = done[i * rows : (i + 1) * rows]
        for i in range(0, size, COPY_HEADS):
            sent(base + i).start()

    def wait_all():
        for base in range(0, heads, COPY_HEADS):
            sent(base).wait()

    grand_total = jnp.zeros((8, HD), jnp.float32)
    for head, at, _, base, size in chunks(q_ref, kv_heads, True):
        acc = acc_in[at, :] + jnp.dot(weight_in[at, :], values[head], preferred_element_type=jnp.float32)
        grand_total = grand_total + sum_totals(acc)
        settle(base, size, acc)
    again = too_large(grand_total)
    wait_all()

    @pl.when(again)
    def _():
        place_keys(0, 1, row, False, sizes, limits, key, keys)
        for head, at, query, base, size in chunks(q_ref, kv_heads, True):
            _, acc = anew(scores(query, keys[head]), top_in[at, :], acc_in[at, :], values[head])
            settle(base, size, acc)
        wait_all()


def kernel_options(queries, total_keys, kv_heads):
    rows, width = queries.shape
    return {
        "compiler_params": pltpu.CompilerParams(vmem_limit_bytes=40 * 1024 * 1024),
        "cost_estimate": pl.CostEstimate(
            flops=6 * rows * width * total_keys,
            bytes_accessed=2 * rows * width,
            transcendentals=rows * (width // HD) * total_keys,
        ),
    }


def room(kv_heads, total_keys):
    return [
        pltpu.VMEM((kv_heads, total_keys, HD), jnp.bfloat16),
        pltpu.VMEM((kv_heads, total_keys, 2 * HD), jnp.bfloat16),
    ]


def state_shapes(queries):
    rows = queries.shape[0] * queries.shape[1] // HD
    return [jax.ShapeDtypeStruct((rows, 2 * HD), jnp.float32), jax.ShapeDtypeStruct((rows, HD), jnp.float32)]


def attend_first(count, sizes, queries, limits, own_keys, own_values):
    kv_heads = own_keys.shape[1] // HD
    total_keys = -(-sum(sizes) // HD) * HD
    vmem = pl.BlockSpec(memory_space=pltpu.VMEM)
    return tuple(
        pl.pallas_call(
            functools.partial(first_kernel, count, sizes),
            out_shape=state_shapes(queries),
            in_specs=[vmem] * 4,
            out_specs=[vmem] * 2,
            scratch_shapes=room(kv_heads, total_keys),
            name="attend_first",
            **kernel_options(queries, total_keys, kv_heads),
        )(queries, limits, own_keys, own_values)
    )


def attend_next(pieces, state, count, sizes, queries, limits):
    rows_of = tuple(piece[0] for piece in pieces)
    blocks = [block for piece in pieces for block in piece[1:]]
    kv_heads = blocks[0].shape[1] // HD
    total_keys = -(-len(pieces) * sum(sizes) // HD) * HD
    vmem = pl.BlockSpec(memory_space=pltpu.VMEM)
    operands = [queries, limits, *blocks, *state]
    return tuple(
        pl.pallas_call(
            functools.partial(next_kernel, rows_of, count, sizes),
            out_shape=state_shapes(queries),
            in_specs=[vmem] * len(operands),
            out_specs=[vmem] * 2,
            scratch_shapes=room(kv_heads, total_keys),
            name="attend_next",
            **kernel_options(queries, total_keys, kv_heads),
        )(*operands)
    )


def attend_last(piece, state, sizes, queries, limits):
    row, key, value = piece
    kv_heads = key.shape[1] // HD
    total_keys = -(-sum(sizes) // HD) * HD
    copies = queries.shape[1] // HD // COPY_HEADS
    vmem = pl.BlockSpec(memory_space=pltpu.VMEM)
    options = kernel_options(queries, total_keys, kv_heads)
    weight = pl.pallas_call(
        functools.partial(weights_kernel, row, sizes),
        out_shape=jax.ShapeDtypeStruct((state[1].shape[0], total_keys), jnp.bfloat16),
        in_specs=[vmem] * 4,
        out_specs=vmem,
        scratch_shapes=room(kv_heads, total_keys)[:1],
        name="attend_weights",
        **options,
    )(queries, limits, key, state[1])
    return pl.pallas_call(
        functools.partial(last_kernel, row, sizes),
        out_shape=jax.ShapeDtypeStruct(queries.shape, queries.dtype),
        in_specs=[vmem] * 7,
        out_specs=pl.BlockSpec(memory_space=pltpu.HBM),
        scratch_shapes=[
            *room(kv_heads, total_keys),
            pltpu.VMEM(queries.shape, queries.dtype),
            pltpu.SemaphoreType.DMA((copies,)),
        ],
        name="attend_last",
        **options,
    )(queries, limits, key, value, weight, *state)


def shards(count, queries, win_keys, win_values, cache_keys, cache_values, valid_counts, first_block):
    sizes = (win_keys.shape[0], cache_keys.shape[0])
    half = count // 2
    ring = [place_at(p, count) for p in range(count)]
    onward = [(ring[p], ring[(p - 1) % count]) for p in range(count)]
    backward = [(b, a) for a, b in onward]

    win_keys, win_values, cache_keys, cache_values, valid_counts, first_block, queries = [
        pltpu.with_memory_space_constraint(x, pltpu.HBM)
        for x in (win_keys, win_values, cache_keys, cache_values, valid_counts, first_block, queries)
    ]
    own_keys, own_values, near, limits = load(
        count, win_keys, win_values, cache_keys, cache_values, queries, valid_counts, first_block
    )
    key_on = key_back = own_keys
    value_on = value_back = own_values
    state = attend_first(count, sizes, near, limits, own_keys, own_values)
    arrived = []
    for step in range(1, half + 1):
        key_on = lax.ppermute(key_on, "ctx", onward)
        value_back = lax.ppermute(value_back, "ctx", backward)
        if step < half:
            value_on = lax.ppermute(value_on, "ctx", onward)
            key_back = lax.ppermute(key_back, "ctx", backward)
            row = 2 * (step - 1)
            arrived.append([(row, key_on, value_on), (row + 1, key_back, value_back)])
        else:
            arrived.append([(2 * (half - 1), key_on, value_back)])
        if step == 1:
            key_on, top = lax.optimization_barrier((key_on, state[1]))
            state = (state[0], top)
    for begin in range(0, half - 2, 2):
        pieces = [piece for step in arrived[begin : min(begin + 2, half - 2)] for piece in step]
        state = attend_next(pieces, state, count, sizes, near, limits)
    state = attend_next(arrived[half - 2], state, count, sizes, near, limits)
    return attend_last(arrived[half - 1][0], state, sizes, near, limits)


def solution(mesh):
    in_specs = (
        P(("groups", "ctx"), "tp"),
        P(("groups", "ctx"), "tp"),
        P(("groups", "ctx"), "tp"),
        P(("groups", "ctx"), "tp"),
        P(("groups", "ctx"), "tp"),
        P("groups"),
        P("groups"),
    )
    out_specs = P(("groups", "ctx"), "tp")
    return jax.shard_map(
        functools.partial(shards, mesh.shape["ctx"]),
        mesh=mesh,
        in_specs=in_specs,
        out_specs=out_specs,
        check_vma=False,
    )
```

```python
import functools
import math

import jax
import jax.numpy as jnp
from jax import lax
from jax.experimental import pallas as pl
from jax.experimental.pallas import tpu as pltpu
from jax.sharding import PartitionSpec as P

HD = 128
EXP_SCALE = HD**-0.5 * math.log2(math.e)
HIDDEN = -1.0e30
CHUNK_HEADS = 4
COPY_HEADS = 2
LARGEST_TOTAL = 2.0**100


def ring_width(count):
    width = round(count ** (1 / 3))
    if width > 1 and count % width == 0 and (count // width) % 2 == 0:
        return width
    return 1


def place_at(position, count):
    width = ring_width(count)
    if width == 1:
        return position
    rows = count // width
    row, step = position // (width - 1), position % (width - 1)
    forth = row * width + 1 + step
    back = row * width + width - 1 - step
    home = (rows - 1 - (position - rows * (width - 1))) * width
    if isinstance(position, int):
        return home if position >= rows * (width - 1) else (back if row % 2 else forth)
    return jnp.where(position >= rows * (width - 1), home, jnp.where(row % 2 == 1, back, forth))


def position_of(place, count):
    width = ring_width(count)
    if width == 1:
        return place
    rows = count // width
    row, column = place // width, place % width
    snake = row * (width - 1) + jnp.where(row % 2 == 1, width - 1 - column, column - 1)
    return jnp.where(column == 0, rows * (width - 1) + rows - 1 - row, snake)


def load_kernel(count, win_keys, win_values, cache_keys, cache_values, q_hbm, valid_hbm, first_hbm, *refs):
    keys, values, q_ref, limits, valid_ref, first_ref, sems = refs
    window_rows = win_keys.shape[0]
    pairs = [
        (valid_hbm, valid_ref),
        (first_hbm, first_ref),
        (q_hbm, q_ref),
        (win_keys, keys.at[:window_rows]),
        (cache_keys, keys.at[window_rows:]),
        (win_values, values.at[:window_rows]),
        (cache_values, values.at[window_rows:]),
    ]
    copies = [pltpu.make_async_copy(*pair, sems.at[index]) for index, pair in enumerate(pairs)]
    for copy in copies:
        copy.start()
    for copy in copies[:2]:
        copy.wait()
    me = lax.axis_index("ctx")
    position = position_of(me, count)
    first = first_ref[me]
    for row, offset in enumerate(ring_offsets(count)):
        place = place_at(lax.rem(position + offset + count, count), count)
        limit = jnp.where((place >= first) & (place <= me), valid_ref[place], 0)
        limits[row : row + 1, :] = jnp.full((1, HD), limit, jnp.int32)
    limits[count - 1 : count, :] = jnp.full((1, HD), valid_ref[me], jnp.int32)
    for copy in copies[2:]:
        copy.wait()


def load(count, win_keys, win_values, cache_keys, cache_values, queries, valid_counts, first_block):
    rows, width = win_keys.shape[0] + cache_keys.shape[0], win_keys.shape[1]
    return pl.pallas_call(
        functools.partial(load_kernel, count),
        out_shape=[
            jax.ShapeDtypeStruct((rows, width), win_keys.dtype),
            jax.ShapeDtypeStruct((rows, width), win_keys.dtype),
            jax.ShapeDtypeStruct(queries.shape, queries.dtype),
            jax.ShapeDtypeStruct((-(-count // 8) * 8, HD), jnp.int32),
        ],
        in_specs=[pl.BlockSpec(memory_space=pltpu.HBM)] * 7,
        out_specs=[pl.BlockSpec(memory_space=pltpu.VMEM)] * 4,
        scratch_shapes=[
            pltpu.SMEM(valid_counts.shape, jnp.int32),
            pltpu.SMEM(first_block.shape, jnp.int32),
            pltpu.SemaphoreType.DMA((7,)),
        ],
        compiler_params=pltpu.CompilerParams(vmem_limit_bytes=4 * 1024 * 1024),
        cost_estimate=pl.CostEstimate(flops=0, bytes_accessed=8 * rows * width, transcendentals=0),
        name="load",
    )(win_keys, win_values, cache_keys, cache_values, queries, valid_counts, first_block)


def ring_offsets(count):
    half = count // 2
    return [sign * step for step in range(1, half) for sign in (1, -1)] + [half]


def place_keys(index, number, limit_row, own, sizes, limits, key, keys):
    window_rows, cache_rows = sizes
    at = slice(index * window_rows, (index + 1) * window_rows)
    cache_at = number * window_rows + index * cache_rows
    if not own:
        row_iota = lax.broadcasted_iota(jnp.int32, (window_rows, HD), 0)
        shown = row_iota < limits[limit_row : limit_row + 1, :]
    for head in range(keys.shape[0]):
        lanes = slice(head * HD, (head + 1) * HD)
        win_key = key[:window_rows, lanes]
        if not own:
            fill = key[window_rows : window_rows + 1, lanes].astype(jnp.float32)
            win_key = jnp.where(shown, win_key.astype(jnp.float32), fill).astype(jnp.bfloat16)
        keys[head, at, :] = win_key
        keys[head, cache_at : cache_at + cache_rows, :] = key[window_rows:, lanes]
        spare = keys.shape[1] - number * sum(sizes)
        if spare and index == 0:
            row = key[window_rows : window_rows + 1, lanes].astype(jnp.float32)
            keys[head, keys.shape[1] - spare :, :] = jnp.broadcast_to(row, (spare, HD)).astype(jnp.bfloat16)


def place_values(index, number, limit_row, own, sizes, limits, value, values):
    window_rows, cache_rows = sizes
    at = slice(index * window_rows, (index + 1) * window_rows)
    cache_at = number * window_rows + index * cache_rows
    if not own:
        row_iota = lax.broadcasted_iota(jnp.int32, (window_rows, HD), 0)
        shown = row_iota < limits[limit_row : limit_row + 1, :]
    for head in range(values.shape[0]):
        lanes = slice(head * HD, (head + 1) * HD)
        win_value, ones = value[:window_rows, lanes], jnp.ones((window_rows, HD), jnp.bfloat16)
        if not own:
            win_value = jnp.where(shown, win_value.astype(jnp.float32), 0.0).astype(jnp.bfloat16)
            ones = jnp.where(shown, 1.0, 0.0).astype(jnp.bfloat16)
        values[head, at, :HD] = win_value
        values[head, at, HD:] = ones
        values[head, cache_at : cache_at + cache_rows, :HD] = value[window_rows:, lanes]
        values[head, cache_at : cache_at + cache_rows, HD:] = jnp.ones((cache_rows, HD), jnp.bfloat16)
        spare = values.shape[1] - number * sum(sizes)
        if spare and index == 0:
            values[head, values.shape[1] - spare :, :] = jnp.zeros((spare, 2 * HD), jnp.bfloat16)


def place_block(index, number, limit_row, own, sizes, limits, key, value, keys, values):
    place_keys(index, number, limit_row, own, sizes, limits, key, keys)
    place_values(index, number, limit_row, own, sizes, limits, value, values)


def scores(query, keys):
    return lax.dot_general(query, keys, (((1,), (1,)), ((), ())), preferred_element_type=jnp.float32)


def weights(score, top):
    lanes = score.shape[1] // HD
    return jnp.exp2(score * EXP_SCALE - jnp.concatenate([top] * lanes, axis=1)).astype(jnp.bfloat16)


def weigh(score, top, values):
    return jnp.dot(weights(score, top), values, preferred_element_type=jnp.float32)


def wide_top(score):
    return jnp.broadcast_to(jnp.max(score, axis=1, keepdims=True) * EXP_SCALE, (score.shape[0], HD))


def normalised(acc):
    total = acc[:, HD:]
    inverse = pl.reciprocal(total, approx=True)
    return (acc[:, :HD] * (inverse * (2.0 - total * inverse))).astype(jnp.bfloat16)


def chunks(q_ref, kv_heads, fine_end=False):
    rows = q_ref.shape[0]
    group = q_ref.shape[1] // HD // kv_heads
    sizes = [CHUNK_HEADS] * (kv_heads * group // CHUNK_HEADS)
    if fine_end:
        sizes[-1:] = [CHUNK_HEADS // 2] * 2
    base = 0
    for size in sizes:
        query = jnp.concatenate([q_ref[:, (base + i) * HD : (base + i + 1) * HD] for i in range(size)], axis=0)
        yield base // group, slice(base * rows, (base + size) * rows), query, base, size
        base += size


def first_kernel(count, sizes, q_ref, limits, own_keys, own_values, acc_out, top_out, keys, values):
    window_rows = sizes[0]
    place_block(0, 1, 0, True, sizes, None, own_keys, own_values, keys, values)
    rows = q_ref.shape[0]
    key_iota = lax.broadcasted_iota(jnp.int32, (rows, window_rows), 1)
    query_iota = lax.broadcasted_iota(jnp.int32, (rows, window_rows), 0)
    seen = (key_iota <= query_iota) & (key_iota < limits[count - 1 : count, :])
    bias = jnp.concatenate([jnp.where(seen, 0.0, HIDDEN)] * CHUNK_HEADS, axis=0)
    for head, at, query, _, _ in chunks(q_ref, keys.shape[0]):
        score = scores(query, keys[head])
        score = jnp.concatenate([score[:, :window_rows] + bias, score[:, window_rows:]], axis=1)
        top = wide_top(score)
        acc_out[at, :] = weigh(score, top, values[head])
        top_out[at, :] = top


def too_large(grand_total):
    return jnp.min(jnp.where(grand_total < LARGEST_TOTAL, 1.0, 0.0)) < 0.5


def sum_totals(acc):
    return jnp.sum(acc[:, HD:].reshape(-1, 8, HD), axis=0)


def anew(score, before, acc, values):
    top = jnp.maximum(before, wide_top(score))
    fade = jnp.exp2(before - top)
    return top, acc * jnp.concatenate([fade, fade], axis=1) + weigh(score, top, values)


def next_kernel(rows_of, sizes, q_ref, limits, *refs):
    number = len(rows_of)
    key_refs, value_refs = refs[: 2 * number : 2], refs[1 : 2 * number : 2]
    acc_in, top_in, acc_out, top_out, keys, values = refs[2 * number :]
    kv_heads = keys.shape[0]
    for index, row in enumerate(rows_of):
        place_block(index, number, row, False, sizes, limits, key_refs[index], value_refs[index], keys, values)

    grand_total = jnp.zeros((8, HD), jnp.float32)
    for head, at, query, _, _ in chunks(q_ref, kv_heads):
        top = top_in[at, :]
        acc = acc_in[at, :] + weigh(scores(query, keys[head]), top, values[head])
        grand_total = grand_total + sum_totals(acc)
        acc_out[at, :] = acc
        top_out[at, :] = top

    @pl.when(too_large(grand_total))
    def _():
        for head, at, query, _, _ in chunks(q_ref, kv_heads):
            top, acc = anew(scores(query, keys[head]), top_in[at, :], acc_in[at, :], values[head])
            acc_out[at, :] = acc
            top_out[at, :] = top


def weights_kernel(row, sizes, q_ref, limits, key, top_in, weight_out, keys):
    place_keys(0, 1, row, False, sizes, limits, key, keys)
    for head, at, query, _, _ in chunks(q_ref, keys.shape[0]):
        weight_out[at, :] = weights(scores(query, keys[head]), top_in[at, :])


def last_kernel(row, sizes, q_ref, limits, key, value, weight_in, acc_in, top_in, out, keys, values, result, sems):
    rows, heads = q_ref.shape[0], q_ref.shape[1] // HD
    kv_heads = keys.shape[0]
    place_values(0, 1, row, False, sizes, limits, value, values)

    def sent(base):
        lanes = slice(base * HD, (base + COPY_HEADS) * HD)
        return pltpu.make_async_copy(result.at[:, lanes], out.at[:, lanes], sems.at[base // COPY_HEADS])

    def settle(base, size, acc):
        done = normalised(acc)
        for i in range(size):
            result[:, (base + i) * HD : (base + i + 1) * HD] = done[i * rows : (i + 1) * rows]
        for i in range(0, size, COPY_HEADS):
            sent(base + i).start()

    def wait_all():
        for base in range(0, heads, COPY_HEADS):
            sent(base).wait()

    grand_total = jnp.zeros((8, HD), jnp.float32)
    for head, at, _, base, size in chunks(q_ref, kv_heads, True):
        acc = acc_in[at, :] + jnp.dot(weight_in[at, :], values[head], preferred_element_type=jnp.float32)
        grand_total = grand_total + sum_totals(acc)
        settle(base, size, acc)
    again = too_large(grand_total)
    wait_all()

    @pl.when(again)
    def _():
        place_keys(0, 1, row, False, sizes, limits, key, keys)
        for head, at, query, base, size in chunks(q_ref, kv_heads, True):
            _, acc = anew(scores(query, keys[head]), top_in[at, :], acc_in[at, :], values[head])
            settle(base, size, acc)
        wait_all()


def kernel_options(queries, total_keys, kv_heads):
    rows, width = queries.shape
    return {
        "compiler_params": pltpu.CompilerParams(vmem_limit_bytes=40 * 1024 * 1024),
        "cost_estimate": pl.CostEstimate(
            flops=6 * rows * width * total_keys,
            bytes_accessed=2 * rows * width,
            transcendentals=rows * (width // HD) * total_keys,
        ),
    }


def room(kv_heads, total_keys):
    return [
        pltpu.VMEM((kv_heads, total_keys, HD), jnp.bfloat16),
        pltpu.VMEM((kv_heads, total_keys, 2 * HD), jnp.bfloat16),
    ]


def state_shapes(queries):
    rows = queries.shape[0] * queries.shape[1] // HD
    return [jax.ShapeDtypeStruct((rows, 2 * HD), jnp.float32), jax.ShapeDtypeStruct((rows, HD), jnp.float32)]


def attend_first(count, sizes, queries, limits, own_keys, own_values):
    kv_heads = own_keys.shape[1] // HD
    total_keys = -(-sum(sizes) // HD) * HD
    vmem = pl.BlockSpec(memory_space=pltpu.VMEM)
    return tuple(
        pl.pallas_call(
            functools.partial(first_kernel, count, sizes),
            out_shape=state_shapes(queries),
            in_specs=[vmem] * 4,
            out_specs=[vmem] * 2,
            scratch_shapes=room(kv_heads, total_keys),
            name="attend_first",
            **kernel_options(queries, total_keys, kv_heads),
        )(queries, limits, own_keys, own_values)
    )


def attend_next(pieces, state, sizes, queries, limits):
    rows_of = tuple(piece[0] for piece in pieces)
    blocks = [block for piece in pieces for block in piece[1:]]
    kv_heads = blocks[0].shape[1] // HD
    total_keys = -(-len(pieces) * sum(sizes) // HD) * HD
    vmem = pl.BlockSpec(memory_space=pltpu.VMEM)
    operands = [queries, limits, *blocks, *state]
    return tuple(
        pl.pallas_call(
            functools.partial(next_kernel, rows_of, sizes),
            out_shape=state_shapes(queries),
            in_specs=[vmem] * len(operands),
            out_specs=[vmem] * 2,
            scratch_shapes=room(kv_heads, total_keys),
            name="attend_next",
            **kernel_options(queries, total_keys, kv_heads),
        )(*operands)
    )


def attend_last(piece, state, sizes, queries, limits):
    row, key, value = piece
    kv_heads = key.shape[1] // HD
    total_keys = -(-sum(sizes) // HD) * HD
    copies = queries.shape[1] // HD // COPY_HEADS
    vmem = pl.BlockSpec(memory_space=pltpu.VMEM)
    options = kernel_options(queries, total_keys, kv_heads)
    weight = pl.pallas_call(
        functools.partial(weights_kernel, row, sizes),
        out_shape=jax.ShapeDtypeStruct((state[1].shape[0], total_keys), jnp.bfloat16),
        in_specs=[vmem] * 4,
        out_specs=vmem,
        scratch_shapes=room(kv_heads, total_keys)[:1],
        name="attend_weights",
        **options,
    )(queries, limits, key, state[1])
    return pl.pallas_call(
        functools.partial(last_kernel, row, sizes),
        out_shape=jax.ShapeDtypeStruct(queries.shape, queries.dtype),
        in_specs=[vmem] * 7,
        out_specs=pl.BlockSpec(memory_space=pltpu.HBM),
        scratch_shapes=[
            *room(kv_heads, total_keys),
            pltpu.VMEM(queries.shape, queries.dtype),
            pltpu.SemaphoreType.DMA((copies,)),
        ],
        name="attend_last",
        **options,
    )(queries, limits, key, value, weight, *state)


def shards(count, queries, win_keys, win_values, cache_keys, cache_values, valid_counts, first_block):
    sizes = (win_keys.shape[0], cache_keys.shape[0])
    half = count // 2
    ring = [place_at(p, count) for p in range(count)]
    onward = [(ring[p], ring[(p - 1) % count]) for p in range(count)]
    backward = [(b, a) for a, b in onward]

    win_keys, win_values, cache_keys, cache_values, valid_counts, first_block, queries = [
        pltpu.with_memory_space_constraint(x, pltpu.HBM)
        for x in (win_keys, win_values, cache_keys, cache_values, valid_counts, first_block, queries)
    ]
    own_keys, own_values, near, limits = load(
        count, win_keys, win_values, cache_keys, cache_values, queries, valid_counts, first_block
    )
    key_on = key_back = own_keys
    value_on = value_back = own_values
    state = attend_first(count, sizes, near, limits, own_keys, own_values)
    arrived = []
    for step in range(1, half + 1):
        key_on = lax.ppermute(key_on, "ctx", onward)
        value_back = lax.ppermute(value_back, "ctx", backward)
        if step < half:
            if step > 2:
                state = attend_next(arrived[step - 3], state, sizes, near, limits)
                value_on, top = lax.optimization_barrier((value_on, state[1]))
                state = (state[0], top)
            value_on = lax.ppermute(value_on, "ctx", onward)
            key_back = lax.ppermute(key_back, "ctx", backward)
            row = 2 * (step - 1)
            arrived.append([(row, key_on, value_on), (row + 1, key_back, value_back)])
        else:
            arrived.append([(2 * (half - 1), key_on, value_back)])
        if step == 1:
            key_on, top = lax.optimization_barrier((key_on, state[1]))
            state = (state[0], top)
    for pieces in arrived[max(half - 3, 0) : half - 1]:
        state = attend_next(pieces, state, sizes, near, limits)
    return attend_last(arrived[half - 1][0], state, sizes, near, limits)


def solution(mesh):
    in_specs = (
        P(("groups", "ctx"), "tp"),
        P(("groups", "ctx"), "tp"),
        P(("groups", "ctx"), "tp"),
        P(("groups", "ctx"), "tp"),
        P(("groups", "ctx"), "tp"),
        P("groups"),
        P("groups"),
    )
    out_specs = P(("groups", "ctx"), "tp")
    return jax.shard_map(
        functools.partial(shards, mesh.shape["ctx"]),
        mesh=mesh,
        in_specs=in_specs,
        out_specs=out_specs,
        check_vma=False,
    )
```

```python
import functools
import math

import jax
import jax.numpy as jnp
from jax import lax
from jax.experimental import pallas as pl
from jax.experimental.pallas import tpu as pltpu
from jax.sharding import PartitionSpec as P

HD = 128
EXP_SCALE = HD**-0.5 * math.log2(math.e)
HIDDEN = -1.0e30
CHUNK_HEADS = 4
COPY_HEADS = 2
LARGEST_TOTAL = 2.0**100


def ring_width(count):
    width = round(count ** (1 / 3))
    if width > 1 and count % width == 0 and (count // width) % 2 == 0:
        return width
    return 1


def place_at(position, count):
    width = ring_width(count)
    if width == 1:
        return position
    rows = count // width
    row, step = position // (width - 1), position % (width - 1)
    forth = row * width + 1 + step
    back = row * width + width - 1 - step
    home = (rows - 1 - (position - rows * (width - 1))) * width
    if isinstance(position, int):
        return home if position >= rows * (width - 1) else (back if row % 2 else forth)
    return jnp.where(position >= rows * (width - 1), home, jnp.where(row % 2 == 1, back, forth))


def position_of(place, count):
    width = ring_width(count)
    if width == 1:
        return place
    rows = count // width
    row, column = place // width, place % width
    snake = row * (width - 1) + jnp.where(row % 2 == 1, width - 1 - column, column - 1)
    return jnp.where(column == 0, rows * (width - 1) + rows - 1 - row, snake)


def load_kernel(count, win_keys, win_values, cache_keys, cache_values, q_hbm, valid_hbm, first_hbm, *refs):
    keys, values, q_ref, limits, valid_ref, first_ref, sems = refs
    window_rows = win_keys.shape[0]
    pairs = [
        (valid_hbm, valid_ref),
        (first_hbm, first_ref),
        (q_hbm, q_ref),
        (win_keys, keys.at[:window_rows]),
        (cache_keys, keys.at[window_rows:]),
        (win_values, values.at[:window_rows]),
        (cache_values, values.at[window_rows:]),
    ]
    copies = [pltpu.make_async_copy(*pair, sems.at[index]) for index, pair in enumerate(pairs)]
    for copy in copies:
        copy.start()
    for copy in copies[:2]:
        copy.wait()
    me = lax.axis_index("ctx")
    position = position_of(me, count)
    first = first_ref[me]
    for row, offset in enumerate(ring_offsets(count)):
        place = place_at(lax.rem(position + offset + count, count), count)
        limit = jnp.where((place >= first) & (place <= me), valid_ref[place], 0)
        limits[row : row + 1, :] = jnp.full((1, HD), limit, jnp.int32)
    limits[count - 1 : count, :] = jnp.full((1, HD), valid_ref[me], jnp.int32)
    for copy in copies[2:]:
        copy.wait()


def load(count, win_keys, win_values, cache_keys, cache_values, queries, valid_counts, first_block):
    rows, width = win_keys.shape[0] + cache_keys.shape[0], win_keys.shape[1]
    return pl.pallas_call(
        functools.partial(load_kernel, count),
        out_shape=[
            jax.ShapeDtypeStruct((rows, width), win_keys.dtype),
            jax.ShapeDtypeStruct((rows, width), win_keys.dtype),
            jax.ShapeDtypeStruct(queries.shape, queries.dtype),
            jax.ShapeDtypeStruct((-(-count // 8) * 8, HD), jnp.int32),
        ],
        in_specs=[pl.BlockSpec(memory_space=pltpu.HBM)] * 7,
        out_specs=[pl.BlockSpec(memory_space=pltpu.VMEM)] * 4,
        scratch_shapes=[
            pltpu.SMEM(valid_counts.shape, jnp.int32),
            pltpu.SMEM(first_block.shape, jnp.int32),
            pltpu.SemaphoreType.DMA((7,)),
        ],
        compiler_params=pltpu.CompilerParams(vmem_limit_bytes=4 * 1024 * 1024),
        cost_estimate=pl.CostEstimate(flops=0, bytes_accessed=8 * rows * width, transcendentals=0),
        name="load",
    )(win_keys, win_values, cache_keys, cache_values, queries, valid_counts, first_block)


def ring_offsets(count):
    half = count // 2
    return [sign * step for step in range(1, half) for sign in (1, -1)] + [half]


def place_keys(index, number, limit_row, own, sizes, limits, key, keys):
    window_rows, cache_rows = sizes
    at = slice(index * window_rows, (index + 1) * window_rows)
    cache_at = number * window_rows + index * cache_rows
    if not own:
        row_iota = lax.broadcasted_iota(jnp.int32, (window_rows, HD), 0)
        shown = row_iota < limits[limit_row : limit_row + 1, :]
    for head in range(keys.shape[0]):
        lanes = slice(head * HD, (head + 1) * HD)
        win_key = key[:window_rows, lanes]
        if not own:
            fill = key[window_rows : window_rows + 1, lanes].astype(jnp.float32)
            win_key = jnp.where(shown, win_key.astype(jnp.float32), fill).astype(jnp.bfloat16)
        keys[head, at, :] = win_key
        keys[head, cache_at : cache_at + cache_rows, :] = key[window_rows:, lanes]
        spare = keys.shape[1] - number * sum(sizes)
        if spare and index == 0:
            row = key[window_rows : window_rows + 1, lanes].astype(jnp.float32)
            keys[head, keys.shape[1] - spare :, :] = jnp.broadcast_to(row, (spare, HD)).astype(jnp.bfloat16)


def place_values(index, number, limit_row, own, sizes, limits, value, values):
    window_rows, cache_rows = sizes
    at = slice(index * window_rows, (index + 1) * window_rows)
    cache_at = number * window_rows + index * cache_rows
    if not own:
        row_iota = lax.broadcasted_iota(jnp.int32, (window_rows, HD), 0)
        shown = row_iota < limits[limit_row : limit_row + 1, :]
    for head in range(values.shape[0]):
        lanes = slice(head * HD, (head + 1) * HD)
        win_value, ones = value[:window_rows, lanes], jnp.ones((window_rows, HD), jnp.bfloat16)
        if not own:
            win_value = jnp.where(shown, win_value.astype(jnp.float32), 0.0).astype(jnp.bfloat16)
            ones = jnp.where(shown, 1.0, 0.0).astype(jnp.bfloat16)
        values[head, at, :HD] = win_value
        values[head, at, HD:] = ones
        values[head, cache_at : cache_at + cache_rows, :HD] = value[window_rows:, lanes]
        values[head, cache_at : cache_at + cache_rows, HD:] = jnp.ones((cache_rows, HD), jnp.bfloat16)
        spare = values.shape[1] - number * sum(sizes)
        if spare and index == 0:
            values[head, values.shape[1] - spare :, :] = jnp.zeros((spare, 2 * HD), jnp.bfloat16)


def place_block(index, number, limit_row, own, sizes, limits, key, value, keys, values):
    place_keys(index, number, limit_row, own, sizes, limits, key, keys)
    place_values(index, number, limit_row, own, sizes, limits, value, values)


def scores(query, keys):
    return lax.dot_general(query, keys, (((1,), (1,)), ((), ())), preferred_element_type=jnp.float32)


def weights(score, top):
    lanes = score.shape[1] // HD
    return jnp.exp2(score * EXP_SCALE - jnp.concatenate([top] * lanes, axis=1))


def weigh(score, top, values):
    return jnp.dot(weights(score, top).astype(jnp.bfloat16), values, preferred_element_type=jnp.float32)


def wide_top(score):
    return jnp.broadcast_to(jnp.max(score, axis=1, keepdims=True) * EXP_SCALE, (score.shape[0], HD))


def inverse_of(total):
    inverse = pl.reciprocal(total, approx=True)
    return inverse * (2.0 - total * inverse)


def chunks(q_ref, kv_heads, fine_end=False):
    rows = q_ref.shape[0]
    group = q_ref.shape[1] // HD // kv_heads
    sizes = [CHUNK_HEADS] * (kv_heads * group // CHUNK_HEADS)
    if fine_end:
        sizes[-1:] = [CHUNK_HEADS // 2] * 2
    base = 0
    for size in sizes:
        query = None
        if not fine_end:
            query = jnp.concatenate([q_ref[:, (base + i) * HD : (base + i + 1) * HD] for i in range(size)], axis=0)
        yield base // group, slice(base * rows, (base + size) * rows), query, base, size
        base += size


def first_kernel(count, sizes, q_ref, limits, own_keys, own_values, acc_out, top_out, keys, values):
    window_rows = sizes[0]
    place_block(0, 1, 0, True, sizes, None, own_keys, own_values, keys, values)
    rows = q_ref.shape[0]
    key_iota = lax.broadcasted_iota(jnp.int32, (rows, window_rows), 1)
    query_iota = lax.broadcasted_iota(jnp.int32, (rows, window_rows), 0)
    seen = (key_iota <= query_iota) & (key_iota < limits[count - 1 : count, :])
    bias = jnp.concatenate([jnp.where(seen, 0.0, HIDDEN)] * CHUNK_HEADS, axis=0)
    for head, at, query, _, _ in chunks(q_ref, keys.shape[0]):
        score = scores(query, keys[head])
        score = jnp.concatenate([score[:, :window_rows] + bias, score[:, window_rows:]], axis=1)
        top = wide_top(score)
        acc_out[at, :] = weigh(score, top, values[head])
        top_out[at, :] = top


def too_large(grand_total):
    return jnp.min(jnp.where(grand_total < LARGEST_TOTAL, 1.0, 0.0)) < 0.5


def sum_totals(acc):
    return jnp.sum(acc[:, HD:].reshape(-1, 8, HD), axis=0)


def anew(score, before, acc, values):
    top = jnp.maximum(before, wide_top(score))
    fade = jnp.exp2(before - top)
    return top, acc * jnp.concatenate([fade, fade], axis=1) + weigh(score, top, values)


def next_kernel(rows_of, count, sizes, q_ref, limits, *refs):
    number = len(rows_of)
    key_refs, value_refs = refs[: 2 * number : 2], refs[1 : 2 * number : 2]
    acc_in, top_in, acc_out, top_out, keys, values = refs[2 * number :]
    kv_heads = keys.shape[0]
    for index, row in enumerate(rows_of):
        place_block(index, number, row, False, sizes, limits, key_refs[index], value_refs[index], keys, values)

    def take_in(begin):
        grand_total = jnp.zeros((8, HD), jnp.float32)
        for head, at, query, _, _ in chunks(q_ref, kv_heads):
            top = top_in[at, :]
            acc = acc_in[at, :] + weigh(scores(query, keys[head, begin:]), top, values[head, begin:])
            grand_total = grand_total + sum_totals(acc)
            acc_out[at, :] = acc
            top_out[at, :] = top

        @pl.when(too_large(grand_total))
        def _():
            for head, at, query, _, _ in chunks(q_ref, kv_heads):
                score = scores(query, keys[head, begin:])
                top, acc = anew(score, top_in[at, :], acc_in[at, :], values[head, begin:])
                acc_out[at, :] = acc
                top_out[at, :] = top

    if number < 4:
        take_in(0)
        return
    me = lax.axis_index("ctx")
    position = position_of(me, count)
    offsets = ring_offsets(count)
    places = [place_at(lax.rem(position + offsets[row] + count, count), count) for row in rows_of]
    earlier = functools.reduce(jnp.logical_or, [place < me for place in places])

    @pl.when(earlier)
    def _():
        take_in(0)

    @pl.when(jnp.logical_not(earlier))
    def _():
        take_in(number * sizes[0])


def weights_kernel(row, sizes, q_ref, limits, key, acc_in, top_in, weight_out, acc_out, keys, shown):
    place_keys(0, 1, row, False, sizes, limits, key, keys)
    window_rows, cache_rows = sizes
    row_iota = lax.broadcasted_iota(jnp.int32, (window_rows, HD), 0)
    shown[:window_rows, :] = jnp.where(row_iota < limits[row : row + 1, :], 1.0, 0.0).astype(jnp.bfloat16)
    shown[window_rows : window_rows + cache_rows, :] = jnp.ones((cache_rows, HD), jnp.bfloat16)
    spare = shown.shape[0] - sum(sizes)
    if spare:
        shown[sum(sizes) :, :] = jnp.zeros((spare, HD), jnp.bfloat16)

    def settle(at, score, top, acc):
        weight = weights(score, top)
        added = jnp.dot(weight.astype(jnp.bfloat16), shown[...], preferred_element_type=jnp.float32)
        total = acc[:, HD:] + added
        inverse = inverse_of(total)
        acc_out[at, :] = acc[:, :HD] * inverse
        lanes = score.shape[1] // HD
        weight_out[at, :] = (weight * jnp.concatenate([inverse] * lanes, axis=1)).astype(jnp.bfloat16)
        return jnp.sum(total.reshape(-1, 8, HD), axis=0)

    grand_total = jnp.zeros((8, HD), jnp.float32)
    for head, at, query, _, _ in chunks(q_ref, keys.shape[0]):
        grand_total = grand_total + settle(at, scores(query, keys[head]), top_in[at, :], acc_in[at, :])

    @pl.when(too_large(grand_total))
    def _():
        for head, at, query, _, _ in chunks(q_ref, keys.shape[0]):
            score, before = scores(query, keys[head]), top_in[at, :]
            top = jnp.maximum(before, wide_top(score))
            fade = jnp.exp2(before - top)
            settle(at, score, top, acc_in[at, :] * jnp.concatenate([fade, fade], axis=1))


def last_kernel(row, sizes, limits, value, weight_in, acc_in, out, values, result, sems):
    rows, heads = result.shape[0], result.shape[1] // HD
    kv_heads = values.shape[0]
    place_values(0, 1, row, False, sizes, limits, value, values)

    def sent(base):
        lanes = slice(base * HD, (base + COPY_HEADS) * HD)
        return pltpu.make_async_copy(result.at[:, lanes], out.at[:, lanes], sems.at[base // COPY_HEADS])

    for head, at, _, base, size in chunks(result, kv_heads, True):
        added = jnp.dot(weight_in[at, :], values[head, :, :HD], preferred_element_type=jnp.float32)
        done = (acc_in[at, :] + added).astype(jnp.bfloat16)
        for i in range(size):
            result[:, (base + i) * HD : (base + i + 1) * HD] = done[i * rows : (i + 1) * rows]
        for i in range(0, size, COPY_HEADS):
            sent(base + i).start()
    for base in range(0, heads, COPY_HEADS):
        sent(base).wait()


def kernel_options(queries, total_keys, kv_heads):
    rows, width = queries.shape
    return {
        "compiler_params": pltpu.CompilerParams(vmem_limit_bytes=40 * 1024 * 1024),
        "cost_estimate": pl.CostEstimate(
            flops=6 * rows * width * total_keys,
            bytes_accessed=2 * rows * width,
            transcendentals=rows * (width // HD) * total_keys,
        ),
    }


def room(kv_heads, total_keys):
    return [
        pltpu.VMEM((kv_heads, total_keys, HD), jnp.bfloat16),
        pltpu.VMEM((kv_heads, total_keys, 2 * HD), jnp.bfloat16),
    ]


def state_shapes(queries):
    rows = queries.shape[0] * queries.shape[1] // HD
    return [jax.ShapeDtypeStruct((rows, 2 * HD), jnp.float32), jax.ShapeDtypeStruct((rows, HD), jnp.float32)]


def attend_first(count, sizes, queries, limits, own_keys, own_values):
    kv_heads = own_keys.shape[1] // HD
    total_keys = -(-sum(sizes) // HD) * HD
    vmem = pl.BlockSpec(memory_space=pltpu.VMEM)
    return tuple(
        pl.pallas_call(
            functools.partial(first_kernel, count, sizes),
            out_shape=state_shapes(queries),
            in_specs=[vmem] * 4,
            out_specs=[vmem] * 2,
            scratch_shapes=room(kv_heads, total_keys),
            name="attend_first",
            **kernel_options(queries, total_keys, kv_heads),
        )(queries, limits, own_keys, own_values)
    )


def attend_next(pieces, state, count, sizes, queries, limits):
    rows_of = tuple(piece[0] for piece in pieces)
    blocks = [block for piece in pieces for block in piece[1:]]
    kv_heads = blocks[0].shape[1] // HD
    total_keys = -(-len(pieces) * sum(sizes) // HD) * HD
    vmem = pl.BlockSpec(memory_space=pltpu.VMEM)
    operands = [queries, limits, *blocks, *state]
    return tuple(
        pl.pallas_call(
            functools.partial(next_kernel, rows_of, count, sizes),
            out_shape=state_shapes(queries),
            in_specs=[vmem] * len(operands),
            out_specs=[vmem] * 2,
            scratch_shapes=room(kv_heads, total_keys),
            name="attend_next",
            **kernel_options(queries, total_keys, kv_heads),
        )(*operands)
    )


def attend_last(piece, state, sizes, queries, limits):
    row, key, value = piece
    kv_heads = key.shape[1] // HD
    total_keys = -(-sum(sizes) // HD) * HD
    copies = queries.shape[1] // HD // COPY_HEADS
    vmem = pl.BlockSpec(memory_space=pltpu.VMEM)
    options = kernel_options(queries, total_keys, kv_heads)
    acc, top = state
    weight, acc = pl.pallas_call(
        functools.partial(weights_kernel, row, sizes),
        out_shape=[
            jax.ShapeDtypeStruct((top.shape[0], total_keys), jnp.bfloat16),
            jax.ShapeDtypeStruct((top.shape[0], HD), jnp.float32),
        ],
        in_specs=[vmem] * 5,
        out_specs=[vmem] * 2,
        scratch_shapes=[room(kv_heads, total_keys)[0], pltpu.VMEM((total_keys, HD), jnp.bfloat16)],
        name="attend_weights",
        **options,
    )(queries, limits, key, acc, top)
    return pl.pallas_call(
        functools.partial(last_kernel, row, sizes),
        out_shape=jax.ShapeDtypeStruct(queries.shape, queries.dtype),
        in_specs=[vmem] * 4,
        out_specs=pl.BlockSpec(memory_space=pltpu.HBM),
        scratch_shapes=[
            room(kv_heads, total_keys)[1],
            pltpu.VMEM(queries.shape, queries.dtype),
            pltpu.SemaphoreType.DMA((copies,)),
        ],
        name="attend_last",
        **options,
    )(limits, value, weight, acc)


def shards(count, queries, win_keys, win_values, cache_keys, cache_values, valid_counts, first_block):
    sizes = (win_keys.shape[0], cache_keys.shape[0])
    half = count // 2
    ring = [place_at(p, count) for p in range(count)]
    onward = [(ring[p], ring[(p - 1) % count]) for p in range(count)]
    backward = [(b, a) for a, b in onward]

    win_keys, win_values, cache_keys, cache_values, valid_counts, first_block, queries = [
        pltpu.with_memory_space_constraint(x, pltpu.HBM)
        for x in (win_keys, win_values, cache_keys, cache_values, valid_counts, first_block, queries)
    ]
    own_keys, own_values, near, limits = load(
        count, win_keys, win_values, cache_keys, cache_values, queries, valid_counts, first_block
    )
    key_on = key_back = own_keys
    value_on = value_back = own_values
    state = attend_first(count, sizes, near, limits, own_keys, own_values)
    arrived = []
    for step in range(1, half + 1):
        key_on = lax.ppermute(key_on, "ctx", onward)
        value_back = lax.ppermute(value_back, "ctx", backward)
        if step < half:
            value_on = lax.ppermute(value_on, "ctx", onward)
            key_back = lax.ppermute(key_back, "ctx", backward)
            row = 2 * (step - 1)
            arrived.append([(row, key_on, value_on), (row + 1, key_back, value_back)])
        else:
            arrived.append([(2 * (half - 1), key_on, value_back)])
        if step == 1:
            key_on, top = lax.optimization_barrier((key_on, state[1]))
            state = (state[0], top)
    for begin in range(0, half - 2, 2):
        pieces = [piece for step in arrived[begin : min(begin + 2, half - 2)] for piece in step]
        state = attend_next(pieces, state, count, sizes, near, limits)
    state = attend_next(arrived[half - 2], state, count, sizes, near, limits)
    return attend_last(arrived[half - 1][0], state, sizes, near, limits)


def solution(mesh):
    in_specs = (
        P(("groups", "ctx"), "tp"),
        P(("groups", "ctx"), "tp"),
        P(("groups", "ctx"), "tp"),
        P(("groups", "ctx"), "tp"),
        P(("groups", "ctx"), "tp"),
        P("groups"),
        P("groups"),
    )
    out_specs = P(("groups", "ctx"), "tp")
    return jax.shard_map(
        functools.partial(shards, mesh.shape["ctx"]),
        mesh=mesh,
        in_specs=in_specs,
        out_specs=out_specs,
        check_vma=False,
    )
```

```python
import functools
import math

import jax
import jax.numpy as jnp
from jax import lax
from jax.experimental import pallas as pl
from jax.experimental.pallas import tpu as pltpu
from jax.sharding import PartitionSpec as P

HD = 128
EXP_SCALE = HD**-0.5 * math.log2(math.e)
HIDDEN = -1.0e30
CHUNK_HEADS = 4
COPY_HEADS = 4
LARGEST_TOTAL = 2.0**100


def ring_width(count):
    width = round(count ** (1 / 3))
    if width > 1 and count % width == 0 and (count // width) % 2 == 0:
        return width
    return 1


def place_at(position, count):
    width = ring_width(count)
    if width == 1:
        return position
    rows = count // width
    row, step = position // (width - 1), position % (width - 1)
    forth = row * width + 1 + step
    back = row * width + width - 1 - step
    home = (rows - 1 - (position - rows * (width - 1))) * width
    if isinstance(position, int):
        return home if position >= rows * (width - 1) else (back if row % 2 else forth)
    return jnp.where(position >= rows * (width - 1), home, jnp.where(row % 2 == 1, back, forth))


def position_of(place, count):
    width = ring_width(count)
    if width == 1:
        return place
    rows = count // width
    row, column = place // width, place % width
    snake = row * (width - 1) + jnp.where(row % 2 == 1, width - 1 - column, column - 1)
    return jnp.where(column == 0, rows * (width - 1) + rows - 1 - row, snake)


def load_kernel(count, win_keys, win_values, cache_keys, cache_values, q_hbm, valid_hbm, first_hbm, *refs):
    keys, values, q_ref, limits, valid_ref, first_ref, sems = refs
    window_rows = win_keys.shape[0]
    pairs = [
        (valid_hbm, valid_ref),
        (first_hbm, first_ref),
        (q_hbm, q_ref),
        (win_keys, keys.at[:window_rows]),
        (cache_keys, keys.at[window_rows:]),
        (win_values, values.at[:window_rows]),
        (cache_values, values.at[window_rows:]),
    ]
    copies = [pltpu.make_async_copy(*pair, sems.at[index]) for index, pair in enumerate(pairs)]
    for copy in copies:
        copy.start()
    for copy in copies[:2]:
        copy.wait()
    me = lax.axis_index("ctx")
    position = position_of(me, count)
    first = first_ref[me]
    for row, offset in enumerate(ring_offsets(count)):
        place = place_at(lax.rem(position + offset + count, count), count)
        limit = jnp.where((place >= first) & (place <= me), valid_ref[place], 0)
        limits[row : row + 1, :] = jnp.full((1, HD), limit, jnp.int32)
    limits[count - 1 : count, :] = jnp.full((1, HD), valid_ref[me], jnp.int32)
    for copy in copies[2:]:
        copy.wait()


def load(count, win_keys, win_values, cache_keys, cache_values, queries, valid_counts, first_block):
    rows, width = win_keys.shape[0] + cache_keys.shape[0], win_keys.shape[1]
    return pl.pallas_call(
        functools.partial(load_kernel, count),
        out_shape=[
            jax.ShapeDtypeStruct((rows, width), win_keys.dtype),
            jax.ShapeDtypeStruct((rows, width), win_keys.dtype),
            jax.ShapeDtypeStruct(queries.shape, queries.dtype),
            jax.ShapeDtypeStruct((-(-count // 8) * 8, HD), jnp.int32),
        ],
        in_specs=[pl.BlockSpec(memory_space=pltpu.HBM)] * 7,
        out_specs=[pl.BlockSpec(memory_space=pltpu.VMEM)] * 4,
        scratch_shapes=[
            pltpu.SMEM(valid_counts.shape, jnp.int32),
            pltpu.SMEM(first_block.shape, jnp.int32),
            pltpu.SemaphoreType.DMA((7,)),
        ],
        compiler_params=pltpu.CompilerParams(vmem_limit_bytes=4 * 1024 * 1024),
        cost_estimate=pl.CostEstimate(flops=0, bytes_accessed=8 * rows * width, transcendentals=0),
        name="load",
    )(win_keys, win_values, cache_keys, cache_values, queries, valid_counts, first_block)


def ring_offsets(count):
    half = count // 2
    return [sign * step for step in range(1, half) for sign in (1, -1)] + [half]


def place_keys(index, number, limit_row, own, sizes, limits, key, keys):
    window_rows, cache_rows = sizes
    at = slice(index * window_rows, (index + 1) * window_rows)
    cache_at = number * window_rows + index * cache_rows
    if not own:
        row_iota = lax.broadcasted_iota(jnp.int32, (window_rows, HD), 0)
        shown = row_iota < limits[limit_row : limit_row + 1, :]
    for head in range(keys.shape[0]):
        lanes = slice(head * HD, (head + 1) * HD)
        win_key = key[:window_rows, lanes]
        if not own:
            fill = key[window_rows : window_rows + 1, lanes].astype(jnp.float32)
            win_key = jnp.where(shown, win_key.astype(jnp.float32), fill).astype(jnp.bfloat16)
        keys[head, at, :] = win_key
        keys[head, cache_at : cache_at + cache_rows, :] = key[window_rows:, lanes]
        spare = keys.shape[1] - number * sum(sizes)
        if spare and index == 0:
            row = key[window_rows : window_rows + 1, lanes].astype(jnp.float32)
            keys[head, keys.shape[1] - spare :, :] = jnp.broadcast_to(row, (spare, HD)).astype(jnp.bfloat16)


def place_values(index, number, limit_row, own, sizes, limits, value, values):
    window_rows, cache_rows = sizes
    at = slice(index * window_rows, (index + 1) * window_rows)
    cache_at = number * window_rows + index * cache_rows
    if not own:
        row_iota = lax.broadcasted_iota(jnp.int32, (window_rows, HD), 0)
        shown = row_iota < limits[limit_row : limit_row + 1, :]
    for head in range(values.shape[0]):
        lanes = slice(head * HD, (head + 1) * HD)
        win_value, ones = value[:window_rows, lanes], jnp.ones((window_rows, HD), jnp.bfloat16)
        if not own:
            win_value = jnp.where(shown, win_value.astype(jnp.float32), 0.0).astype(jnp.bfloat16)
            ones = jnp.where(shown, 1.0, 0.0).astype(jnp.bfloat16)
        values[head, at, :HD] = win_value
        values[head, at, HD:] = ones
        values[head, cache_at : cache_at + cache_rows, :HD] = value[window_rows:, lanes]
        values[head, cache_at : cache_at + cache_rows, HD:] = jnp.ones((cache_rows, HD), jnp.bfloat16)
        spare = values.shape[1] - number * sum(sizes)
        if spare and index == 0:
            values[head, values.shape[1] - spare :, :] = jnp.zeros((spare, 2 * HD), jnp.bfloat16)


def place_block(index, number, limit_row, own, sizes, limits, key, value, keys, values):
    place_keys(index, number, limit_row, own, sizes, limits, key, keys)
    place_values(index, number, limit_row, own, sizes, limits, value, values)


def scores(query, keys):
    return lax.dot_general(query, keys, (((1,), (1,)), ((), ())), preferred_element_type=jnp.float32)


def weights(score, top):
    lanes = score.shape[1] // HD
    return jnp.exp2(score * EXP_SCALE - jnp.concatenate([top] * lanes, axis=1)).astype(jnp.bfloat16)


def weigh(score, top, values):
    return jnp.dot(weights(score, top), values, preferred_element_type=jnp.float32)


def wide_top(score):
    return jnp.broadcast_to(jnp.max(score, axis=1, keepdims=True) * EXP_SCALE, (score.shape[0], HD))


def normalised(acc):
    total = acc[:, HD:]
    inverse = pl.reciprocal(total, approx=True)
    return (acc[:, :HD] * (inverse * (2.0 - total * inverse))).astype(jnp.bfloat16)


def chunks(q_ref, kv_heads, fine_end=False):
    rows = q_ref.shape[0]
    group = q_ref.shape[1] // HD // kv_heads
    sizes = [CHUNK_HEADS] * (kv_heads * group // CHUNK_HEADS)
    if fine_end:
        sizes[-1:] = [CHUNK_HEADS // 2] * 2
    base = 0
    for size in sizes:
        query = jnp.concatenate([q_ref[:, (base + i) * HD : (base + i + 1) * HD] for i in range(size)], axis=0)
        yield base // group, slice(base * rows, (base + size) * rows), query, base, size
        base += size


def first_kernel(count, sizes, q_ref, limits, own_keys, own_values, acc_out, top_out, keys, values):
    window_rows = sizes[0]
    place_block(0, 1, 0, True, sizes, None, own_keys, own_values, keys, values)
    rows = q_ref.shape[0]
    key_iota = lax.broadcasted_iota(jnp.int32, (rows, window_rows), 1)
    query_iota = lax.broadcasted_iota(jnp.int32, (rows, window_rows), 0)
    seen = (key_iota <= query_iota) & (key_iota < limits[count - 1 : count, :])
    bias = jnp.concatenate([jnp.where(seen, 0.0, HIDDEN)] * CHUNK_HEADS, axis=0)
    for head, at, query, _, _ in chunks(q_ref, keys.shape[0]):
        score = scores(query, keys[head])
        score = jnp.concatenate([score[:, :window_rows] + bias, score[:, window_rows:]], axis=1)
        top = wide_top(score)
        acc_out[at, :] = weigh(score, top, values[head])
        top_out[at, :] = top


def too_large(grand_total):
    return jnp.min(jnp.where(grand_total < LARGEST_TOTAL, 1.0, 0.0)) < 0.5


def sum_totals(acc):
    return jnp.sum(acc[:, HD:].reshape(-1, 8, HD), axis=0)


def anew(score, before, acc, values):
    top = jnp.maximum(before, wide_top(score))
    fade = jnp.exp2(before - top)
    return top, acc * jnp.concatenate([fade, fade], axis=1) + weigh(score, top, values)


def next_kernel(rows_of, count, sizes, q_ref, limits, *refs):
    number = len(rows_of)
    key_refs, value_refs = refs[: 2 * number : 2], refs[1 : 2 * number : 2]
    acc_in, top_in, acc_out, top_out, keys, values = refs[2 * number :]
    kv_heads = keys.shape[0]
    for index, row in enumerate(rows_of):
        place_block(index, number, row, False, sizes, limits, key_refs[index], value_refs[index], keys, values)

    def take_in(begin):
        grand_total = jnp.zeros((8, HD), jnp.float32)
        for head, at, query, _, _ in chunks(q_ref, kv_heads):
            top = top_in[at, :]
            acc = acc_in[at, :] + weigh(scores(query, keys[head, begin:]), top, values[head, begin:])
            grand_total = grand_total + sum_totals(acc)
            acc_out[at, :] = acc
            top_out[at, :] = top

        @pl.when(too_large(grand_total))
        def _():
            for head, at, query, _, _ in chunks(q_ref, kv_heads):
                score = scores(query, keys[head, begin:])
                top, acc = anew(score, top_in[at, :], acc_in[at, :], values[head, begin:])
                acc_out[at, :] = acc
                top_out[at, :] = top

    if number < 4:
        take_in(0)
        return
    me = lax.axis_index("ctx")
    position = position_of(me, count)
    offsets = ring_offsets(count)
    places = [place_at(lax.rem(position + offsets[row] + count, count), count) for row in rows_of]
    earlier = functools.reduce(jnp.logical_or, [place < me for place in places])

    @pl.when(earlier)
    def _():
        take_in(0)

    @pl.when(jnp.logical_not(earlier))
    def _():
        take_in(number * sizes[0])


def weights_kernel(row, sizes, q_ref, limits, key, top_in, weight_out, keys):
    place_keys(0, 1, row, False, sizes, limits, key, keys)
    for head, at, query, _, _ in chunks(q_ref, keys.shape[0]):
        weight_out[at, :] = weights(scores(query, keys[head]), top_in[at, :])


def last_kernel(row, sizes, q_ref, limits, key, value, weight_in, acc_in, top_in, out, keys, values, result, sems):
    rows, heads = q_ref.shape[0], q_ref.shape[1] // HD
    kv_heads = keys.shape[0]
    place_values(0, 1, row, False, sizes, limits, value, values)

    def sent(base):
        lanes = slice(base * HD, (base + COPY_HEADS) * HD)
        return pltpu.make_async_copy(result.at[:, lanes], out.at[:, lanes], sems.at[base // COPY_HEADS])

    def settle(base, size, acc):
        done = normalised(acc)
        for i in range(size):
            result[:, (base + i) * HD : (base + i + 1) * HD] = done[i * rows : (i + 1) * rows]
        for i in range(0, size, COPY_HEADS):
            sent(base + i).start()

    def wait_all():
        for base in range(0, heads, COPY_HEADS):
            sent(base).wait()

    grand_total = jnp.zeros((8, HD), jnp.float32)
    for head, at, _, base, size in chunks(q_ref, kv_heads):
        acc = acc_in[at, :] + jnp.dot(weight_in[at, :], values[head], preferred_element_type=jnp.float32)
        grand_total = grand_total + sum_totals(acc)
        settle(base, size, acc)
    again = too_large(grand_total)
    wait_all()

    @pl.when(again)
    def _():
        place_keys(0, 1, row, False, sizes, limits, key, keys)
        for head, at, query, base, size in chunks(q_ref, kv_heads):
            _, acc = anew(scores(query, keys[head]), top_in[at, :], acc_in[at, :], values[head])
            settle(base, size, acc)
        wait_all()


def kernel_options(queries, total_keys, kv_heads):
    rows, width = queries.shape
    return {
        "compiler_params": pltpu.CompilerParams(vmem_limit_bytes=40 * 1024 * 1024),
        "cost_estimate": pl.CostEstimate(
            flops=6 * rows * width * total_keys,
            bytes_accessed=2 * rows * width,
            transcendentals=rows * (width // HD) * total_keys,
        ),
    }


def room(kv_heads, total_keys):
    return [
        pltpu.VMEM((kv_heads, total_keys, HD), jnp.bfloat16),
        pltpu.VMEM((kv_heads, total_keys, 2 * HD), jnp.bfloat16),
    ]


def state_shapes(queries):
    rows = queries.shape[0] * queries.shape[1] // HD
    return [jax.ShapeDtypeStruct((rows, 2 * HD), jnp.float32), jax.ShapeDtypeStruct((rows, HD), jnp.float32)]


def attend_first(count, sizes, queries, limits, own_keys, own_values):
    kv_heads = own_keys.shape[1] // HD
    total_keys = -(-sum(sizes) // HD) * HD
    vmem = pl.BlockSpec(memory_space=pltpu.VMEM)
    return tuple(
        pl.pallas_call(
            functools.partial(first_kernel, count, sizes),
            out_shape=state_shapes(queries),
            in_specs=[vmem] * 4,
            out_specs=[vmem] * 2,
            scratch_shapes=room(kv_heads, total_keys),
            name="attend_first",
            **kernel_options(queries, total_keys, kv_heads),
        )(queries, limits, own_keys, own_values)
    )


def attend_next(pieces, state, count, sizes, queries, limits):
    rows_of = tuple(piece[0] for piece in pieces)
    blocks = [block for piece in pieces for block in piece[1:]]
    kv_heads = blocks[0].shape[1] // HD
    total_keys = -(-len(pieces) * sum(sizes) // HD) * HD
    vmem = pl.BlockSpec(memory_space=pltpu.VMEM)
    operands = [queries, limits, *blocks, *state]
    return tuple(
        pl.pallas_call(
            functools.partial(next_kernel, rows_of, count, sizes),
            out_shape=state_shapes(queries),
            in_specs=[vmem] * len(operands),
            out_specs=[vmem] * 2,
            scratch_shapes=room(kv_heads, total_keys),
            name="attend_next",
            **kernel_options(queries, total_keys, kv_heads),
        )(*operands)
    )


def attend_last(piece, state, sizes, queries, limits):
    row, key, value = piece
    kv_heads = key.shape[1] // HD
    total_keys = -(-sum(sizes) // HD) * HD
    copies = queries.shape[1] // HD // COPY_HEADS
    vmem = pl.BlockSpec(memory_space=pltpu.VMEM)
    options = kernel_options(queries, total_keys, kv_heads)
    weight = pl.pallas_call(
        functools.partial(weights_kernel, row, sizes),
        out_shape=jax.ShapeDtypeStruct((state[1].shape[0], total_keys), jnp.bfloat16),
        in_specs=[vmem] * 4,
        out_specs=vmem,
        scratch_shapes=room(kv_heads, total_keys)[:1],
        name="attend_weights",
        **options,
    )(queries, limits, key, state[1])
    return pl.pallas_call(
        functools.partial(last_kernel, row, sizes),
        out_shape=jax.ShapeDtypeStruct(queries.shape, queries.dtype),
        in_specs=[vmem] * 7,
        out_specs=pl.BlockSpec(memory_space=pltpu.HBM),
        scratch_shapes=[
            *room(kv_heads, total_keys),
            pltpu.VMEM(queries.shape, queries.dtype),
            pltpu.SemaphoreType.DMA((copies,)),
        ],
        name="attend_last",
        **options,
    )(queries, limits, key, value, weight, *state)


def shards(count, queries, win_keys, win_values, cache_keys, cache_values, valid_counts, first_block):
    sizes = (win_keys.shape[0], cache_keys.shape[0])
    half = count // 2
    ring = [place_at(p, count) for p in range(count)]
    onward = [(ring[p], ring[(p - 1) % count]) for p in range(count)]
    backward = [(b, a) for a, b in onward]

    win_keys, win_values, cache_keys, cache_values, valid_counts, first_block, queries = [
        pltpu.with_memory_space_constraint(x, pltpu.HBM)
        for x in (win_keys, win_values, cache_keys, cache_values, valid_counts, first_block, queries)
    ]
    own_keys, own_values, near, limits = load(
        count, win_keys, win_values, cache_keys, cache_values, queries, valid_counts, first_block
    )
    key_on = key_back = own_keys
    value_on = value_back = own_values
    state = attend_first(count, sizes, near, limits, own_keys, own_values)
    arrived = []
    for step in range(1, half + 1):
        key_on = lax.ppermute(key_on, "ctx", onward)
        value_back = lax.ppermute(value_back, "ctx", backward)
        if step < half:
            value_on = lax.ppermute(value_on, "ctx", onward)
            key_back = lax.ppermute(key_back, "ctx", backward)
            row = 2 * (step - 1)
            arrived.append([(row, key_on, value_on), (row + 1, key_back, value_back)])
        else:
            arrived.append([(2 * (half - 1), key_on, value_back)])
        if step == 1:
            key_on, top = lax.optimization_barrier((key_on, state[1]))
            state = (state[0], top)
    for begin in range(0, half - 2, 2):
        pieces = [piece for step in arrived[begin : min(begin + 2, half - 2)] for piece in step]
        state = attend_next(pieces, state, count, sizes, near, limits)
    state = attend_next(arrived[half - 2], state, count, sizes, near, limits)
    return attend_last(arrived[half - 1][0], state, sizes, near, limits)


def solution(mesh):
    in_specs = (
        P(("groups", "ctx"), "tp"),
        P(("groups", "ctx"), "tp"),
        P(("groups", "ctx"), "tp"),
        P(("groups", "ctx"), "tp"),
        P(("groups", "ctx"), "tp"),
        P("groups"),
        P("groups"),
    )
    out_specs = P(("groups", "ctx"), "tp")
    return jax.shard_map(
        functools.partial(shards, mesh.shape["ctx"]),
        mesh=mesh,
        in_specs=in_specs,
        out_specs=out_specs,
        check_vma=False,
    )
```

```python
import functools
import math

import jax
import jax.numpy as jnp
from jax import lax
from jax.experimental import pallas as pl
from jax.experimental.pallas import tpu as pltpu
from jax.sharding import PartitionSpec as P

HD = 128
EXP_SCALE = HD**-0.5 * math.log2(math.e)
HIDDEN = -1.0e30
CHUNK_HEADS = 4
COPY_HEADS = 2
LARGEST_TOTAL = 2.0**100


def ring_width(count):
    width = round(count ** (1 / 3))
    if width > 1 and count % width == 0 and (count // width) % 2 == 0:
        return width
    return 1


def place_at(position, count):
    width = ring_width(count)
    if width == 1:
        return position
    rows = count // width
    row, step = position // (width - 1), position % (width - 1)
    forth = row * width + 1 + step
    back = row * width + width - 1 - step
    home = (rows - 1 - (position - rows * (width - 1))) * width
    if isinstance(position, int):
        return home if position >= rows * (width - 1) else (back if row % 2 else forth)
    return jnp.where(position >= rows * (width - 1), home, jnp.where(row % 2 == 1, back, forth))


def position_of(place, count):
    width = ring_width(count)
    if width == 1:
        return place
    rows = count // width
    row, column = place // width, place % width
    snake = row * (width - 1) + jnp.where(row % 2 == 1, width - 1 - column, column - 1)
    return jnp.where(column == 0, rows * (width - 1) + rows - 1 - row, snake)


def load_kernel(count, win_keys, win_values, cache_keys, cache_values, q_hbm, valid_hbm, first_hbm, *refs):
    keys, values, q_ref, limits, valid_ref, first_ref, sems = refs
    window_rows = win_keys.shape[0]
    pairs = [
        (valid_hbm, valid_ref),
        (first_hbm, first_ref),
        (q_hbm, q_ref),
        (win_keys, keys.at[:window_rows]),
        (cache_keys, keys.at[window_rows:]),
        (win_values, values.at[:window_rows]),
        (cache_values, values.at[window_rows:]),
    ]
    copies = [pltpu.make_async_copy(*pair, sems.at[index]) for index, pair in enumerate(pairs)]
    for copy in copies:
        copy.start()
    for copy in copies[:2]:
        copy.wait()
    me = lax.axis_index("ctx")
    position = position_of(me, count)
    first = first_ref[me]
    for row, offset in enumerate(ring_offsets(count)):
        place = place_at(lax.rem(position + offset + count, count), count)
        limit = jnp.where((place >= first) & (place <= me), valid_ref[place], 0)
        limits[row : row + 1, :] = jnp.full((1, HD), limit, jnp.int32)
    limits[count - 1 : count, :] = jnp.full((1, HD), valid_ref[me], jnp.int32)
    for copy in copies[2:]:
        copy.wait()


def load(count, win_keys, win_values, cache_keys, cache_values, queries, valid_counts, first_block):
    rows, width = win_keys.shape[0] + cache_keys.shape[0], win_keys.shape[1]
    return pl.pallas_call(
        functools.partial(load_kernel, count),
        out_shape=[
            jax.ShapeDtypeStruct((rows, width), win_keys.dtype),
            jax.ShapeDtypeStruct((rows, width), win_keys.dtype),
            jax.ShapeDtypeStruct(queries.shape, queries.dtype),
            jax.ShapeDtypeStruct((-(-count // 8) * 8, HD), jnp.int32),
        ],
        in_specs=[pl.BlockSpec(memory_space=pltpu.HBM)] * 7,
        out_specs=[pl.BlockSpec(memory_space=pltpu.VMEM)] * 4,
        scratch_shapes=[
            pltpu.SMEM(valid_counts.shape, jnp.int32),
            pltpu.SMEM(first_block.shape, jnp.int32),
            pltpu.SemaphoreType.DMA((7,)),
        ],
        compiler_params=pltpu.CompilerParams(vmem_limit_bytes=4 * 1024 * 1024),
        cost_estimate=pl.CostEstimate(flops=0, bytes_accessed=8 * rows * width, transcendentals=0),
        name="load",
    )(win_keys, win_values, cache_keys, cache_values, queries, valid_counts, first_block)


def ring_offsets(count):
    half = count // 2
    return [sign * step for step in range(1, half) for sign in (1, -1)] + [half]


def place_keys(index, number, limit_row, own, sizes, limits, key, keys):
    window_rows, cache_rows = sizes
    at = slice(index * window_rows, (index + 1) * window_rows)
    cache_at = number * window_rows + index * cache_rows
    if not own:
        row_iota = lax.broadcasted_iota(jnp.int32, (window_rows, HD), 0)
        shown = row_iota < limits[limit_row : limit_row + 1, :]
    for head in range(keys.shape[0]):
        lanes = slice(head * HD, (head + 1) * HD)
        win_key = key[:window_rows, lanes]
        if not own:
            fill = key[window_rows : window_rows + 1, lanes].astype(jnp.float32)
            win_key = jnp.where(shown, win_key.astype(jnp.float32), fill).astype(jnp.bfloat16)
        keys[head, at, :] = win_key
        keys[head, cache_at : cache_at + cache_rows, :] = key[window_rows:, lanes]
        spare = keys.shape[1] - number * sum(sizes)
        if spare and index == 0:
            row = key[window_rows : window_rows + 1, lanes].astype(jnp.float32)
            keys[head, keys.shape[1] - spare :, :] = jnp.broadcast_to(row, (spare, HD)).astype(jnp.bfloat16)


def place_values(index, number, limit_row, own, sizes, limits, value, values):
    window_rows, cache_rows = sizes
    at = slice(index * window_rows, (index + 1) * window_rows)
    cache_at = number * window_rows + index * cache_rows
    if not own:
        row_iota = lax.broadcasted_iota(jnp.int32, (window_rows, HD), 0)
        shown = row_iota < limits[limit_row : limit_row + 1, :]
    for head in range(values.shape[0]):
        lanes = slice(head * HD, (head + 1) * HD)
        win_value, ones = value[:window_rows, lanes], jnp.ones((window_rows, HD), jnp.bfloat16)
        if not own:
            win_value = jnp.where(shown, win_value.astype(jnp.float32), 0.0).astype(jnp.bfloat16)
            ones = jnp.where(shown, 1.0, 0.0).astype(jnp.bfloat16)
        values[head, at, :HD] = win_value
        values[head, at, HD:] = ones
        values[head, cache_at : cache_at + cache_rows, :HD] = value[window_rows:, lanes]
        values[head, cache_at : cache_at + cache_rows, HD:] = jnp.ones((cache_rows, HD), jnp.bfloat16)
        spare = values.shape[1] - number * sum(sizes)
        if spare and index == 0:
            values[head, values.shape[1] - spare :, :] = jnp.zeros((spare, 2 * HD), jnp.bfloat16)


def place_block(index, number, limit_row, own, sizes, limits, key, value, keys, values):
    place_keys(index, number, limit_row, own, sizes, limits, key, keys)
    place_values(index, number, limit_row, own, sizes, limits, value, values)


def scores(query, keys):
    return lax.dot_general(query, keys, (((1,), (1,)), ((), ())), preferred_element_type=jnp.float32)


def weights(score, top):
    lanes = score.shape[1] // HD
    return jnp.exp2(score * EXP_SCALE - jnp.concatenate([top] * lanes, axis=1)).astype(jnp.bfloat16)


def weigh(score, top, values):
    return jnp.dot(weights(score, top), values, preferred_element_type=jnp.float32)


def wide_top(score):
    return jnp.broadcast_to(jnp.max(score, axis=1, keepdims=True) * EXP_SCALE, (score.shape[0], HD))


def normalised(acc):
    total = acc[:, HD:]
    inverse = pl.reciprocal(total, approx=True)
    return (acc[:, :HD] * (inverse * (2.0 - total * inverse))).astype(jnp.bfloat16)


def chunks(q_ref, kv_heads, fine_end=False):
    rows = q_ref.shape[0]
    group = q_ref.shape[1] // HD // kv_heads
    sizes = [CHUNK_HEADS] * (kv_heads * group // CHUNK_HEADS)
    if fine_end:
        sizes[-1:] = [CHUNK_HEADS // 2] * 2
    base = 0
    for size in sizes:
        query = jnp.concatenate([q_ref[:, (base + i) * HD : (base + i + 1) * HD] for i in range(size)], axis=0)
        yield base // group, slice(base * rows, (base + size) * rows), query, base, size
        base += size


def first_kernel(count, sizes, q_ref, limits, own_keys, own_values, acc_out, top_out, keys, values):
    window_rows = sizes[0]
    place_block(0, 1, 0, True, sizes, None, own_keys, own_values, keys, values)
    rows = q_ref.shape[0]
    key_iota = lax.broadcasted_iota(jnp.int32, (rows, window_rows), 1)
    query_iota = lax.broadcasted_iota(jnp.int32, (rows, window_rows), 0)
    seen = (key_iota <= query_iota) & (key_iota < limits[count - 1 : count, :])
    bias = jnp.concatenate([jnp.where(seen, 0.0, HIDDEN)] * CHUNK_HEADS, axis=0)
    for head, at, query, _, _ in chunks(q_ref, keys.shape[0]):
        score = scores(query, keys[head])
        score = jnp.concatenate([score[:, :window_rows] + bias, score[:, window_rows:]], axis=1)
        top = wide_top(score)
        acc_out[at, :] = weigh(score, top, values[head])
        top_out[at, :] = top


def too_large(grand_total):
    return jnp.min(jnp.where(grand_total < LARGEST_TOTAL, 1.0, 0.0)) < 0.5


def sum_totals(acc):
    return jnp.sum(acc[:, HD:].reshape(-1, 8, HD), axis=0)


def anew(score, before, acc, values):
    top = jnp.maximum(before, wide_top(score))
    fade = jnp.exp2(before - top)
    return top, acc * jnp.concatenate([fade, fade], axis=1) + weigh(score, top, values)


def next_kernel(rows_of, count, sizes, q_ref, limits, *refs):
    number = len(rows_of)
    key_refs, value_refs = refs[: 2 * number : 2], refs[1 : 2 * number : 2]
    acc_in, top_in, acc_out, top_out, keys, values = refs[2 * number :]
    kv_heads = keys.shape[0]
    for index, row in enumerate(rows_of):
        place_block(index, number, row, False, sizes, limits, key_refs[index], value_refs[index], keys, values)

    def take_in(begin):
        grand_total = jnp.zeros((8, HD), jnp.float32)
        for head, at, query, _, _ in chunks(q_ref, kv_heads):
            top = top_in[at, :]
            acc = acc_in[at, :] + weigh(scores(query, keys[head, begin:]), top, values[head, begin:])
            grand_total = grand_total + sum_totals(acc)
            acc_out[at, :] = acc
            top_out[at, :] = top

        @pl.when(too_large(grand_total))
        def _():
            for head, at, query, _, _ in chunks(q_ref, kv_heads):
                score = scores(query, keys[head, begin:])
                top, acc = anew(score, top_in[at, :], acc_in[at, :], values[head, begin:])
                acc_out[at, :] = acc
                top_out[at, :] = top

    if number < 3:
        take_in(0)
        return
    me = lax.axis_index("ctx")
    position = position_of(me, count)
    offsets = ring_offsets(count)
    places = [place_at(lax.rem(position + offsets[row] + count, count), count) for row in rows_of]
    earlier = functools.reduce(jnp.logical_or, [place < me for place in places])

    @pl.when(earlier)
    def _():
        take_in(0)

    @pl.when(jnp.logical_not(earlier))
    def _():
        take_in(number * sizes[0])


def weights_kernel(row, sizes, q_ref, limits, key, top_in, weight_out, keys):
    place_keys(0, 1, row, False, sizes, limits, key, keys)
    for head, at, query, _, _ in chunks(q_ref, keys.shape[0]):
        weight_out[at, :] = weights(scores(query, keys[head]), top_in[at, :])


def last_kernel(row, sizes, q_ref, limits, key, value, weight_in, acc_in, top_in, out, keys, values, result, sems):
    rows, heads = q_ref.shape[0], q_ref.shape[1] // HD
    kv_heads = keys.shape[0]
    place_values(0, 1, row, False, sizes, limits, value, values)

    def sent(base):
        lanes = slice(base * HD, (base + COPY_HEADS) * HD)
        return pltpu.make_async_copy(result.at[:, lanes], out.at[:, lanes], sems.at[base // COPY_HEADS])

    def settle(base, size, acc):
        done = normalised(acc)
        for i in range(size):
            result[:, (base + i) * HD : (base + i + 1) * HD] = done[i * rows : (i + 1) * rows]
        for i in range(0, size, COPY_HEADS):
            sent(base + i).start()

    def wait_all():
        for base in range(0, heads, COPY_HEADS):
            sent(base).wait()

    grand_total = jnp.zeros((8, HD), jnp.float32)
    for head, at, _, base, size in chunks(q_ref, kv_heads, True):
        acc = acc_in[at, :] + jnp.dot(weight_in[at, :], values[head], preferred_element_type=jnp.float32)
        grand_total = grand_total + sum_totals(acc)
        settle(base, size, acc)
    again = too_large(grand_total)
    wait_all()

    @pl.when(again)
    def _():
        place_keys(0, 1, row, False, sizes, limits, key, keys)
        for head, at, query, base, size in chunks(q_ref, kv_heads, True):
            _, acc = anew(scores(query, keys[head]), top_in[at, :], acc_in[at, :], values[head])
            settle(base, size, acc)
        wait_all()


def kernel_options(queries, total_keys, kv_heads):
    rows, width = queries.shape
    return {
        "compiler_params": pltpu.CompilerParams(vmem_limit_bytes=40 * 1024 * 1024),
        "cost_estimate": pl.CostEstimate(
            flops=6 * rows * width * total_keys,
            bytes_accessed=2 * rows * width,
            transcendentals=rows * (width // HD) * total_keys,
        ),
    }


def room(kv_heads, total_keys):
    return [
        pltpu.VMEM((kv_heads, total_keys, HD), jnp.bfloat16),
        pltpu.VMEM((kv_heads, total_keys, 2 * HD), jnp.bfloat16),
    ]


def state_shapes(queries):
    rows = queries.shape[0] * queries.shape[1] // HD
    return [jax.ShapeDtypeStruct((rows, 2 * HD), jnp.float32), jax.ShapeDtypeStruct((rows, HD), jnp.float32)]


def attend_first(count, sizes, queries, limits, own_keys, own_values):
    kv_heads = own_keys.shape[1] // HD
    total_keys = -(-sum(sizes) // HD) * HD
    vmem = pl.BlockSpec(memory_space=pltpu.VMEM)
    return tuple(
        pl.pallas_call(
            functools.partial(first_kernel, count, sizes),
            out_shape=state_shapes(queries),
            in_specs=[vmem] * 4,
            out_specs=[vmem] * 2,
            scratch_shapes=room(kv_heads, total_keys),
            name="attend_first",
            **kernel_options(queries, total_keys, kv_heads),
        )(queries, limits, own_keys, own_values)
    )


def attend_next(pieces, state, count, sizes, queries, limits):
    rows_of = tuple(piece[0] for piece in pieces)
    blocks = [block for piece in pieces for block in piece[1:]]
    kv_heads = blocks[0].shape[1] // HD
    total_keys = -(-len(pieces) * sum(sizes) // HD) * HD
    vmem = pl.BlockSpec(memory_space=pltpu.VMEM)
    operands = [queries, limits, *blocks, *state]
    return tuple(
        pl.pallas_call(
            functools.partial(next_kernel, rows_of, count, sizes),
            out_shape=state_shapes(queries),
            in_specs=[vmem] * len(operands),
            out_specs=[vmem] * 2,
            scratch_shapes=room(kv_heads, total_keys),
            name="attend_next",
            **kernel_options(queries, total_keys, kv_heads),
        )(*operands)
    )


def attend_last(piece, state, sizes, queries, limits):
    row, key, value = piece
    kv_heads = key.shape[1] // HD
    total_keys = -(-sum(sizes) // HD) * HD
    copies = queries.shape[1] // HD // COPY_HEADS
    vmem = pl.BlockSpec(memory_space=pltpu.VMEM)
    options = kernel_options(queries, total_keys, kv_heads)
    weight = pl.pallas_call(
        functools.partial(weights_kernel, row, sizes),
        out_shape=jax.ShapeDtypeStruct((state[1].shape[0], total_keys), jnp.bfloat16),
        in_specs=[vmem] * 4,
        out_specs=vmem,
        scratch_shapes=room(kv_heads, total_keys)[:1],
        name="attend_weights",
        **options,
    )(queries, limits, key, state[1])
    return pl.pallas_call(
        functools.partial(last_kernel, row, sizes),
        out_shape=jax.ShapeDtypeStruct(queries.shape, queries.dtype),
        in_specs=[vmem] * 7,
        out_specs=pl.BlockSpec(memory_space=pltpu.HBM),
        scratch_shapes=[
            *room(kv_heads, total_keys),
            pltpu.VMEM(queries.shape, queries.dtype),
            pltpu.SemaphoreType.DMA((copies,)),
        ],
        name="attend_last",
        **options,
    )(queries, limits, key, value, weight, *state)


def shards(count, queries, win_keys, win_values, cache_keys, cache_values, valid_counts, first_block):
    sizes = (win_keys.shape[0], cache_keys.shape[0])
    half = count // 2
    ring = [place_at(p, count) for p in range(count)]
    onward = [(ring[p], ring[(p - 1) % count]) for p in range(count)]
    backward = [(b, a) for a, b in onward]

    win_keys, win_values, cache_keys, cache_values, valid_counts, first_block, queries = [
        pltpu.with_memory_space_constraint(x, pltpu.HBM)
        for x in (win_keys, win_values, cache_keys, cache_values, valid_counts, first_block, queries)
    ]
    own_keys, own_values, near, limits = load(
        count, win_keys, win_values, cache_keys, cache_values, queries, valid_counts, first_block
    )
    key_on = key_back = own_keys
    value_on = value_back = own_values
    state = attend_first(count, sizes, near, limits, own_keys, own_values)
    arrived, pending = [], []
    for step in range(1, half + 1):
        key_on = lax.ppermute(key_on, "ctx", onward)
        value_back = lax.ppermute(value_back, "ctx", backward)
        if step < half:
            if step > 2:
                pending += arrived[step - 3]
                state = attend_next([pending.pop(0)], state, count, sizes, near, limits)
                value_on, top = lax.optimization_barrier((value_on, state[1]))
                state = (state[0], top)
            value_on = lax.ppermute(value_on, "ctx", onward)
            key_back = lax.ppermute(key_back, "ctx", backward)
            row = 2 * (step - 1)
            arrived.append([(row, key_on, value_on), (row + 1, key_back, value_back)])
        else:
            arrived.append([(2 * (half - 1), key_on, value_back)])
        if step == 1:
            key_on, top = lax.optimization_barrier((key_on, state[1]))
            state = (state[0], top)
    if half > 2:
        pending += arrived[half - 3]
    for begin in range(0, len(pending), 4):
        state = attend_next(pending[begin : begin + 4], state, count, sizes, near, limits)
    state = attend_next(arrived[half - 2], state, count, sizes, near, limits)
    return attend_last(arrived[half - 1][0], state, sizes, near, limits)


def solution(mesh):
    in_specs = (
        P(("groups", "ctx"), "tp"),
        P(("groups", "ctx"), "tp"),
        P(("groups", "ctx"), "tp"),
        P(("groups", "ctx"), "tp"),
        P(("groups", "ctx"), "tp"),
        P("groups"),
        P("groups"),
    )
    out_specs = P(("groups", "ctx"), "tp")
    return jax.shard_map(
        functools.partial(shards, mesh.shape["ctx"]),
        mesh=mesh,
        in_specs=in_specs,
        out_specs=out_specs,
        check_vma=False,
    )
```

```python
import functools
import math

import jax
import jax.numpy as jnp
from jax import lax
from jax.experimental import pallas as pl
from jax.experimental.pallas import tpu as pltpu
from jax.sharding import PartitionSpec as P

HD = 128
EXP_SCALE = HD**-0.5 * math.log2(math.e)
HIDDEN = -1.0e30
CHUNK_HEADS = 4
COPY_HEADS = 2
LARGEST_TOTAL = 2.0**100


def ring_width(count):
    width = round(count ** (1 / 3))
    if width > 1 and count % width == 0 and (count // width) % 2 == 0:
        return width
    return 1


def place_at(position, count):
    width = ring_width(count)
    if width == 1:
        return position
    rows = count // width
    row, step = position // (width - 1), position % (width - 1)
    forth = row * width + 1 + step
    back = row * width + width - 1 - step
    home = (rows - 1 - (position - rows * (width - 1))) * width
    if isinstance(position, int):
        return home if position >= rows * (width - 1) else (back if row % 2 else forth)
    return jnp.where(position >= rows * (width - 1), home, jnp.where(row % 2 == 1, back, forth))


def position_of(place, count):
    width = ring_width(count)
    if width == 1:
        return place
    rows = count // width
    row, column = place // width, place % width
    snake = row * (width - 1) + jnp.where(row % 2 == 1, width - 1 - column, column - 1)
    return jnp.where(column == 0, rows * (width - 1) + rows - 1 - row, snake)


def load_kernel(count, win_keys, win_values, cache_keys, cache_values, q_hbm, valid_hbm, first_hbm, *refs):
    keys, values, q_ref, limits, valid_ref, first_ref, sems = refs
    window_rows = win_keys.shape[0]
    pairs = [
        (valid_hbm, valid_ref),
        (first_hbm, first_ref),
        (q_hbm, q_ref),
        (win_keys, keys.at[:window_rows]),
        (cache_keys, keys.at[window_rows:]),
        (win_values, values.at[:window_rows]),
        (cache_values, values.at[window_rows:]),
    ]
    copies = [pltpu.make_async_copy(*pair, sems.at[index]) for index, pair in enumerate(pairs)]
    for copy in copies:
        copy.start()
    for copy in copies[:2]:
        copy.wait()
    me = lax.axis_index("ctx")
    position = position_of(me, count)
    first = first_ref[me]
    for row, offset in enumerate(ring_offsets(count)):
        place = place_at(lax.rem(position + offset + count, count), count)
        limit = jnp.where((place >= first) & (place <= me), valid_ref[place], 0)
        limits[row : row + 1, :] = jnp.full((1, HD), limit, jnp.int32)
    limits[count - 1 : count, :] = jnp.full((1, HD), valid_ref[me], jnp.int32)
    for copy in copies[2:]:
        copy.wait()


def load(count, win_keys, win_values, cache_keys, cache_values, queries, valid_counts, first_block):
    rows, width = win_keys.shape[0] + cache_keys.shape[0], win_keys.shape[1]
    return pl.pallas_call(
        functools.partial(load_kernel, count),
        out_shape=[
            jax.ShapeDtypeStruct((rows, width), win_keys.dtype),
            jax.ShapeDtypeStruct((rows, width), win_keys.dtype),
            jax.ShapeDtypeStruct(queries.shape, queries.dtype),
            jax.ShapeDtypeStruct((-(-count // 8) * 8, HD), jnp.int32),
        ],
        in_specs=[pl.BlockSpec(memory_space=pltpu.HBM)] * 7,
        out_specs=[pl.BlockSpec(memory_space=pltpu.VMEM)] * 4,
        scratch_shapes=[
            pltpu.SMEM(valid_counts.shape, jnp.int32),
            pltpu.SMEM(first_block.shape, jnp.int32),
            pltpu.SemaphoreType.DMA((7,)),
        ],
        compiler_params=pltpu.CompilerParams(vmem_limit_bytes=4 * 1024 * 1024),
        cost_estimate=pl.CostEstimate(flops=0, bytes_accessed=8 * rows * width, transcendentals=0),
        name="load",
    )(win_keys, win_values, cache_keys, cache_values, queries, valid_counts, first_block)


def ring_offsets(count):
    half = count // 2
    return [sign * step for step in range(1, half) for sign in (-1, 1)] + [half]


def place_keys(index, number, limit_row, own, sizes, limits, key, keys):
    window_rows, cache_rows = sizes
    at = slice(index * window_rows, (index + 1) * window_rows)
    cache_at = number * window_rows + index * cache_rows
    if not own:
        row_iota = lax.broadcasted_iota(jnp.int32, (window_rows, HD), 0)
        shown = row_iota < limits[limit_row : limit_row + 1, :]
    for head in range(keys.shape[0]):
        lanes = slice(head * HD, (head + 1) * HD)
        win_key = key[:window_rows, lanes]
        if not own:
            fill = key[window_rows : window_rows + 1, lanes].astype(jnp.float32)
            win_key = jnp.where(shown, win_key.astype(jnp.float32), fill).astype(jnp.bfloat16)
        keys[head, at, :] = win_key
        keys[head, cache_at : cache_at + cache_rows, :] = key[window_rows:, lanes]
        spare = keys.shape[1] - number * sum(sizes)
        if spare and index == 0:
            row = key[window_rows : window_rows + 1, lanes].astype(jnp.float32)
            keys[head, keys.shape[1] - spare :, :] = jnp.broadcast_to(row, (spare, HD)).astype(jnp.bfloat16)


def place_values(index, number, limit_row, own, sizes, limits, value, values):
    window_rows, cache_rows = sizes
    at = slice(index * window_rows, (index + 1) * window_rows)
    cache_at = number * window_rows + index * cache_rows
    if not own:
        row_iota = lax.broadcasted_iota(jnp.int32, (window_rows, HD), 0)
        shown = row_iota < limits[limit_row : limit_row + 1, :]
    for head in range(values.shape[0]):
        lanes = slice(head * HD, (head + 1) * HD)
        win_value, ones = value[:window_rows, lanes], jnp.ones((window_rows, HD), jnp.bfloat16)
        if not own:
            win_value = jnp.where(shown, win_value.astype(jnp.float32), 0.0).astype(jnp.bfloat16)
            ones = jnp.where(shown, 1.0, 0.0).astype(jnp.bfloat16)
        values[head, at, :HD] = win_value
        values[head, at, HD:] = ones
        values[head, cache_at : cache_at + cache_rows, :HD] = value[window_rows:, lanes]
        values[head, cache_at : cache_at + cache_rows, HD:] = jnp.ones((cache_rows, HD), jnp.bfloat16)
        spare = values.shape[1] - number * sum(sizes)
        if spare and index == 0:
            values[head, values.shape[1] - spare :, :] = jnp.zeros((spare, 2 * HD), jnp.bfloat16)


def place_block(index, number, limit_row, own, sizes, limits, key, value, keys, values):
    place_keys(index, number, limit_row, own, sizes, limits, key, keys)
    place_values(index, number, limit_row, own, sizes, limits, value, values)


def scores(query, keys):
    return lax.dot_general(query, keys, (((1,), (1,)), ((), ())), preferred_element_type=jnp.float32)


def weights(score, top):
    lanes = score.shape[1] // HD
    return jnp.exp2(score * EXP_SCALE - jnp.concatenate([top] * lanes, axis=1)).astype(jnp.bfloat16)


def weigh(score, top, values):
    return jnp.dot(weights(score, top), values, preferred_element_type=jnp.float32)


def wide_top(score):
    return jnp.broadcast_to(jnp.max(score, axis=1, keepdims=True) * EXP_SCALE, (score.shape[0], HD))


def normalised(acc):
    total = acc[:, HD:]
    inverse = pl.reciprocal(total, approx=True)
    return (acc[:, :HD] * (inverse * (2.0 - total * inverse))).astype(jnp.bfloat16)


def chunks(q_ref, kv_heads, fine_end=False):
    rows = q_ref.shape[0]
    group = q_ref.shape[1] // HD // kv_heads
    sizes = [CHUNK_HEADS] * (kv_heads * group // CHUNK_HEADS)
    if fine_end:
        sizes[-1:] = [CHUNK_HEADS // 2] * 2
    base = 0
    for size in sizes:
        query = jnp.concatenate([q_ref[:, (base + i) * HD : (base + i + 1) * HD] for i in range(size)], axis=0)
        yield base // group, slice(base * rows, (base + size) * rows), query, base, size
        base += size


def first_kernel(count, sizes, q_ref, limits, own_keys, own_values, acc_out, top_out, keys, values):
    window_rows = sizes[0]
    place_block(0, 1, 0, True, sizes, None, own_keys, own_values, keys, values)
    rows = q_ref.shape[0]
    key_iota = lax.broadcasted_iota(jnp.int32, (rows, window_rows), 1)
    query_iota = lax.broadcasted_iota(jnp.int32, (rows, window_rows), 0)
    seen = (key_iota <= query_iota) & (key_iota < limits[count - 1 : count, :])
    bias = jnp.concatenate([jnp.where(seen, 0.0, HIDDEN)] * CHUNK_HEADS, axis=0)
    for head, at, query, _, _ in chunks(q_ref, keys.shape[0]):
        score = scores(query, keys[head])
        score = jnp.concatenate([score[:, :window_rows] + bias, score[:, window_rows:]], axis=1)
        top = wide_top(score)
        acc_out[at, :] = weigh(score, top, values[head])
        top_out[at, :] = top


def too_large(grand_total):
    return jnp.min(jnp.where(grand_total < LARGEST_TOTAL, 1.0, 0.0)) < 0.5


def sum_totals(acc):
    return jnp.sum(acc[:, HD:].reshape(-1, 8, HD), axis=0)


def anew(score, before, acc, values):
    top = jnp.maximum(before, wide_top(score))
    fade = jnp.exp2(before - top)
    return top, acc * jnp.concatenate([fade, fade], axis=1) + weigh(score, top, values)


def next_kernel(rows_of, count, sizes, q_ref, limits, *refs):
    number = len(rows_of)
    key_refs, value_refs = refs[: 2 * number : 2], refs[1 : 2 * number : 2]
    acc_in, top_in, acc_out, top_out, keys, values = refs[2 * number :]
    kv_heads = keys.shape[0]
    for index, row in enumerate(rows_of):
        place_block(index, number, row, False, sizes, limits, key_refs[index], value_refs[index], keys, values)

    def take_in(begin):
        grand_total = jnp.zeros((8, HD), jnp.float32)
        for head, at, query, _, _ in chunks(q_ref, kv_heads):
            top = top_in[at, :]
            acc = acc_in[at, :] + weigh(scores(query, keys[head, begin:]), top, values[head, begin:])
            grand_total = grand_total + sum_totals(acc)
            acc_out[at, :] = acc
            top_out[at, :] = top

        @pl.when(too_large(grand_total))
        def _():
            for head, at, query, _, _ in chunks(q_ref, kv_heads):
                score = scores(query, keys[head, begin:])
                top, acc = anew(score, top_in[at, :], acc_in[at, :], values[head, begin:])
                acc_out[at, :] = acc
                top_out[at, :] = top

    if number < 4:
        take_in(0)
        return
    me = lax.axis_index("ctx")
    position = position_of(me, count)
    offsets = ring_offsets(count)
    places = [place_at(lax.rem(position + offsets[row] + count, count), count) for row in rows_of]
    earlier = functools.reduce(jnp.logical_or, [place < me for place in places])

    @pl.when(earlier)
    def _():
        take_in(0)

    @pl.when(jnp.logical_not(earlier))
    def _():
        take_in(number * sizes[0])


def weights_kernel(row, sizes, q_ref, limits, key, top_in, weight_out, keys):
    place_keys(0, 1, row, False, sizes, limits, key, keys)
    for head, at, query, _, _ in chunks(q_ref, keys.shape[0]):
        weight_out[at, :] = weights(scores(query, keys[head]), top_in[at, :])


def last_kernel(row, sizes, q_ref, limits, key, value, weight_in, acc_in, top_in, out, keys, values, result, sems):
    rows, heads = q_ref.shape[0], q_ref.shape[1] // HD
    kv_heads = keys.shape[0]
    place_values(0, 1, row, False, sizes, limits, value, values)

    def sent(base):
        lanes = slice(base * HD, (base + COPY_HEADS) * HD)
        return pltpu.make_async_copy(result.at[:, lanes], out.at[:, lanes], sems.at[base // COPY_HEADS])

    def settle(base, size, acc):
        done = normalised(acc)
        for i in range(size):
            result[:, (base + i) * HD : (base + i + 1) * HD] = done[i * rows : (i + 1) * rows]
        for i in range(0, size, COPY_HEADS):
            sent(base + i).start()

    def wait_all():
        for base in range(0, heads, COPY_HEADS):
            sent(base).wait()

    grand_total = jnp.zeros((8, HD), jnp.float32)
    for head, at, _, base, size in chunks(q_ref, kv_heads, True):
        acc = acc_in[at, :] + jnp.dot(weight_in[at, :], values[head], preferred_element_type=jnp.float32)
        grand_total = grand_total + sum_totals(acc)
        settle(base, size, acc)
    again = too_large(grand_total)
    wait_all()

    @pl.when(again)
    def _():
        place_keys(0, 1, row, False, sizes, limits, key, keys)
        for head, at, query, base, size in chunks(q_ref, kv_heads, True):
            _, acc = anew(scores(query, keys[head]), top_in[at, :], acc_in[at, :], values[head])
            settle(base, size, acc)
        wait_all()


def kernel_options(queries, total_keys, kv_heads):
    rows, width = queries.shape
    return {
        "compiler_params": pltpu.CompilerParams(vmem_limit_bytes=40 * 1024 * 1024),
        "cost_estimate": pl.CostEstimate(
            flops=6 * rows * width * total_keys,
            bytes_accessed=2 * rows * width,
            transcendentals=rows * (width // HD) * total_keys,
        ),
    }


def room(kv_heads, total_keys):
    return [
        pltpu.VMEM((kv_heads, total_keys, HD), jnp.bfloat16),
        pltpu.VMEM((kv_heads, total_keys, 2 * HD), jnp.bfloat16),
    ]


def state_shapes(queries):
    rows = queries.shape[0] * queries.shape[1] // HD
    return [jax.ShapeDtypeStruct((rows, 2 * HD), jnp.float32), jax.ShapeDtypeStruct((rows, HD), jnp.float32)]


def attend_first(count, sizes, queries, limits, own_keys, own_values):
    kv_heads = own_keys.shape[1] // HD
    total_keys = -(-sum(sizes) // HD) * HD
    vmem = pl.BlockSpec(memory_space=pltpu.VMEM)
    return tuple(
        pl.pallas_call(
            functools.partial(first_kernel, count, sizes),
            out_shape=state_shapes(queries),
            in_specs=[vmem] * 4,
            out_specs=[vmem] * 2,
            scratch_shapes=room(kv_heads, total_keys),
            name="attend_first",
            **kernel_options(queries, total_keys, kv_heads),
        )(queries, limits, own_keys, own_values)
    )


def attend_next(pieces, state, count, sizes, queries, limits):
    rows_of = tuple(piece[0] for piece in pieces)
    blocks = [block for piece in pieces for block in piece[1:]]
    kv_heads = blocks[0].shape[1] // HD
    total_keys = -(-len(pieces) * sum(sizes) // HD) * HD
    vmem = pl.BlockSpec(memory_space=pltpu.VMEM)
    operands = [queries, limits, *blocks, *state]
    return tuple(
        pl.pallas_call(
            functools.partial(next_kernel, rows_of, count, sizes),
            out_shape=state_shapes(queries),
            in_specs=[vmem] * len(operands),
            out_specs=[vmem] * 2,
            scratch_shapes=room(kv_heads, total_keys),
            name="attend_next",
            **kernel_options(queries, total_keys, kv_heads),
        )(*operands)
    )


def attend_last(piece, state, sizes, queries, limits):
    row, key, value = piece
    kv_heads = key.shape[1] // HD
    total_keys = -(-sum(sizes) // HD) * HD
    copies = queries.shape[1] // HD // COPY_HEADS
    vmem = pl.BlockSpec(memory_space=pltpu.VMEM)
    options = kernel_options(queries, total_keys, kv_heads)
    weight = pl.pallas_call(
        functools.partial(weights_kernel, row, sizes),
        out_shape=jax.ShapeDtypeStruct((state[1].shape[0], total_keys), jnp.bfloat16),
        in_specs=[vmem] * 4,
        out_specs=vmem,
        scratch_shapes=room(kv_heads, total_keys)[:1],
        name="attend_weights",
        **options,
    )(queries, limits, key, state[1])
    return pl.pallas_call(
        functools.partial(last_kernel, row, sizes),
        out_shape=jax.ShapeDtypeStruct(queries.shape, queries.dtype),
        in_specs=[vmem] * 7,
        out_specs=pl.BlockSpec(memory_space=pltpu.HBM),
        scratch_shapes=[
            *room(kv_heads, total_keys),
            pltpu.VMEM(queries.shape, queries.dtype),
            pltpu.SemaphoreType.DMA((copies,)),
        ],
        name="attend_last",
        **options,
    )(queries, limits, key, value, weight, *state)


def shards(count, queries, win_keys, win_values, cache_keys, cache_values, valid_counts, first_block):
    sizes = (win_keys.shape[0], cache_keys.shape[0])
    half = count // 2
    ring = [place_at(p, count) for p in range(count)]
    onward = [(ring[p], ring[(p + 1) % count]) for p in range(count)]
    backward = [(b, a) for a, b in onward]

    win_keys, win_values, cache_keys, cache_values, valid_counts, first_block, queries = [
        pltpu.with_memory_space_constraint(x, pltpu.HBM)
        for x in (win_keys, win_values, cache_keys, cache_values, valid_counts, first_block, queries)
    ]
    own_keys, own_values, near, limits = load(
        count, win_keys, win_values, cache_keys, cache_values, queries, valid_counts, first_block
    )
    key_on = key_back = own_keys
    value_on = value_back = own_values
    state = attend_first(count, sizes, near, limits, own_keys, own_values)
    arrived = []
    for step in range(1, half + 1):
        key_on = lax.ppermute(key_on, "ctx", onward)
        value_back = lax.ppermute(value_back, "ctx", backward)
        if step < half:
            value_on = lax.ppermute(value_on, "ctx", onward)
            key_back = lax.ppermute(key_back, "ctx", backward)
            row = 2 * (step - 1)
            arrived.append([(row, key_on, value_on), (row + 1, key_back, value_back)])
        else:
            arrived.append([(2 * (half - 1), key_on, value_back)])
        if step == 1:
            key_on, top = lax.optimization_barrier((key_on, state[1]))
            state = (state[0], top)
    for begin in range(0, half - 2, 2):
        pieces = [piece for step in arrived[begin : min(begin + 2, half - 2)] for piece in step]
        state = attend_next(pieces, state, count, sizes, near, limits)
    state = attend_next(arrived[half - 2], state, count, sizes, near, limits)
    return attend_last(arrived[half - 1][0], state, sizes, near, limits)


def solution(mesh):
    in_specs = (
        P(("groups", "ctx"), "tp"),
        P(("groups", "ctx"), "tp"),
        P(("groups", "ctx"), "tp"),
        P(("groups", "ctx"), "tp"),
        P(("groups", "ctx"), "tp"),
        P("groups"),
        P("groups"),
    )
    out_specs = P(("groups", "ctx"), "tp")
    return jax.shard_map(
        functools.partial(shards, mesh.shape["ctx"]),
        mesh=mesh,
        in_specs=in_specs,
        out_specs=out_specs,
        check_vma=False,
    )
```
